512 devices in a mesh: gx: 64 (over z, y), yz: 8 (over x, core).
Axes of the slice: x: 4, y: 4, z: 16, core: 2. Of those that a mesh axis runs over, the one named last changes fastest.
Arguments:
- velocity: float32 [3, 4096, 16384], P(None, 'gx', 'yz'), may hold values from -45 to 45
- blocks: float32 [64, 62, 62], P('gx'), may hold values from -10 to 10, as said below
Outputs:
- derivative: float32 [3, 4096, 16384], P(None, 'gx', 'yz')
- mean_square: float32 [], replicated
The draws below stay inside these ranges and needn't reach their ends.
Inputs may be any that keep to these rules, and one draw needn't show every extreme that they name: `blocks`: every row of the reduced system is strictly diagonally dominant.
All inputs are finite; a program needn't handle non-finite values.
Results may differ from the reference program's by a relative error of at most 0.0003.
Values sent between devices are 32-bit elements; how exact they have to be, the bound alone decides.
No kernel may reach another device: no remote copies, remote signals or barrier semaphores. Data moves between devices by JAX's collectives and lax.ppermute only.
A program may use at most 64 MiB of HBM per device.

```python
import math
import jax
import jax.numpy as jnp
from jax import lax

CX = 64
COMPONENTS = 3
CI = 62
NX = 4096
NL = 16384
MR = 128
N_GX = 64


def draw_velocity(key, part):
    key = jax.random.fold_in(key, 11)
    x_pos = (jnp.arange(NX, dtype=jnp.float32) / NX)[None, :, None]
    line_pos = (jnp.arange(NL, dtype=jnp.float32) / NL)[None, None, :]
    noise = jnp.clip(jax.random.normal(key, (COMPONENTS, NX, NL), jnp.float32), -5.0, 5.0)
    scale = jnp.exp(math.log(3.0) * x_pos) * jnp.exp(math.log(3.0) * line_pos)
    return noise * scale


def draw_blocks(key, part):
    key = jax.random.fold_in(key, 7)
    first_key, second_key, third_key = jax.random.split(key, 3)
    row_index = jnp.arange(CI, dtype=jnp.float32)[:, None]
    col_index = jnp.arange(CI, dtype=jnp.float32)[None, :]
    distance = jnp.abs(row_index - col_index)
    parity = jnp.where(distance % 2.0 == 0.0, 1.0, -1.0)
    base = 1.342 * parity * jnp.power(0.382, distance)
    corner = -3.0 * (jnp.power(0.8, row_index + (CI - 1) - col_index) + jnp.power(0.8, CI - 1 - row_index + col_index))
    first_factor = jax.random.uniform(first_key, (N_GX, CI, CI), jnp.float32, 0.75, 1.25)
    second_factor = jax.random.uniform(second_key, (N_GX, CI, CI), jnp.float32, 0.75, 1.25)
    values = base[None] * first_factor + corner[None] * second_factor
    end_draws = jax.random.uniform(third_key, (4, N_GX), jnp.float32, 0.0, 1.0)
    diag_first = 1.1 + 0.3 * end_draws[0]
    diag_last = 1.1 + 0.3 * end_draws[1]
    margin_first = 0.0015 + 0.0025 * end_draws[2]
    margin_last = 0.0015 + 0.0025 * end_draws[3]
    top_left = 9.0 * (1.0 - diag_first)
    top_right = 9.0 * (diag_first - 1.0 / 3.0 - margin_first)
    bottom_left = 9.0 * (diag_last - 1.0 / 3.0 - margin_last)
    bottom_right = 9.0 * (1.0 - diag_last)
    row_first = row_index == 0.0
    row_final = row_index == CI - 1.0
    col_first = col_index == 0.0
    col_final = col_index == CI - 1.0
    values = jnp.where((row_first & col_first)[None], top_left[:, None, None], values)
    values = jnp.where((row_first & col_final)[None], top_right[:, None, None], values)
    values = jnp.where((row_final & col_first)[None], bottom_left[:, None, None], values)
    values = jnp.where((row_final & col_final)[None], bottom_right[:, None, None], values)
    return values


def setup_inputs(seed: int = 0) -> dict:
    keys = jax.random.split(jax.random.key(seed), 3)
    return {
        "velocity": draw_velocity(jax.random.fold_in(keys[2], 71), 0),
        "blocks": draw_blocks(jax.random.fold_in(keys[2], 71), 0),
    }


COUPLING = 1.0 / 3.0
NEAR_WEIGHT = 7.0 / 9.0
FAR_WEIGHT = 1.0 / 36.0


def reduce_level(state, below, above):
    lower_coef, diag_coef, upper_coef, right_rows = state
    below_lower, below_diag, below_upper, below_right = below
    above_lower, above_diag, above_upper, above_right = above
    ratio_low = lower_coef / below_diag
    ratio_high = upper_coef / above_diag
    new_lower = -ratio_low * below_lower
    new_upper = -ratio_high * above_upper
    new_diag = diag_coef - ratio_low * below_upper - ratio_high * above_lower
    new_right = right_rows - ratio_low * below_right - ratio_high * above_right
    return (new_lower, new_diag, new_upper, new_right)


def cyclic_solve(state):
    total = state[3].shape[0]
    stride = 1
    while stride < total:
        below = tuple(jnp.roll(member, stride, 0) for member in state)
        above = tuple(jnp.roll(member, -stride, 0) for member in state)
        state = reduce_level(state, below, above)
        stride = stride * 2
    return state[3] / (state[0] + state[1] + state[2])


def reference(velocity, blocks):
    right = NEAR_WEIGHT * (jnp.roll(velocity, -1, 1) - jnp.roll(velocity, 1, 1)) + FAR_WEIGHT * (jnp.roll(velocity, -2, 1) - jnp.roll(velocity, 2, 1))
    segments = right.reshape(COMPONENTS, N_GX, CX, NL)
    interior = segments[:, :, 1:CX - 1, :]
    solved_int = jnp.einsum("kij,ckjl->ckil", blocks, interior, precision=lax.Precision.HIGHEST)
    first_col = COUPLING * blocks[:, :, 0]
    last_col = COUPLING * blocks[:, :, CI - 1]
    lower_first = jnp.full((N_GX,), COUPLING, jnp.float32)
    diag_first = 1.0 - COUPLING * first_col[:, 0]
    upper_first = -COUPLING * last_col[:, 0]
    lower_last = -COUPLING * first_col[:, CI - 1]
    diag_last = 1.0 - COUPLING * last_col[:, CI - 1]
    upper_last = jnp.full((N_GX,), COUPLING, jnp.float32)
    lower_coef = jnp.stack([lower_first, lower_last], 1).reshape(MR, 1, 1)
    diag_coef = jnp.stack([diag_first, diag_last], 1).reshape(MR, 1, 1)
    upper_coef = jnp.stack([upper_first, upper_last], 1).reshape(MR, 1, 1)
    right_first = segments[:, :, 0, :] - COUPLING * solved_int[:, :, 0, :]
    right_last = segments[:, :, CX - 1, :] - COUPLING * solved_int[:, :, CI - 1, :]
    reduced = jnp.stack([right_first, right_last], 2)
    reduced = jnp.transpose(reduced, (1, 2, 0, 3)).reshape(MR, COMPONENTS, NL)
    ends = cyclic_solve((lower_coef, diag_coef, upper_coef, reduced))
    ends = jnp.transpose(ends.reshape(N_GX, 2, COMPONENTS, NL), (2, 0, 1, 3))
    first_val = ends[:, :, 0:1, :]
    last_val = ends[:, :, 1:2, :]
    inner = solved_int - first_col[None, :, :, None] * first_val - last_col[None, :, :, None] * last_val
    derivative = jnp.concatenate([first_val, inner, last_val], 2).reshape(COMPONENTS, NX, NL)
    mean_square = jnp.mean(derivative * derivative)
    return derivative, mean_square
```

```python
import functools

import jax
import jax.numpy as jnp
from jax import lax
from jax.experimental import pallas as pl
from jax.experimental.pallas import tpu as pltpu
from jax.sharding import PartitionSpec as P

COUPLING = 1.0 / 3.0
NEAR_WEIGHT = 7.0 / 9.0
FAR_WEIGHT = 1.0 / 36.0

GROUP = 16
GROUPS = 4
LANES = 128
CELLS = 64
F32 = jnp.float32


def lane_row(value, lanes=LANES):
    return jnp.broadcast_to(value, (1, lanes))


def tiled(value, copies):
    return jnp.concatenate([value] * copies, axis=1)


def local_kernel(v_ref, block_ref, g_ref, send_ref, p_ref, q_ref, mat_ref, pad_ref, energy_ref):
    comp = pl.program_id(0)
    inner = CELLS - 2
    lines = v_ref.shape[2]
    row8 = lax.broadcasted_iota(jnp.int32, (8, lines), 0)

    @pl.when(comp == 0)
    def _():
        pad_ref[...] = jnp.zeros(pad_ref.shape, F32)
        pad_ref[0:inner, 0:inner] = block_ref[0]
        padded = pltpu.roll(pltpu.roll(pad_ref[...], 1, 0), 1, 1)
        first = jnp.broadcast_to(COUPLING * padded[:, 1:2], (CELLS, LANES))
        last = jnp.broadcast_to(COUPLING * padded[:, inner : inner + 1], (CELLS, LANES))
        p_ref[...] = first
        q_ref[...] = last
        cols = lax.broadcasted_iota(jnp.int32, (1, LANES), 1)
        top = jnp.where(cols == 0, 1.0, 0.0) - COUPLING * padded[1:2]
        bottom = jnp.where(cols == CELLS - 1, 1.0, 0.0) - COUPLING * padded[inner : inner + 1]
        first_sum = jnp.sum(first * padded, axis=0, keepdims=True)
        last_sum = jnp.sum(last * padded, axis=0, keepdims=True)
        mat_ref[0:CELLS, :] = padded
        rows = lax.broadcasted_iota(jnp.int32, (8, LANES), 0)
        extra = jnp.where(rows == 0, top, 0.0)
        extra = jnp.where(rows == 1, bottom, extra)
        extra = jnp.where(rows == 2, first_sum, extra)
        extra = jnp.where(rows == 3, last_sum, extra)
        mat_ref[CELLS : CELLS + 8, :] = extra
        energy_ref[...] = jnp.zeros(energy_ref.shape, F32)

    v = v_ref[0]
    low, high = v[0:1], v[CELLS - 1 : CELLS]
    below_1 = jnp.concatenate([low, v[: CELLS - 1]], 0)
    below_2 = jnp.concatenate([low, low, v[: CELLS - 2]], 0)
    above_1 = jnp.concatenate([v[1:], high], 0)
    above_2 = jnp.concatenate([v[2:], high, high], 0)
    right = NEAR_WEIGHT * (above_1 - below_1) + FAR_WEIGHT * (above_2 - below_2)
    out = jnp.dot(
        mat_ref[:, 0:CELLS], right, precision=lax.Precision.HIGHEST, preferred_element_type=F32
    )
    g = out[0:CELLS]
    g_ref[0] = g
    squares = jnp.sum(g * g, axis=0, keepdims=True)
    part = squares[:, 0:LANES]
    for j in range(1, GROUP):
        part = part + squares[:, j * LANES : (j + 1) * LANES]
    energy_ref[0:1, :] += part
    rows = out[CELLS : CELLS + 8]
    rows = jnp.where((row8 == 4) | (row8 == 5), pltpu.roll(v[0:8], 4, 0), rows)
    rows = jnp.where(row8 >= 6, v[CELLS - 8 : CELLS], rows)
    at = pl.multiple_of(comp * 8, 8)
    for j in range(GROUP):
        send_ref[j, pl.ds(at, 8), :] = rows[:, j * LANES : (j + 1) * LANES]

    @pl.when(comp == pl.num_programs(0) - 1)
    def _():
        first, last = p_ref[...], q_ref[...]
        coefs = jnp.concatenate(
            [
                first[1:2],
                last[1:2],
                first[inner : inner + 1],
                last[inner : inner + 1],
                jnp.sum(first * first, axis=0, keepdims=True),
                jnp.sum(first * last, axis=0, keepdims=True),
                jnp.sum(last * last, axis=0, keepdims=True),
                energy_ref[0:1, :],
            ],
            0,
        )
        for j in range(GROUP):
            send_ref[j, send_ref.shape[1] - 8 :, :] = coefs


def group_kernel(recv_ref, msg_ref, state_ref, open_ref):
    stride = recv_ref.shape[0] // GROUP
    comps = stride // 8 - 1
    width = comps * LANES

    def rows(r):
        parts = [recv_ref[pl.ds(8 * i + r, GROUP, stride=stride), :] for i in range(comps)]
        return jnp.concatenate(parts, 1)

    def coef(r):
        return recv_ref[pl.ds(8 * comps + r, GROUP, stride=stride), :]

    seg = lax.broadcasted_iota(jnp.int32, (GROUP, width), 0)
    seg_1 = lax.broadcasted_iota(jnp.int32, (GROUP, LANES), 0)

    def prev(x, s=1):
        return pltpu.roll(x, s, 0)

    def following(x, s=1):
        return pltpu.roll(x, GROUP - s, 0)

    b_first, b_last, pg, qg, v_0, v_1, v_62, v_63 = [rows(r) for r in range(8)]
    p_0, q_0, p_61, q_61, pp, pq, qq, energy = [coef(r) for r in range(8)]
    jump_l = jnp.where(seg == 0, 0.0, prev(v_63) - v_0)
    jump_l2 = jnp.where(seg == 0, 0.0, prev(v_62) - v_0)
    jump_r = jnp.where(seg == GROUP - 1, 0.0, v_63 - following(v_0))
    jump_r2 = jnp.where(seg == GROUP - 1, 0.0, following(v_1) - v_63)
    b_first = b_first - (2.0 / 3.0) * jump_l - FAR_WEIGHT * jump_l2
    b_last = b_last - (2.0 / 3.0) * jump_r + FAR_WEIGHT * jump_r2

    unit_first = jnp.where(seg_1 == 0, 1.0, 0.0)
    unit_last = jnp.where(seg_1 == GROUP - 1, 1.0, 0.0)
    zero = jnp.zeros((GROUP, LANES), F32)
    third = jnp.full((GROUP, LANES), COUPLING, F32)
    rhs_f = jnp.concatenate([b_first, unit_first, zero], 1)
    rhs_l = jnp.concatenate([b_last, zero, unit_last], 1)
    f = (jnp.where(seg_1 == 0, 0.0, third), 1.0 - COUPLING * p_0, -COUPLING * q_0, rhs_f)
    l = (-COUPLING * p_61, 1.0 - COUPLING * q_61, jnp.where(seg_1 == GROUP - 1, 0.0, third), rhs_l)

    def reduce_level(mine, below, above):
        ratio_low = mine[0] / below[1]
        ratio_high = mine[2] / above[1]
        return (
            -ratio_low * below[0],
            mine[1] - ratio_low * below[2] - ratio_high * above[0],
            -ratio_high * above[2],
            mine[3] - tiled(ratio_low, comps + 2) * below[3] - tiled(ratio_high, comps + 2) * above[3],
        )

    f, l = (
        reduce_level(f, tuple(prev(x) for x in l), l),
        reduce_level(l, f, tuple(following(x) for x in f)),
    )
    step = 1
    while step < GROUP:
        f = reduce_level(f, tuple(prev(x, step) for x in f), tuple(following(x, step) for x in f))
        l = reduce_level(l, tuple(prev(x, step) for x in l), tuple(following(x, step) for x in l))
        step *= 2
    sol_f = f[3] / tiled(f[1], comps + 2)
    sol_l = l[3] / tiled(l[1], comps + 2)
    x_f, a_f, c_f = sol_f[:, :width], sol_f[:, width : width + LANES], sol_f[:, width + LANES :]
    x_l, a_l, c_l = sol_l[:, :width], sol_l[:, width : width + LANES], sol_l[:, width + LANES :]

    pp1, qq1 = pp + 1.0, qq + 1.0
    d_l, d_r = jump_l * (1.0 / 12.0), jump_r * (1.0 / 12.0)
    pq_w = tiled(pq, comps)
    m_f = tiled(pp1, comps) * x_f + pq_w * x_l - pg - d_l
    m_l = tiled(qq1, comps) * x_l + pq_w * x_f - qg - d_r

    def total(x):
        return jnp.sum(x, axis=0, keepdims=True)

    line_a = 2.0 * total(tiled(a_f, comps) * m_f + tiled(a_l, comps) * m_l)
    line_c = 2.0 * total(tiled(c_f, comps) * m_f + tiled(c_l, comps) * m_l)
    base = total(x_f * (m_f - pg - d_l) + x_l * (m_l - qg - d_r) + d_l * d_l + d_r * d_r)
    part = total(energy) * (1.0 / GROUP)
    for i in range(comps):
        part = part + base[:, i * LANES : (i + 1) * LANES]
    quad_aa = total(pp1 * a_f * a_f + 2.0 * pq * a_f * a_l + qq1 * a_l * a_l)
    quad_ac = total(pp1 * a_f * c_f + pq * (a_f * c_l + a_l * c_f) + qq1 * a_l * c_l)
    quad_cc = total(pp1 * c_f * c_f + 2.0 * pq * c_f * c_l + qq1 * c_l * c_l)

    end = GROUP - 1
    msg_ref[:, 0:width] = jnp.concatenate(
        [x_f[0:1], x_l[end:], line_a, line_c, v_0[0:1], v_1[0:1], v_62[end:], v_63[end:]], 0
    )
    msg_ref[:, width : width + LANES] = jnp.concatenate(
        [a_f[0:1], a_l[end:], c_f[0:1], c_l[end:], quad_aa, quad_ac, quad_cc, part], 0
    )
    state_ref[0] = x_f
    state_ref[1] = x_l
    state_ref[2] = jump_l
    state_ref[3] = jump_r
    open_ref[0] = a_f
    open_ref[1] = a_l
    open_ref[2] = c_f
    open_ref[3] = c_l


def eliminate(matrix, rhs, wide):
    size = len(rhs)
    matrix = [list(r) for r in matrix]
    rhs = list(rhs)
    inverse = [None] * size
    for k in range(size):
        inverse[k] = 1.0 / matrix[k][k]
        for i in range(k + 1, size):
            if matrix[i][k] is None:
                continue
            ratio = matrix[i][k] * inverse[k]
            for j in range(k + 1, size):
                if matrix[k][j] is not None:
                    old = matrix[i][j]
                    change = ratio * matrix[k][j]
                    matrix[i][j] = -change if old is None else old - change
            rhs[i] = rhs[i] - wide(ratio) * rhs[k]
    found = [None] * size
    for k in reversed(range(size)):
        value = rhs[k]
        for j in range(k + 1, size):
            if matrix[k][j] is not None:
                value = value - wide(matrix[k][j]) * found[j]
        found[k] = value * wide(inverse[k])
    return found


def join_kernel(own_ref, near_ref, far_ref, state_ref, open_ref, send_ref, all_ref):
    width = state_ref.shape[2]
    comps = width // LANES
    group = lax.axis_index("gx") // GROUP
    all_ref[0] = own_ref[...]
    all_ref[1] = near_ref[...]
    all_ref[2] = far_ref[1]
    all_ref[3] = far_ref[0]

    def wide(x):
        return tiled(x, comps)

    tile = []
    for t in range(GROUPS):
        own = group % 4
        slot = jnp.where(own >= 2, (t // 2) ^ 1, t // 2) * 2 + jnp.where(own % 2 == 1, (t % 2) ^ 1, t % 2)
        tile.append(all_ref[slot])
    data = [[m[r : r + 1, 0:width] for r in range(8)] for m in tile]
    scal = [[m[r : r + 1, width:] for r in range(8)] for m in tile]
    x_f, x_l, line_a, line_c, v_0, v_1, v_62, v_63 = [[d[r] for d in data] for r in range(8)]
    a_f, a_l, c_f, c_l, q_aa, q_ac, q_cc, part = [[s[r] for s in scal] for r in range(8)]

    one = jnp.ones((1, LANES), F32)
    jump = [v_63[t - 1] - v_0[t] for t in range(GROUPS)]
    matrix, rhs = [], []
    for t in range(GROUPS):
        before, after = (t - 1) % GROUPS, (t + 1) % GROUPS
        row_a, row_c = [None] * (2 * GROUPS), [None] * (2 * GROUPS)
        row_a[2 * t] = one
        row_a[2 * before] = COUPLING * a_l[before]
        row_a[2 * before + 1] = COUPLING * c_l[before]
        row_c[2 * t + 1] = one
        row_c[2 * after] = COUPLING * a_f[after]
        row_c[2 * after + 1] = COUPLING * c_f[after]
        matrix += [row_a, row_c]
        rhs.append(
            -COUPLING * x_l[before] - (2.0 / 3.0) * jump[t] - FAR_WEIGHT * (v_62[before] - v_0[t])
        )
        rhs.append(
            -COUPLING * x_f[after] - (2.0 / 3.0) * jump[after] + FAR_WEIGHT * (v_1[after] - v_63[t])
        )
    found = eliminate(matrix, rhs, wide)
    value_a, value_c = found[0::2], found[1::2]

    energy = jnp.zeros((1, LANES), F32)
    for t in range(GROUPS):
        a, c = value_a[t], value_c[t]
        after = (t + 1) % GROUPS
        u_end = x_f[t] + wide(a_f[t]) * a + wide(c_f[t]) * c
        w_end = x_l[t] + wide(a_l[t]) * a + wide(c_l[t]) * c
        d_l, d_r = jump[t] * (1.0 / 12.0), jump[after] * (1.0 / 12.0)
        lines = a * (line_a[t] + wide(q_aa[t]) * a + wide(2.0 * q_ac[t]) * c)
        lines = lines + c * (line_c[t] + wide(q_cc[t]) * c)
        lines = lines + d_l * (d_l - 2.0 * u_end) + d_r * (d_r - 2.0 * w_end)
        energy = energy + part[t]
        for i in range(comps):
            energy = energy + lines[:, i * LANES : (i + 1) * LANES]

    def mine(values):
        result = values[0]
        for t in range(1, GROUPS):
            result = jnp.where(group == t, values[t], result)
        return result

    a, c = mine(value_a), mine(value_c)
    left, right = mine(jump), mine(jump[1:] + jump[:1])
    seg = lax.broadcasted_iota(jnp.int32, (GROUP, width), 0)
    u_t = state_ref[0] + wide(open_ref[0]) * a + wide(open_ref[2]) * c
    w_t = state_ref[1] + wide(open_ref[1]) * a + wide(open_ref[3]) * c
    jump_l = jnp.where(seg == 0, left, state_ref[2])
    jump_r = jnp.where(seg == GROUP - 1, right, state_ref[3])
    u = u_t - jump_l * (1.0 / 12.0)
    w = w_t - jump_r * (1.0 / 12.0)
    send_ref[...] = jnp.zeros(send_ref.shape, F32)
    for i in range(comps):
        for r, value in enumerate((u_t, w_t, u, w)):
            part_i = value[:, i * LANES : (i + 1) * LANES]
            send_ref[pl.ds(8 * i + r, GROUP, stride=8 * comps), :] = part_i
    send_ref[pl.ds(4, GROUP, stride=8 * comps), :] = jnp.broadcast_to(energy, (GROUP, LANES))


def final_kernel(recv_ref, g_ref, p_ref, q_ref, out_ref, energy_ref):
    row8 = lax.broadcasted_iota(jnp.int32, (8, LANES), 0)
    first, last = p_ref[...], q_ref[...]

    @pl.when(pl.program_id(0) == 0)
    def _():
        energy = recv_ref[0, 4:5, :]
        for j in range(1, GROUP):
            energy = energy + recv_ref[j, 4:5, :]
        energy_ref[...] = jnp.broadcast_to(energy, energy_ref.shape)

    for j in range(GROUP):
        at = slice(j * LANES, (j + 1) * LANES)
        u_t, w_t = recv_ref[j, 0:1, :], recv_ref[j, 1:2, :]
        u, w = recv_ref[j, 2:3, :], recv_ref[j, 3:4, :]
        value = g_ref[0, :, at] - first * u_t - last * w_t
        out_ref[0, 0:8, at] = jnp.where(row8 == 0, u, value[0:8])
        out_ref[0, 8 : CELLS - 8, at] = value[8 : CELLS - 8]
        out_ref[0, CELLS - 8 :, at] = jnp.where(row8 == 7, w, value[CELLS - 8 :])


def on_device(velocity, blocks):
    comps, cells, lines = velocity.shape
    width = comps * LANES
    yz_count = lax.axis_size("yz")
    groups = [[GROUP * t + i for i in range(GROUP)] for t in range(GROUPS)]
    shape = functools.partial(jax.ShapeDtypeStruct, dtype=F32)

    g, send, p_rows, q_rows = pl.pallas_call(
        local_kernel,
        grid=(comps,),
        in_specs=[
            pl.BlockSpec((1, cells, lines), lambda c: (c, 0, 0)),
            pl.BlockSpec(blocks.shape, lambda c: (0, 0, 0)),
        ],
        out_specs=[
            pl.BlockSpec((1, cells, lines), lambda c: (c, 0, 0)),
            pl.BlockSpec((GROUP, 8 * (comps + 1), LANES), lambda c: (0, 0, 0)),
            pl.BlockSpec((cells, LANES), lambda c: (0, 0)),
            pl.BlockSpec((cells, LANES), lambda c: (0, 0)),
        ],
        out_shape=[
            shape((comps, cells, lines)),
            shape((GROUP, 8 * (comps + 1), LANES)),
            shape((cells, LANES)),
            shape((cells, LANES)),
        ],
        scratch_shapes=[
            pltpu.VMEM((cells + 8, LANES), F32),
            pltpu.VMEM((cells, LANES), F32),
            pltpu.VMEM((8, LANES), F32),
        ],
        compiler_params=pltpu.CompilerParams(vmem_limit_bytes=32 * 1024 * 1024),
        name="local_solve",
    )(velocity, blocks)

    recv = lax.all_to_all(send, "gx", 0, 0, axis_index_groups=groups, tiled=True)
    msg, state, opened = pl.pallas_call(
        group_kernel,
        out_shape=[
            shape((8, width + LANES)),
            shape((4, GROUP, width)),
            shape((4, GROUP, LANES)),
        ],
        name="group_solve",
    )(recv.reshape(GROUP * 8 * (comps + 1), LANES))

    def swapped(value, mask):
        pairs = [
            (t * GROUP + i, (t ^ mask) * GROUP + i) for t in range(GROUPS) for i in range(GROUP)
        ]
        return lax.ppermute(value, "gx", pairs)

    near = swapped(msg, 1)
    far = swapped(jnp.stack([msg, near]), 3)
    send_back = pl.pallas_call(
        join_kernel,
        out_shape=shape((GROUP * 8 * comps, LANES)),
        scratch_shapes=[pltpu.VMEM((GROUPS, 8, width + LANES), F32)],
        name="join_groups",
    )(msg, near, far, state, opened)
    back = lax.all_to_all(
        send_back.reshape(GROUP, 8 * comps, LANES), "gx", 0, 0, axis_index_groups=groups, tiled=True
    )

    derivative, energy = pl.pallas_call(
        final_kernel,
        grid=(comps,),
        in_specs=[
            pl.BlockSpec((GROUP, 8, LANES), lambda c: (0, c, 0)),
            pl.BlockSpec((1, cells, lines), lambda c: (c, 0, 0)),
            pl.BlockSpec((cells, LANES), lambda c: (0, 0)),
            pl.BlockSpec((cells, LANES), lambda c: (0, 0)),
        ],
        out_specs=[
            pl.BlockSpec((1, cells, lines), lambda c: (c, 0, 0)),
            pl.BlockSpec((yz_count, LANES), lambda c: (0, 0)),
        ],
        out_shape=[shape((comps, cells, lines)), shape((yz_count, LANES))],
        compiler_params=pltpu.CompilerParams(vmem_limit_bytes=32 * 1024 * 1024),
        name="final_update",
    )(back, g, p_rows, q_rows)
    energies = lax.all_to_all(energy, "yz", 0, 0, tiled=True)
    total_count = comps * cells * lines * lax.axis_size("gx") * yz_count
    return derivative, jnp.sum(energies) / total_count


def solution(mesh):
    placed = (P(None, "gx", "yz"), P("gx", None, None))
    return jax.shard_map(
        on_device, mesh=mesh, in_specs=placed, out_specs=(P(None, "gx", "yz"), P()), check_vma=False
    )
```

```python
import functools

import jax
import jax.numpy as jnp
from jax import lax
from jax.experimental import pallas as pl
from jax.experimental.pallas import tpu as pltpu
from jax.sharding import PartitionSpec as P

COUPLING = 1.0 / 3.0
NEAR_WEIGHT = 7.0 / 9.0
FAR_WEIGHT = 1.0 / 36.0

GROUP = 16
GROUPS = 4
LANES = 128
CELLS = 64
CHUNK = 512
F32 = jnp.float32
BF16 = jnp.bfloat16
SMALL = pltpu.CompilerParams(vmem_limit_bytes=8 * 1024 * 1024)
LARGE = pltpu.CompilerParams(vmem_limit_bytes=16 * 1024 * 1024)


def lane_row(value, lanes=LANES):
    return jnp.broadcast_to(value, (1, lanes))


def tiled(value, copies):
    return jnp.concatenate([value] * copies, axis=1)


def parts_of(value):
    high = value.astype(BF16)
    rest = value - high.astype(F32)
    middle = rest.astype(BF16)
    return high, middle, (rest - middle.astype(F32)).astype(BF16)


def local_kernel(
    v_hbm, block_hbm, g_ref, send_ref, p_ref, q_ref, v_ref, mat_ref, pad_ref, block_ref, sems
):
    comps, _, lines = v_ref.shape
    inner = CELLS - 2
    block_copy = pltpu.make_async_copy(block_hbm, block_ref, sems.at[comps])
    block_copy.start()
    copies = [pltpu.make_async_copy(v_hbm.at[c], v_ref.at[c], sems.at[c]) for c in range(comps)]
    for copy in copies:
        copy.start()

    pad_ref[...] = jnp.zeros(pad_ref.shape, F32)
    block_copy.wait()
    pad_ref[0:inner, 0:inner] = block_ref[:, 0, :]
    padded = pltpu.roll(pltpu.roll(pad_ref[...], 1, 0), 1, 1)
    first = jnp.broadcast_to(COUPLING * padded[:, 1:2], (CELLS, LANES))
    last = jnp.broadcast_to(COUPLING * padded[:, inner : inner + 1], (CELLS, LANES))
    p_ref[...] = first
    q_ref[...] = last
    cols = lax.broadcasted_iota(jnp.int32, (1, LANES), 1)
    top = jnp.where(cols == 0, 1.0, 0.0) - COUPLING * padded[1:2]
    bottom = jnp.where(cols == CELLS - 1, 1.0, 0.0) - COUPLING * padded[inner : inner + 1]
    first_sum = jnp.sum(first * padded, axis=0, keepdims=True)
    last_sum = jnp.sum(last * padded, axis=0, keepdims=True)
    rows = lax.broadcasted_iota(jnp.int32, (16, LANES), 0)
    extra = jnp.where(rows == 0, top, 0.0)
    extra = jnp.where(rows == 1, bottom, extra)
    extra = jnp.where(rows == 2, first_sum, extra)
    extra = jnp.where(rows == 3, last_sum, extra)
    matrix = jnp.concatenate([padded, extra], 0)
    high, middle, low = parts_of(matrix[:, 0:CELLS])
    mat_ref[...] = jnp.concatenate([high, middle, low, high, middle, high], 1)

    row8 = lax.broadcasted_iota(jnp.int32, (8, CHUNK), 0)
    energy = jnp.zeros((1, LANES), F32)
    for c in range(comps):
        copies[c].wait()
        for start in range(0, lines, CHUNK):
            v = v_ref[c, :, start : start + CHUNK]
            edge_0, edge_1 = v[0:1], v[CELLS - 1 : CELLS]
            below_1 = jnp.concatenate([edge_0, v[: CELLS - 1]], 0)
            below_2 = jnp.concatenate([edge_0, edge_0, v[: CELLS - 2]], 0)
            above_1 = jnp.concatenate([v[1:], edge_1], 0)
            above_2 = jnp.concatenate([v[2:], edge_1, edge_1], 0)
            right = NEAR_WEIGHT * (above_1 - below_1) + FAR_WEIGHT * (above_2 - below_2)
            high, middle, low = parts_of(right)
            stacked = jnp.concatenate([high, high, high, middle, middle, low], 0)
            out = jnp.dot(mat_ref[...], stacked, preferred_element_type=F32)
            g = out[0:CELLS]
            g_ref[c, :, start : start + CHUNK] = g
            squares = jnp.sum(g * g, axis=0, keepdims=True)
            rows = out[CELLS : CELLS + 8]
            rows = jnp.where((row8 == 4) | (row8 == 5), pltpu.roll(v[0:8], 4, 0), rows)
            rows = jnp.where(row8 >= 6, v[CELLS - 8 : CELLS], rows)
            for j in range(CHUNK // LANES):
                at = slice(j * LANES, (j + 1) * LANES)
                energy = energy + squares[:, at]
                send_ref[start // LANES + j, 8 * c : 8 * c + 8, :] = rows[:, at]

    coefs = jnp.concatenate(
        [
            first[1:2],
            last[1:2],
            first[inner : inner + 1],
            last[inner : inner + 1],
            jnp.sum(first * first, axis=0, keepdims=True),
            jnp.sum(first * last, axis=0, keepdims=True),
            jnp.sum(last * last, axis=0, keepdims=True),
            energy,
        ],
        0,
    )
    for j in range(GROUP):
        send_ref[j, 8 * comps :, :] = coefs


def group_kernel(recv_ref, msg_ref, state_ref, open_ref):
    stride = recv_ref.shape[0] // GROUP
    comps = stride // 8 - 1
    width = comps * LANES

    def rows(r):
        parts = [recv_ref[pl.ds(8 * i + r, GROUP, stride=stride), :] for i in range(comps)]
        return jnp.concatenate(parts, 1)

    def coef(r):
        return recv_ref[pl.ds(8 * comps + r, GROUP, stride=stride), :]

    seg = lax.broadcasted_iota(jnp.int32, (GROUP, width), 0)
    seg_1 = lax.broadcasted_iota(jnp.int32, (GROUP, LANES), 0)

    def prev(x, s=1):
        return pltpu.roll(x, s, 0)

    def following(x, s=1):
        return pltpu.roll(x, GROUP - s, 0)

    b_first, b_last, pg, qg, v_0, v_1, v_62, v_63 = [rows(r) for r in range(8)]
    p_0, q_0, p_61, q_61, pp, pq, qq, energy = [coef(r) for r in range(8)]
    jump_l = jnp.where(seg == 0, 0.0, prev(v_63) - v_0)
    jump_l2 = jnp.where(seg == 0, 0.0, prev(v_62) - v_0)
    jump_r = jnp.where(seg == GROUP - 1, 0.0, v_63 - following(v_0))
    jump_r2 = jnp.where(seg == GROUP - 1, 0.0, following(v_1) - v_63)
    b_first = b_first - (2.0 / 3.0) * jump_l - FAR_WEIGHT * jump_l2
    b_last = b_last - (2.0 / 3.0) * jump_r + FAR_WEIGHT * jump_r2

    unit_first = jnp.where(seg_1 == 0, 1.0, 0.0)
    unit_last = jnp.where(seg_1 == GROUP - 1, 1.0, 0.0)
    zero = jnp.zeros((GROUP, LANES), F32)
    third = jnp.full((GROUP, LANES), COUPLING, F32)
    rhs_f = jnp.concatenate([b_first, unit_first, zero], 1)
    rhs_l = jnp.concatenate([b_last, zero, unit_last], 1)
    f = (jnp.where(seg_1 == 0, 0.0, third), 1.0 - COUPLING * p_0, -COUPLING * q_0, rhs_f)
    l = (-COUPLING * p_61, 1.0 - COUPLING * q_61, jnp.where(seg_1 == GROUP - 1, 0.0, third), rhs_l)

    def reduce_level(mine, below, above):
        ratio_low = mine[0] / below[1]
        ratio_high = mine[2] / above[1]
        return (
            -ratio_low * below[0],
            mine[1] - ratio_low * below[2] - ratio_high * above[0],
            -ratio_high * above[2],
            mine[3] - tiled(ratio_low, comps + 2) * below[3] - tiled(ratio_high, comps + 2) * above[3],
        )

    f, l = (
        reduce_level(f, tuple(prev(x) for x in l), l),
        reduce_level(l, f, tuple(following(x) for x in f)),
    )
    step = 1
    while step < GROUP:
        f = reduce_level(f, tuple(prev(x, step) for x in f), tuple(following(x, step) for x in f))
        l = reduce_level(l, tuple(prev(x, step) for x in l), tuple(following(x, step) for x in l))
        step *= 2
    sol_f = f[3] / tiled(f[1], comps + 2)
    sol_l = l[3] / tiled(l[1], comps + 2)
    x_f, a_f, c_f = sol_f[:, :width], sol_f[:, width : width + LANES], sol_f[:, width + LANES :]
    x_l, a_l, c_l = sol_l[:, :width], sol_l[:, width : width + LANES], sol_l[:, width + LANES :]

    pp1, qq1 = pp + 1.0, qq + 1.0
    d_l, d_r = jump_l * (1.0 / 12.0), jump_r * (1.0 / 12.0)
    pq_w = tiled(pq, comps)
    m_f = tiled(pp1, comps) * x_f + pq_w * x_l - pg - d_l
    m_l = tiled(qq1, comps) * x_l + pq_w * x_f - qg - d_r

    def total(x):
        return jnp.sum(x, axis=0, keepdims=True)

    line_a = 2.0 * total(tiled(a_f, comps) * m_f + tiled(a_l, comps) * m_l)
    line_c = 2.0 * total(tiled(c_f, comps) * m_f + tiled(c_l, comps) * m_l)
    base = total(x_f * (m_f - pg - d_l) + x_l * (m_l - qg - d_r) + d_l * d_l + d_r * d_r)
    part = total(energy) * (1.0 / GROUP)
    for i in range(comps):
        part = part + base[:, i * LANES : (i + 1) * LANES]
    quad_aa = total(pp1 * a_f * a_f + 2.0 * pq * a_f * a_l + qq1 * a_l * a_l)
    quad_ac = total(pp1 * a_f * c_f + pq * (a_f * c_l + a_l * c_f) + qq1 * a_l * c_l)
    quad_cc = total(pp1 * c_f * c_f + 2.0 * pq * c_f * c_l + qq1 * c_l * c_l)

    end = GROUP - 1
    msg_ref[:, 0:width] = jnp.concatenate(
        [x_f[0:1], x_l[end:], line_a, line_c, v_0[0:1], v_1[0:1], v_62[end:], v_63[end:]], 0
    )
    msg_ref[:, width : width + LANES] = jnp.concatenate(
        [a_f[0:1], a_l[end:], c_f[0:1], c_l[end:], quad_aa, quad_ac, quad_cc, part], 0
    )
    state_ref[0] = x_f
    state_ref[1] = x_l
    state_ref[2] = jump_l
    state_ref[3] = jump_r
    open_ref[0] = a_f
    open_ref[1] = a_l
    open_ref[2] = c_f
    open_ref[3] = c_l


def eliminate(matrix, rhs, wide):
    size = len(rhs)
    matrix = [list(r) for r in matrix]
    rhs = list(rhs)
    inverse = [None] * size
    for k in range(size):
        inverse[k] = 1.0 / matrix[k][k]
        for i in range(k + 1, size):
            if matrix[i][k] is None:
                continue
            ratio = matrix[i][k] * inverse[k]
            for j in range(k + 1, size):
                if matrix[k][j] is not None:
                    old = matrix[i][j]
                    change = ratio * matrix[k][j]
                    matrix[i][j] = -change if old is None else old - change
            rhs[i] = rhs[i] - wide(ratio) * rhs[k]
    found = [None] * size
    for k in reversed(range(size)):
        value = rhs[k]
        for j in range(k + 1, size):
            if matrix[k][j] is not None:
                value = value - wide(matrix[k][j]) * found[j]
        found[k] = value * wide(inverse[k])
    return found


def join_kernel(own_ref, near_ref, far_ref, state_ref, open_ref, send_ref, all_ref):
    width = state_ref.shape[2]
    comps = width // LANES
    group = lax.axis_index("gx") // GROUP
    all_ref[0] = own_ref[...]
    all_ref[1] = near_ref[...]
    all_ref[2] = far_ref[1]
    all_ref[3] = far_ref[0]

    def wide(x):
        return tiled(x, comps)

    tile = []
    for t in range(GROUPS):
        own = group % 4
        slot = jnp.where(own >= 2, (t // 2) ^ 1, t // 2) * 2 + jnp.where(own % 2 == 1, (t % 2) ^ 1, t % 2)
        tile.append(all_ref[slot])
    data = [[m[r : r + 1, 0:width] for r in range(8)] for m in tile]
    scal = [[m[r : r + 1, width:] for r in range(8)] for m in tile]
    x_f, x_l, line_a, line_c, v_0, v_1, v_62, v_63 = [[d[r] for d in data] for r in range(8)]
    a_f, a_l, c_f, c_l, q_aa, q_ac, q_cc, part = [[s[r] for s in scal] for r in range(8)]

    one = jnp.ones((1, LANES), F32)
    jump = [v_63[t - 1] - v_0[t] for t in range(GROUPS)]
    matrix, rhs = [], []
    for t in range(GROUPS):
        before, after = (t - 1) % GROUPS, (t + 1) % GROUPS
        row_a, row_c = [None] * (2 * GROUPS), [None] * (2 * GROUPS)
        row_a[2 * t] = one
        row_a[2 * before] = COUPLING * a_l[before]
        row_a[2 * before + 1] = COUPLING * c_l[before]
        row_c[2 * t + 1] = one
        row_c[2 * after] = COUPLING * a_f[after]
        row_c[2 * after + 1] = COUPLING * c_f[after]
        matrix += [row_a, row_c]
        rhs.append(
            -COUPLING * x_l[before] - (2.0 / 3.0) * jump[t] - FAR_WEIGHT * (v_62[before] - v_0[t])
        )
        rhs.append(
            -COUPLING * x_f[after] - (2.0 / 3.0) * jump[after] + FAR_WEIGHT * (v_1[after] - v_63[t])
        )
    found = eliminate(matrix, rhs, wide)
    value_a, value_c = found[0::2], found[1::2]

    energy = jnp.zeros((1, LANES), F32)
    for t in range(GROUPS):
        a, c = value_a[t], value_c[t]
        after = (t + 1) % GROUPS
        u_end = x_f[t] + wide(a_f[t]) * a + wide(c_f[t]) * c
        w_end = x_l[t] + wide(a_l[t]) * a + wide(c_l[t]) * c
        d_l, d_r = jump[t] * (1.0 / 12.0), jump[after] * (1.0 / 12.0)
        lines = a * (line_a[t] + wide(q_aa[t]) * a + wide(2.0 * q_ac[t]) * c)
        lines = lines + c * (line_c[t] + wide(q_cc[t]) * c)
        lines = lines + d_l * (d_l - 2.0 * u_end) + d_r * (d_r - 2.0 * w_end)
        energy = energy + part[t]
        for i in range(comps):
            energy = energy + lines[:, i * LANES : (i + 1) * LANES]

    def mine(values):
        result = values[0]
        for t in range(1, GROUPS):
            result = jnp.where(group == t, values[t], result)
        return result

    a, c = mine(value_a), mine(value_c)
    left, right = mine(jump), mine(jump[1:] + jump[:1])
    seg = lax.broadcasted_iota(jnp.int32, (GROUP, width), 0)
    u_t = state_ref[0] + wide(open_ref[0]) * a + wide(open_ref[2]) * c
    w_t = state_ref[1] + wide(open_ref[1]) * a + wide(open_ref[3]) * c
    jump_l = jnp.where(seg == 0, left, state_ref[2])
    jump_r = jnp.where(seg == GROUP - 1, right, state_ref[3])
    u = u_t - jump_l * (1.0 / 12.0)
    w = w_t - jump_r * (1.0 / 12.0)
    stride = send_ref.shape[0] // GROUP
    send_ref[...] = jnp.zeros(send_ref.shape, F32)
    for i in range(comps):
        for r, value in enumerate((u_t, w_t, u, w)):
            part_i = value[:, i * LANES : (i + 1) * LANES]
            send_ref[pl.ds(4 * i + r, GROUP, stride=stride), :] = part_i
    send_ref[pl.ds(4 * comps, GROUP, stride=stride), :] = jnp.broadcast_to(energy, (GROUP, LANES))


def final_kernel(recv_ref, g_ref, p_ref, q_ref, out_hbm, energy_ref, out_ref, sems):
    comps, _, lines = g_ref.shape
    row8 = lax.broadcasted_iota(jnp.int32, (8, LANES), 0)
    first, last = p_ref[...], q_ref[...]
    energy = recv_ref[0, 4 * comps : 4 * comps + 1, :]
    for j in range(1, GROUP):
        energy = energy + recv_ref[j, 4 * comps : 4 * comps + 1, :]
    energy_ref[...] = jnp.broadcast_to(energy, energy_ref.shape)

    copies = []
    for c in range(comps):
        for j in range(GROUP):
            at = slice(j * LANES, (j + 1) * LANES)
            u_t, w_t, u, w = [recv_ref[j, 4 * c + r : 4 * c + r + 1, :] for r in range(4)]
            value = g_ref[c, :, at] - first * u_t - last * w_t
            out_ref[c, 0:8, at] = jnp.where(row8 == 0, u, value[0:8])
            out_ref[c, 8 : CELLS - 8, at] = value[8 : CELLS - 8]
            out_ref[c, CELLS - 8 :, at] = jnp.where(row8 == 7, w, value[CELLS - 8 :])
        copy = pltpu.make_async_copy(out_ref.at[c], out_hbm.at[c], sems.at[c])
        copy.start()
        copies.append(copy)
    for copy in copies:
        copy.wait()


def sum_kernel(scale, parts_ref, out_ref):
    out_ref[0, 0] = jnp.sum(parts_ref[...]) * scale


def on_device(velocity, blocks):
    comps, cells, lines = velocity.shape
    width = comps * LANES
    back_rows = -(-(4 * comps + 1) // 8) * 8
    yz_count = lax.axis_size("yz")
    groups = [[GROUP * t + i for i in range(GROUP)] for t in range(GROUPS)]
    shape = functools.partial(jax.ShapeDtypeStruct, dtype=F32)

    g, send, p_rows, q_rows = pl.pallas_call(
        local_kernel,
        in_specs=[
            pl.BlockSpec(memory_space=pltpu.HBM),
            pl.BlockSpec(memory_space=pltpu.HBM),
        ],
        out_specs=[pl.BlockSpec(memory_space=pltpu.VMEM)] * 4,
        out_shape=[
            shape((comps, cells, lines)),
            shape((GROUP, 8 * (comps + 1), LANES)),
            shape((cells, LANES)),
            shape((cells, LANES)),
        ],
        scratch_shapes=[
            pltpu.VMEM((comps, cells, lines), F32),
            pltpu.VMEM((cells + 16, 6 * cells), BF16),
            pltpu.VMEM((cells, LANES), F32),
            pltpu.VMEM((cells - 2, 1, cells - 2), F32),
            pltpu.SemaphoreType.DMA((comps + 1,)),
        ],
        compiler_params=LARGE,
        name="local_solve",
    )(
        pltpu.with_memory_space_constraint(velocity, pltpu.HBM),
        pltpu.with_memory_space_constraint(jnp.transpose(blocks, (1, 0, 2)), pltpu.HBM),
    )

    recv = lax.all_to_all(send, "gx", 0, 0, axis_index_groups=groups, tiled=True)
    msg, state, opened = pl.pallas_call(
        group_kernel,
        out_shape=[
            shape((8, width + LANES)),
            shape((4, GROUP, width)),
            shape((4, GROUP, LANES)),
        ],
        compiler_params=SMALL,
        name="group_solve",
    )(recv.reshape(GROUP * 8 * (comps + 1), LANES))

    def swapped(value, mask):
        pairs = [
            (t * GROUP + i, (t ^ mask) * GROUP + i) for t in range(GROUPS) for i in range(GROUP)
        ]
        return lax.ppermute(value, "gx", pairs)

    near = swapped(msg, 1)
    far = swapped(jnp.stack([msg, near]), 3)
    send_back = pl.pallas_call(
        join_kernel,
        out_shape=shape((GROUP * back_rows, LANES)),
        scratch_shapes=[pltpu.VMEM((GROUPS, 8, width + LANES), F32)],
        compiler_params=SMALL,
        name="join_groups",
    )(msg, near, far, state, opened)
    back = lax.all_to_all(
        send_back.reshape(GROUP, back_rows, LANES), "gx", 0, 0, axis_index_groups=groups, tiled=True
    )

    derivative, energy = pl.pallas_call(
        final_kernel,
        in_specs=[pl.BlockSpec(memory_space=pltpu.VMEM)] * 4,
        out_specs=[
            pl.BlockSpec(memory_space=pltpu.HBM),
            pl.BlockSpec(memory_space=pltpu.VMEM),
        ],
        out_shape=[shape((comps, cells, lines)), shape((yz_count, LANES))],
        scratch_shapes=[
            pltpu.VMEM((comps, cells, lines), F32),
            pltpu.SemaphoreType.DMA((comps,)),
        ],
        compiler_params=LARGE,
        name="final_update",
    )(back, g, p_rows, q_rows)
    energies = lax.all_to_all(energy, "yz", 0, 0, tiled=True)
    total_count = comps * cells * lines * lax.axis_size("gx") * yz_count
    mean_square = pl.pallas_call(
        functools.partial(sum_kernel, 1.0 / total_count),
        out_specs=pl.BlockSpec(memory_space=pltpu.SMEM),
        out_shape=shape((1, 1)),
        compiler_params=SMALL,
        name="mean_square",
    )(energies)
    return derivative, mean_square[0, 0]


def solution(mesh):
    placed = (P(None, "gx", "yz"), P("gx", None, None))
    return jax.shard_map(
        on_device, mesh=mesh, in_specs=placed, out_specs=(P(None, "gx", "yz"), P()), check_vma=False
    )
```

```python
import functools

import jax
import jax.numpy as jnp
from jax import lax
from jax.experimental import pallas as pl
from jax.experimental.pallas import tpu as pltpu
from jax.sharding import PartitionSpec as P

COUPLING = 1.0 / 3.0
NEAR_WEIGHT = 7.0 / 9.0
FAR_WEIGHT = 1.0 / 36.0

GROUP = 16
GROUPS = 4
LANES = 128
CELLS = 64
CHUNK = 512
F32 = jnp.float32
BF16 = jnp.bfloat16
SMALL = pltpu.CompilerParams(vmem_limit_bytes=8 * 1024 * 1024)
LARGE = pltpu.CompilerParams(vmem_limit_bytes=16 * 1024 * 1024)


def lane_row(value, lanes=LANES):
    return jnp.broadcast_to(value, (1, lanes))


def tiled(value, copies):
    return jnp.concatenate([value] * copies, axis=1)


def parts_of(value):
    high = value.astype(BF16)
    rest = value - high.astype(F32)
    middle = rest.astype(BF16)
    return high, middle, (rest - middle.astype(F32)).astype(BF16)


def local_kernel(
    v_hbm, block_hbm, g_ref, send_ref, p_ref, q_ref, v_ref, mat_ref, pad_ref, block_ref, part_ref, sems
):
    comps, _, lines = v_ref.shape
    inner = CELLS - 2
    stride = send_ref.shape[0] // GROUP
    copies = [pltpu.make_async_copy(v_hbm.at[c], v_ref.at[c], sems.at[c]) for c in range(comps)]
    block_copy = pltpu.make_async_copy(block_hbm, block_ref, sems.at[comps])
    copies[0].start()
    block_copy.start()
    for copy in copies[1:]:
        copy.start()

    def split_right(c):
        for start in range(0, lines, CHUNK):
            at = slice(start, start + CHUNK)
            v = v_ref[c, :, at]
            edge_0, edge_1 = v[0:1], v[CELLS - 1 : CELLS]
            below_1 = jnp.concatenate([edge_0, v[: CELLS - 1]], 0)
            below_2 = jnp.concatenate([edge_0, edge_0, v[: CELLS - 2]], 0)
            above_1 = jnp.concatenate([v[1:], edge_1], 0)
            above_2 = jnp.concatenate([v[2:], edge_1, edge_1], 0)
            right = NEAR_WEIGHT * (above_1 - below_1) + FAR_WEIGHT * (above_2 - below_2)
            for i, part in enumerate(parts_of(right)):
                part_ref[c, i * CELLS : (i + 1) * CELLS, at] = part

    row8 = lax.broadcasted_iota(jnp.int32, (8, CHUNK), 0)

    def multiply(c, squares):
        for start in range(0, lines, CHUNK):
            at = slice(start, start + CHUNK)
            high = part_ref[c, 0:CELLS, at]
            middle = part_ref[c, CELLS : 2 * CELLS, at]
            low = part_ref[c, 2 * CELLS : 3 * CELLS, at]
            stacked = jnp.concatenate([high, high, high, middle, middle, low], 0)
            out = jnp.dot(mat_ref[...], stacked, preferred_element_type=F32)
            g = out[0:CELLS]
            g_ref[c, :, at] = g
            square = g * g
            tiles = [square[8 * i : 8 * i + 8] for i in range(CELLS // 8)]
            while len(tiles) > 1:
                tiles = [x + y for x, y in zip(tiles[0::2], tiles[1::2])]
            squares = squares + tiles[0]
            rows = out[CELLS : CELLS + 8]
            rows = jnp.where((row8 == 4) | (row8 == 5), pltpu.roll(v_ref[c, 0:8, at], 4, 0), rows)
            rows = jnp.where(row8 >= 6, v_ref[c, CELLS - 8 : CELLS, at], rows)
            for j in range(CHUNK // LANES):
                to = stride * (start // LANES + j) + 8 * c
                send_ref[to : to + 8, :] = rows[:, j * LANES : (j + 1) * LANES]
        return squares

    copies[0].wait()
    split_right(0)
    copies[1].wait()
    block_copy.wait()
    pad_ref[...] = jnp.zeros(pad_ref.shape, F32)
    pad_ref[0:inner, 0:inner] = block_ref[:, 0, :]
    padded = pltpu.roll(pltpu.roll(pad_ref[...], 1, 0), 1, 1)
    first = jnp.broadcast_to(COUPLING * padded[:, 1:2], (CELLS, LANES))
    last = jnp.broadcast_to(COUPLING * padded[:, inner : inner + 1], (CELLS, LANES))
    p_ref[...] = first
    q_ref[...] = last
    cols = lax.broadcasted_iota(jnp.int32, (1, LANES), 1)
    top = jnp.where(cols == 0, 1.0, 0.0) - COUPLING * padded[1:2]
    bottom = jnp.where(cols == CELLS - 1, 1.0, 0.0) - COUPLING * padded[inner : inner + 1]
    first_sum = jnp.sum(first * padded, axis=0, keepdims=True)
    last_sum = jnp.sum(last * padded, axis=0, keepdims=True)
    rows = lax.broadcasted_iota(jnp.int32, (16, LANES), 0)
    extra = jnp.where(rows == 0, top, 0.0)
    extra = jnp.where(rows == 1, bottom, extra)
    extra = jnp.where(rows == 2, first_sum, extra)
    extra = jnp.where(rows == 3, last_sum, extra)
    matrix = jnp.concatenate([padded, extra], 0)
    high, middle, low = parts_of(matrix[:, 0:CELLS])
    mat_ref[...] = jnp.concatenate([high, middle, low, high, middle, high], 1)
    split_right(1)
    squares = multiply(0, jnp.zeros((8, CHUNK), F32))
    for c in range(2, comps):
        copies[c].wait()
        split_right(c)
        squares = multiply(c - 1, squares)
    squares = multiply(comps - 1, squares)

    energy = squares[:, 0:LANES]
    for j in range(1, CHUNK // LANES):
        energy = energy + squares[:, j * LANES : (j + 1) * LANES]
    energy = jnp.sum(energy, axis=0, keepdims=True)
    coefs = energy + pltpu.roll(energy, LANES // 2, 1)
    numbers = [
        first[1:2],
        last[1:2],
        first[inner : inner + 1],
        last[inner : inner + 1],
        jnp.sum(first * first, axis=0, keepdims=True),
        jnp.sum(first * last, axis=0, keepdims=True),
        jnp.sum(last * last, axis=0, keepdims=True),
    ]
    for i, number in enumerate(numbers):
        coefs = jnp.where(cols == i, number, coefs)
    for j in range(GROUP):
        to = stride * j + 8 * comps
        send_ref[to : to + 1, :] = coefs


def group_kernel(recv_ref, msg_ref, state_ref, open_ref):
    stride = recv_ref.shape[0] // GROUP
    comps = stride // 8
    width = comps * LANES

    def rows(r):
        parts = [recv_ref[pl.ds(8 * i + r, GROUP, stride=stride), :] for i in range(comps)]
        return jnp.concatenate(parts, 1)

    numbers = recv_ref[pl.ds(8 * comps, GROUP, stride=stride), :]

    def coef(r):
        return jnp.broadcast_to(numbers[:, r : r + 1], (GROUP, LANES))

    seg = lax.broadcasted_iota(jnp.int32, (GROUP, width), 0)
    seg_1 = lax.broadcasted_iota(jnp.int32, (GROUP, LANES), 0)

    def prev(x, s=1):
        return pltpu.roll(x, s, 0)

    def following(x, s=1):
        return pltpu.roll(x, GROUP - s, 0)

    b_first, b_last, pg, qg, v_0, v_1, v_62, v_63 = [rows(r) for r in range(8)]
    p_0, q_0, p_61, q_61, pp, pq, qq = [coef(r) for r in range(7)]
    upper = lax.broadcasted_iota(jnp.int32, (GROUP, LANES), 1) >= LANES // 2
    energy = jnp.where(upper, numbers, 0.0)
    jump_l = jnp.where(seg == 0, 0.0, prev(v_63) - v_0)
    jump_l2 = jnp.where(seg == 0, 0.0, prev(v_62) - v_0)
    jump_r = jnp.where(seg == GROUP - 1, 0.0, v_63 - following(v_0))
    jump_r2 = jnp.where(seg == GROUP - 1, 0.0, following(v_1) - v_63)
    b_first = b_first - (2.0 / 3.0) * jump_l - FAR_WEIGHT * jump_l2
    b_last = b_last - (2.0 / 3.0) * jump_r + FAR_WEIGHT * jump_r2

    unit_first = jnp.where(seg_1 == 0, 1.0, 0.0)
    unit_last = jnp.where(seg_1 == GROUP - 1, 1.0, 0.0)
    zero = jnp.zeros((GROUP, LANES), F32)
    third = jnp.full((GROUP, LANES), COUPLING, F32)
    rhs_f = jnp.concatenate([b_first, unit_first, zero], 1)
    rhs_l = jnp.concatenate([b_last, zero, unit_last], 1)
    f = (jnp.where(seg_1 == 0, 0.0, third), 1.0 - COUPLING * p_0, -COUPLING * q_0, rhs_f)
    l = (-COUPLING * p_61, 1.0 - COUPLING * q_61, jnp.where(seg_1 == GROUP - 1, 0.0, third), rhs_l)

    def reduce_level(mine, below, above):
        ratio_low = mine[0] / below[1]
        ratio_high = mine[2] / above[1]
        return (
            -ratio_low * below[0],
            mine[1] - ratio_low * below[2] - ratio_high * above[0],
            -ratio_high * above[2],
            mine[3] - tiled(ratio_low, comps + 2) * below[3] - tiled(ratio_high, comps + 2) * above[3],
        )

    f, l = (
        reduce_level(f, tuple(prev(x) for x in l), l),
        reduce_level(l, f, tuple(following(x) for x in f)),
    )
    step = 1
    while step < GROUP:
        f = reduce_level(f, tuple(prev(x, step) for x in f), tuple(following(x, step) for x in f))
        l = reduce_level(l, tuple(prev(x, step) for x in l), tuple(following(x, step) for x in l))
        step *= 2
    sol_f = f[3] / tiled(f[1], comps + 2)
    sol_l = l[3] / tiled(l[1], comps + 2)
    x_f, a_f, c_f = sol_f[:, :width], sol_f[:, width : width + LANES], sol_f[:, width + LANES :]
    x_l, a_l, c_l = sol_l[:, :width], sol_l[:, width : width + LANES], sol_l[:, width + LANES :]

    pp1, qq1 = pp + 1.0, qq + 1.0
    d_l, d_r = jump_l * (1.0 / 12.0), jump_r * (1.0 / 12.0)
    pq_w = tiled(pq, comps)
    m_f = tiled(pp1, comps) * x_f + pq_w * x_l - pg - d_l
    m_l = tiled(qq1, comps) * x_l + pq_w * x_f - qg - d_r

    def total(x):
        return jnp.sum(x, axis=0, keepdims=True)

    line_a = 2.0 * total(tiled(a_f, comps) * m_f + tiled(a_l, comps) * m_l)
    line_c = 2.0 * total(tiled(c_f, comps) * m_f + tiled(c_l, comps) * m_l)
    base = total(x_f * (m_f - pg - d_l) + x_l * (m_l - qg - d_r) + d_l * d_l + d_r * d_r)
    part = total(energy) * (1.0 / GROUP)
    for i in range(comps):
        part = part + base[:, i * LANES : (i + 1) * LANES]
    quad_aa = total(pp1 * a_f * a_f + 2.0 * pq * a_f * a_l + qq1 * a_l * a_l)
    quad_ac = total(pp1 * a_f * c_f + pq * (a_f * c_l + a_l * c_f) + qq1 * a_l * c_l)
    quad_cc = total(pp1 * c_f * c_f + 2.0 * pq * c_f * c_l + qq1 * c_l * c_l)

    end = GROUP - 1
    msg_ref[:, 0:width] = jnp.concatenate(
        [x_f[0:1], x_l[end:], line_a, line_c, v_0[0:1], v_1[0:1], v_62[end:], v_63[end:]], 0
    )
    msg_ref[:, width : width + LANES] = jnp.concatenate(
        [a_f[0:1], a_l[end:], c_f[0:1], c_l[end:], quad_aa, quad_ac, quad_cc, part], 0
    )
    state_ref[0] = x_f
    state_ref[1] = x_l
    state_ref[2] = jump_l
    state_ref[3] = jump_r
    open_ref[0] = a_f
    open_ref[1] = a_l
    open_ref[2] = c_f
    open_ref[3] = c_l


def eliminate(matrix, rhs, wide):
    size = len(rhs)
    matrix = [list(r) for r in matrix]
    rhs = list(rhs)
    inverse = [None] * size
    for k in range(size):
        inverse[k] = 1.0 / matrix[k][k]
        for i in range(k + 1, size):
            if matrix[i][k] is None:
                continue
            ratio = matrix[i][k] * inverse[k]
            for j in range(k + 1, size):
                if matrix[k][j] is not None:
                    old = matrix[i][j]
                    change = ratio * matrix[k][j]
                    matrix[i][j] = -change if old is None else old - change
            rhs[i] = rhs[i] - wide(ratio) * rhs[k]
    found = [None] * size
    for k in reversed(range(size)):
        value = rhs[k]
        for j in range(k + 1, size):
            if matrix[k][j] is not None:
                value = value - wide(matrix[k][j]) * found[j]
        found[k] = value * wide(inverse[k])
    return found


def join_kernel(own_ref, near_ref, far_ref, state_ref, open_ref, send_ref, all_ref):
    width = state_ref.shape[2]
    comps = width // LANES
    group = lax.axis_index("gx") // GROUP
    all_ref[0] = own_ref[...]
    all_ref[1] = near_ref[...]
    all_ref[2] = far_ref[1]
    all_ref[3] = far_ref[0]

    def wide(x):
        return tiled(x, comps)

    tile = []
    for t in range(GROUPS):
        own = group % 4
        slot = jnp.where(own >= 2, (t // 2) ^ 1, t // 2) * 2 + jnp.where(own % 2 == 1, (t % 2) ^ 1, t % 2)
        tile.append(all_ref[slot])
    data = [[m[r : r + 1, 0:width] for r in range(8)] for m in tile]
    scal = [[m[r : r + 1, width:] for r in range(8)] for m in tile]
    x_f, x_l, line_a, line_c, v_0, v_1, v_62, v_63 = [[d[r] for d in data] for r in range(8)]
    a_f, a_l, c_f, c_l, q_aa, q_ac, q_cc, part = [[s[r] for s in scal] for r in range(8)]

    one = jnp.ones((1, LANES), F32)
    jump = [v_63[t - 1] - v_0[t] for t in range(GROUPS)]
    matrix, rhs = [], []
    for t in range(GROUPS):
        before, after = (t - 1) % GROUPS, (t + 1) % GROUPS
        row_a, row_c = [None] * (2 * GROUPS), [None] * (2 * GROUPS)
        row_a[2 * t] = one
        row_a[2 * before] = COUPLING * a_l[before]
        row_a[2 * before + 1] = COUPLING * c_l[before]
        row_c[2 * t + 1] = one
        row_c[2 * after] = COUPLING * a_f[after]
        row_c[2 * after + 1] = COUPLING * c_f[after]
        matrix += [row_a, row_c]
        rhs.append(
            -COUPLING * x_l[before] - (2.0 / 3.0) * jump[t] - FAR_WEIGHT * (v_62[before] - v_0[t])
        )
        rhs.append(
            -COUPLING * x_f[after] - (2.0 / 3.0) * jump[after] + FAR_WEIGHT * (v_1[after] - v_63[t])
        )
    found = eliminate(matrix, rhs, wide)
    value_a, value_c = found[0::2], found[1::2]

    energy = jnp.zeros((1, LANES), F32)
    for t in range(GROUPS):
        a, c = value_a[t], value_c[t]
        after = (t + 1) % GROUPS
        u_end = x_f[t] + wide(a_f[t]) * a + wide(c_f[t]) * c
        w_end = x_l[t] + wide(a_l[t]) * a + wide(c_l[t]) * c
        d_l, d_r = jump[t] * (1.0 / 12.0), jump[after] * (1.0 / 12.0)
        lines = a * (line_a[t] + wide(q_aa[t]) * a + wide(2.0 * q_ac[t]) * c)
        lines = lines + c * (line_c[t] + wide(q_cc[t]) * c)
        lines = lines + d_l * (d_l - 2.0 * u_end) + d_r * (d_r - 2.0 * w_end)
        energy = energy + part[t]
        for i in range(comps):
            energy = energy + lines[:, i * LANES : (i + 1) * LANES]

    def mine(values):
        result = values[0]
        for t in range(1, GROUPS):
            result = jnp.where(group == t, values[t], result)
        return result

    a, c = mine(value_a), mine(value_c)
    left, right = mine(jump), mine(jump[1:] + jump[:1])
    seg = lax.broadcasted_iota(jnp.int32, (GROUP, width), 0)
    u_t = state_ref[0] + wide(open_ref[0]) * a + wide(open_ref[2]) * c
    w_t = state_ref[1] + wide(open_ref[1]) * a + wide(open_ref[3]) * c
    jump_l = jnp.where(seg == 0, left, state_ref[2])
    jump_r = jnp.where(seg == GROUP - 1, right, state_ref[3])
    u = u_t - jump_l * (1.0 / 12.0)
    w = w_t - jump_r * (1.0 / 12.0)
    stride = send_ref.shape[0] // GROUP
    for i in range(comps):
        for r, value in enumerate((u_t, w_t, u, w)):
            part_i = value[:, i * LANES : (i + 1) * LANES]
            send_ref[pl.ds(4 * i + r, GROUP, stride=stride), :] = part_i
    send_ref[pl.ds(4 * comps, GROUP, stride=stride), :] = jnp.broadcast_to(energy, (GROUP, LANES))


def energy_kernel(recv_ref, out_ref):
    stride = recv_ref.shape[0] // GROUP
    energy = recv_ref[pl.ds(stride - 1, GROUP, stride=stride), :]
    out_ref[...] = jnp.broadcast_to(jnp.sum(energy, axis=0, keepdims=True), out_ref.shape)


def final_kernel(scale, recv_ref, energy_ref, g_ref, p_ref, q_ref, out_hbm, mean_ref, out_ref, sems):
    comps, _, lines = g_ref.shape
    stride = recv_ref.shape[0] // GROUP
    row8 = lax.broadcasted_iota(jnp.int32, (8, LANES), 0)
    first, last = p_ref[...], q_ref[...]
    copies = []
    for c in range(comps):
        for j in range(GROUP):
            at = slice(j * LANES, (j + 1) * LANES)
            base = stride * j + 4 * c
            u_t, w_t, u, w = [recv_ref[base + r : base + r + 1, :] for r in range(4)]
            value = g_ref[c, :, at] - first * u_t - last * w_t
            out_ref[c, 0:8, at] = jnp.where(row8 == 0, u, value[0:8])
            out_ref[c, 8 : CELLS - 8, at] = value[8 : CELLS - 8]
            out_ref[c, CELLS - 8 :, at] = jnp.where(row8 == 7, w, value[CELLS - 8 :])
        copy = pltpu.make_async_copy(out_ref.at[c], out_hbm.at[c], sems.at[c])
        copy.start()
        copies.append(copy)
    mean_ref[0, 0] = jnp.sum(energy_ref[...]) * scale
    for copy in copies:
        copy.wait()


def on_device(velocity, blocks):
    comps, cells, lines = velocity.shape
    width = comps * LANES
    send_rows, back_rows = 8 * comps + 1, 4 * comps + 1
    yz_count = lax.axis_size("yz")
    groups = [[GROUP * t + i for i in range(GROUP)] for t in range(GROUPS)]
    shape = functools.partial(jax.ShapeDtypeStruct, dtype=F32)

    g, send, p_rows, q_rows = pl.pallas_call(
        local_kernel,
        in_specs=[
            pl.BlockSpec(memory_space=pltpu.HBM),
            pl.BlockSpec(memory_space=pltpu.HBM),
        ],
        out_specs=[pl.BlockSpec(memory_space=pltpu.VMEM)] * 4,
        out_shape=[
            shape((comps, cells, lines)),
            shape((GROUP * send_rows, LANES)),
            shape((cells, LANES)),
            shape((cells, LANES)),
        ],
        scratch_shapes=[
            pltpu.VMEM((comps, cells, lines), F32),
            pltpu.VMEM((cells + 16, 6 * cells), BF16),
            pltpu.VMEM((cells, LANES), F32),
            pltpu.VMEM((cells - 2, 1, cells - 2), F32),
            pltpu.VMEM((comps, 3 * cells, lines), BF16),
            pltpu.SemaphoreType.DMA((comps + 1,)),
        ],
        compiler_params=LARGE,
        name="local_solve",
    )(
        pltpu.with_memory_space_constraint(velocity, pltpu.HBM),
        pltpu.with_memory_space_constraint(jnp.transpose(blocks, (1, 0, 2)), pltpu.HBM),
    )

    def spread(value, axis, **kwargs):
        rows = value.reshape(value.shape[0], 1, LANES)
        return lax.all_to_all(rows, axis, 0, 0, tiled=True, **kwargs).reshape(value.shape)

    recv = spread(send, "gx", axis_index_groups=groups)
    msg, state, opened = pl.pallas_call(
        group_kernel,
        out_shape=[
            shape((8, width + LANES)),
            shape((4, GROUP, width)),
            shape((4, GROUP, LANES)),
        ],
        compiler_params=SMALL,
        name="group_solve",
    )(recv)

    def swapped(value, mask):
        pairs = [
            (t * GROUP + i, (t ^ mask) * GROUP + i) for t in range(GROUPS) for i in range(GROUP)
        ]
        return lax.ppermute(value, "gx", pairs)

    near = swapped(msg, 1)
    far = swapped(jnp.stack([msg, near]), 3)
    send_back = pl.pallas_call(
        join_kernel,
        out_shape=shape((GROUP * back_rows, LANES)),
        scratch_shapes=[pltpu.VMEM((GROUPS, 8, width + LANES), F32)],
        compiler_params=SMALL,
        name="join_groups",
    )(msg, near, far, state, opened)
    back = spread(send_back, "gx", axis_index_groups=groups)
    energy = pl.pallas_call(
        energy_kernel,
        out_shape=shape((yz_count, LANES)),
        compiler_params=SMALL,
        name="line_energy",
    )(back)
    energies = spread(energy, "yz")
    total_count = comps * cells * lines * lax.axis_size("gx") * yz_count
    derivative, mean_square = pl.pallas_call(
        functools.partial(final_kernel, 1.0 / total_count),
        in_specs=[pl.BlockSpec(memory_space=pltpu.VMEM)] * 5,
        out_specs=[
            pl.BlockSpec(memory_space=pltpu.HBM),
            pl.BlockSpec(memory_space=pltpu.SMEM),
        ],
        out_shape=[shape((comps, cells, lines)), shape((1, 1))],
        scratch_shapes=[
            pltpu.VMEM((comps, cells, lines), F32),
            pltpu.SemaphoreType.DMA((comps,)),
        ],
        compiler_params=LARGE,
        name="final_update",
    )(back, energies, g, p_rows, q_rows)
    return derivative, mean_square[0, 0]


def solution(mesh):
    placed = (P(None, "gx", "yz"), P("gx", None, None))
    return jax.shard_map(
        on_device, mesh=mesh, in_specs=placed, out_specs=(P(None, "gx", "yz"), P()), check_vma=False
    )
```

```python
import functools

import jax
import jax.numpy as jnp
from jax import lax
from jax.experimental import pallas as pl
from jax.experimental.pallas import tpu as pltpu
from jax.sharding import PartitionSpec as P

COUPLING = 1.0 / 3.0
NEAR_WEIGHT = 7.0 / 9.0
FAR_WEIGHT = 1.0 / 36.0

GROUP = 16
GROUPS = 4
LANES = 128
CELLS = 64
CHUNK = 512
F32 = jnp.float32
BF16 = jnp.bfloat16
SMALL = pltpu.CompilerParams(vmem_limit_bytes=8 * 1024 * 1024)
LARGE = pltpu.CompilerParams(vmem_limit_bytes=16 * 1024 * 1024)


def lane_row(value, lanes=LANES):
    return jnp.broadcast_to(value, (1, lanes))


def tiled(value, copies):
    return jnp.concatenate([value] * copies, axis=1)


def parts_of(value):
    high = value.astype(BF16)
    rest = value - high.astype(F32)
    middle = rest.astype(BF16)
    return high, middle, (rest - middle.astype(F32)).astype(BF16)


def local_kernel(
    v_hbm, block_hbm, g_ref, send_ref, p_ref, q_ref, v_ref, mat_ref, pad_ref, block_ref, sems
):
    comps, _, lines = v_ref.shape
    inner = CELLS - 2
    stride = send_ref.shape[0] // GROUP
    block_copy = pltpu.make_async_copy(block_hbm, block_ref, sems.at[comps])
    block_copy.start()
    copies = [pltpu.make_async_copy(v_hbm.at[c], v_ref.at[c], sems.at[c]) for c in range(comps)]
    for copy in copies:
        copy.start()

    pad_ref[...] = jnp.zeros(pad_ref.shape, F32)
    block_copy.wait()
    pad_ref[0:inner, 0:inner] = block_ref[:, 0, :]
    padded = pltpu.roll(pltpu.roll(pad_ref[...], 1, 0), 1, 1)
    first = jnp.broadcast_to(COUPLING * padded[:, 1:2], (CELLS, LANES))
    last = jnp.broadcast_to(COUPLING * padded[:, inner : inner + 1], (CELLS, LANES))
    p_ref[...] = first
    q_ref[...] = last
    cols = lax.broadcasted_iota(jnp.int32, (1, LANES), 1)
    top = jnp.where(cols == 0, 1.0, 0.0) - COUPLING * padded[1:2]
    bottom = jnp.where(cols == CELLS - 1, 1.0, 0.0) - COUPLING * padded[inner : inner + 1]
    first_sum = jnp.sum(first * padded, axis=0, keepdims=True)
    last_sum = jnp.sum(last * padded, axis=0, keepdims=True)
    rows = lax.broadcasted_iota(jnp.int32, (16, LANES), 0)
    extra = jnp.where(rows == 0, top, 0.0)
    extra = jnp.where(rows == 1, bottom, extra)
    extra = jnp.where(rows == 2, first_sum, extra)
    extra = jnp.where(rows == 3, last_sum, extra)
    matrix = jnp.concatenate([padded, extra], 0)
    high, middle, low = parts_of(matrix[:, 0:CELLS])
    mat_ref[...] = jnp.concatenate([high, middle, low, high, middle, high], 1)

    row8 = lax.broadcasted_iota(jnp.int32, (8, CHUNK), 0)
    energy = jnp.zeros((1, LANES), F32)
    for c in range(comps):
        copies[c].wait()
        for start in range(0, lines, CHUNK):
            v = v_ref[c, :, start : start + CHUNK]
            edge_0, edge_1 = v[0:1], v[CELLS - 1 : CELLS]
            below_1 = jnp.concatenate([edge_0, v[: CELLS - 1]], 0)
            below_2 = jnp.concatenate([edge_0, edge_0, v[: CELLS - 2]], 0)
            above_1 = jnp.concatenate([v[1:], edge_1], 0)
            above_2 = jnp.concatenate([v[2:], edge_1, edge_1], 0)
            right = NEAR_WEIGHT * (above_1 - below_1) + FAR_WEIGHT * (above_2 - below_2)
            high, middle, low = parts_of(right)
            stacked = jnp.concatenate([high, high, high, middle, middle, low], 0)
            out = jnp.dot(mat_ref[...], stacked, preferred_element_type=F32)
            g = out[0:CELLS]
            g_ref[c, :, start : start + CHUNK] = g
            squares = jnp.sum(g * g, axis=0, keepdims=True)
            rows = out[CELLS : CELLS + 8]
            rows = jnp.where((row8 == 4) | (row8 == 5), pltpu.roll(v[0:8], 4, 0), rows)
            rows = jnp.where(row8 >= 6, v[CELLS - 8 : CELLS], rows)
            for j in range(CHUNK // LANES):
                at = slice(j * LANES, (j + 1) * LANES)
                energy = energy + squares[:, at]
                to = stride * (start // LANES + j) + 8 * c
                send_ref[to : to + 8, :] = rows[:, at]

    coefs = energy + pltpu.roll(energy, LANES // 2, 1)
    numbers = [
        first[1:2],
        last[1:2],
        first[inner : inner + 1],
        last[inner : inner + 1],
        jnp.sum(first * first, axis=0, keepdims=True),
        jnp.sum(first * last, axis=0, keepdims=True),
        jnp.sum(last * last, axis=0, keepdims=True),
    ]
    for i, number in enumerate(numbers):
        coefs = jnp.where(cols == i, number, coefs)
    for j in range(GROUP):
        to = stride * j + 8 * comps
        send_ref[to : to + 1, :] = coefs


def group_kernel(recv_ref, msg_ref, state_ref, open_ref):
    stride = recv_ref.shape[0] // GROUP
    comps = stride // 8
    width = comps * LANES

    def rows(r):
        parts = [recv_ref[pl.ds(8 * i + r, GROUP, stride=stride), :] for i in range(comps)]
        return jnp.concatenate(parts, 1)

    numbers = recv_ref[pl.ds(8 * comps, GROUP, stride=stride), :]

    def coef(r):
        return jnp.broadcast_to(numbers[:, r : r + 1], (GROUP, LANES))

    seg = lax.broadcasted_iota(jnp.int32, (GROUP, width), 0)
    seg_1 = lax.broadcasted_iota(jnp.int32, (GROUP, LANES), 0)

    def prev(x, s=1):
        return pltpu.roll(x, s, 0)

    def following(x, s=1):
        return pltpu.roll(x, GROUP - s, 0)

    b_first, b_last, pg, qg, v_0, v_1, v_62, v_63 = [rows(r) for r in range(8)]
    p_0, q_0, p_61, q_61, pp, pq, qq = [coef(r) for r in range(7)]
    upper = lax.broadcasted_iota(jnp.int32, (GROUP, LANES), 1) >= LANES // 2
    energy = jnp.where(upper, numbers, 0.0)
    jump_l = jnp.where(seg == 0, 0.0, prev(v_63) - v_0)
    jump_l2 = jnp.where(seg == 0, 0.0, prev(v_62) - v_0)
    jump_r = jnp.where(seg == GROUP - 1, 0.0, v_63 - following(v_0))
    jump_r2 = jnp.where(seg == GROUP - 1, 0.0, following(v_1) - v_63)
    b_first = b_first - (2.0 / 3.0) * jump_l - FAR_WEIGHT * jump_l2
    b_last = b_last - (2.0 / 3.0) * jump_r + FAR_WEIGHT * jump_r2

    unit_first = jnp.where(seg_1 == 0, 1.0, 0.0)
    unit_last = jnp.where(seg_1 == GROUP - 1, 1.0, 0.0)
    zero = jnp.zeros((GROUP, LANES), F32)
    third = jnp.full((GROUP, LANES), COUPLING, F32)
    rhs_f = jnp.concatenate([b_first, unit_first, zero], 1)
    rhs_l = jnp.concatenate([b_last, zero, unit_last], 1)
    f = (jnp.where(seg_1 == 0, 0.0, third), 1.0 - COUPLING * p_0, -COUPLING * q_0, rhs_f)
    l = (-COUPLING * p_61, 1.0 - COUPLING * q_61, jnp.where(seg_1 == GROUP - 1, 0.0, third), rhs_l)

    def reduce_level(mine, below, above):
        ratio_low = mine[0] / below[1]
        ratio_high = mine[2] / above[1]
        return (
            -ratio_low * below[0],
            mine[1] - ratio_low * below[2] - ratio_high * above[0],
            -ratio_high * above[2],
            mine[3] - tiled(ratio_low, comps + 2) * below[3] - tiled(ratio_high, comps + 2) * above[3],
        )

    f, l = (
        reduce_level(f, tuple(prev(x) for x in l), l),
        reduce_level(l, f, tuple(following(x) for x in f)),
    )
    step = 1
    while step < GROUP:
        f = reduce_level(f, tuple(prev(x, step) for x in f), tuple(following(x, step) for x in f))
        l = reduce_level(l, tuple(prev(x, step) for x in l), tuple(following(x, step) for x in l))
        step *= 2
    sol_f = f[3] / tiled(f[1], comps + 2)
    sol_l = l[3] / tiled(l[1], comps + 2)
    x_f, a_f, c_f = sol_f[:, :width], sol_f[:, width : width + LANES], sol_f[:, width + LANES :]
    x_l, a_l, c_l = sol_l[:, :width], sol_l[:, width : width + LANES], sol_l[:, width + LANES :]

    pp1, qq1 = pp + 1.0, qq + 1.0
    d_l, d_r = jump_l * (1.0 / 12.0), jump_r * (1.0 / 12.0)
    pq_w = tiled(pq, comps)
    m_f = tiled(pp1, comps) * x_f + pq_w * x_l - pg - d_l
    m_l = tiled(qq1, comps) * x_l + pq_w * x_f - qg - d_r

    def total(x):
        return jnp.sum(x, axis=0, keepdims=True)

    line_a = 2.0 * total(tiled(a_f, comps) * m_f + tiled(a_l, comps) * m_l)
    line_c = 2.0 * total(tiled(c_f, comps) * m_f + tiled(c_l, comps) * m_l)
    base = total(x_f * (m_f - pg - d_l) + x_l * (m_l - qg - d_r) + d_l * d_l + d_r * d_r)
    part = total(energy) * (1.0 / GROUP)
    for i in range(comps):
        part = part + base[:, i * LANES : (i + 1) * LANES]
    quad_aa = total(pp1 * a_f * a_f + 2.0 * pq * a_f * a_l + qq1 * a_l * a_l)
    quad_ac = total(pp1 * a_f * c_f + pq * (a_f * c_l + a_l * c_f) + qq1 * a_l * c_l)
    quad_cc = total(pp1 * c_f * c_f + 2.0 * pq * c_f * c_l + qq1 * c_l * c_l)

    end = GROUP - 1
    msg_ref[:, 0:width] = jnp.concatenate(
        [x_f[0:1], x_l[end:], line_a, line_c, v_0[0:1], v_1[0:1], v_62[end:], v_63[end:]], 0
    )
    msg_ref[:, width : width + LANES] = jnp.concatenate(
        [a_f[0:1], a_l[end:], c_f[0:1], c_l[end:], quad_aa, quad_ac, quad_cc, part], 0
    )
    state_ref[0] = x_f
    state_ref[1] = x_l
    state_ref[2] = jump_l
    state_ref[3] = jump_r
    open_ref[0] = a_f
    open_ref[1] = a_l
    open_ref[2] = c_f
    open_ref[3] = c_l


def eliminate(matrix, rhs, wide):
    size = len(rhs)
    matrix = [list(r) for r in matrix]
    rhs = list(rhs)
    inverse = [None] * size
    for k in range(size):
        inverse[k] = 1.0 / matrix[k][k]
        for i in range(k + 1, size):
            if matrix[i][k] is None:
                continue
            ratio = matrix[i][k] * inverse[k]
            for j in range(k + 1, size):
                if matrix[k][j] is not None:
                    old = matrix[i][j]
                    change = ratio * matrix[k][j]
                    matrix[i][j] = -change if old is None else old - change
            rhs[i] = rhs[i] - wide(ratio) * rhs[k]
    found = [None] * size
    for k in reversed(range(size)):
        value = rhs[k]
        for j in range(k + 1, size):
            if matrix[k][j] is not None:
                value = value - wide(matrix[k][j]) * found[j]
        found[k] = value * wide(inverse[k])
    return found


def join_kernel(all_ref, state_ref, open_ref, send_ref):
    width = state_ref.shape[2]
    comps = width // LANES
    group = lax.axis_index("gx") // GROUP

    def wide(x):
        return tiled(x, comps)

    tile = [all_ref[t] for t in range(GROUPS)]
    data = [[m[r : r + 1, 0:width] for r in range(8)] for m in tile]
    scal = [[m[r : r + 1, width:] for r in range(8)] for m in tile]
    x_f, x_l, line_a, line_c, v_0, v_1, v_62, v_63 = [[d[r] for d in data] for r in range(8)]
    a_f, a_l, c_f, c_l, q_aa, q_ac, q_cc, part = [[s[r] for s in scal] for r in range(8)]

    one = jnp.ones((1, LANES), F32)
    jump = [v_63[t - 1] - v_0[t] for t in range(GROUPS)]
    matrix, rhs = [], []
    for t in range(GROUPS):
        before, after = (t - 1) % GROUPS, (t + 1) % GROUPS
        row_a, row_c = [None] * (2 * GROUPS), [None] * (2 * GROUPS)
        row_a[2 * t] = one
        row_a[2 * before] = COUPLING * a_l[before]
        row_a[2 * before + 1] = COUPLING * c_l[before]
        row_c[2 * t + 1] = one
        row_c[2 * after] = COUPLING * a_f[after]
        row_c[2 * after + 1] = COUPLING * c_f[after]
        matrix += [row_a, row_c]
        rhs.append(
            -COUPLING * x_l[before] - (2.0 / 3.0) * jump[t] - FAR_WEIGHT * (v_62[before] - v_0[t])
        )
        rhs.append(
            -COUPLING * x_f[after] - (2.0 / 3.0) * jump[after] + FAR_WEIGHT * (v_1[after] - v_63[t])
        )
    found = eliminate(matrix, rhs, wide)
    value_a, value_c = found[0::2], found[1::2]

    energy = jnp.zeros((1, LANES), F32)
    for t in range(GROUPS):
        a, c = value_a[t], value_c[t]
        after = (t + 1) % GROUPS
        u_end = x_f[t] + wide(a_f[t]) * a + wide(c_f[t]) * c
        w_end = x_l[t] + wide(a_l[t]) * a + wide(c_l[t]) * c
        d_l, d_r = jump[t] * (1.0 / 12.0), jump[after] * (1.0 / 12.0)
        lines = a * (line_a[t] + wide(q_aa[t]) * a + wide(2.0 * q_ac[t]) * c)
        lines = lines + c * (line_c[t] + wide(q_cc[t]) * c)
        lines = lines + d_l * (d_l - 2.0 * u_end) + d_r * (d_r - 2.0 * w_end)
        energy = energy + part[t]
        for i in range(comps):
            energy = energy + lines[:, i * LANES : (i + 1) * LANES]

    def mine(values):
        result = values[0]
        for t in range(1, GROUPS):
            result = jnp.where(group == t, values[t], result)
        return result

    a, c = mine(value_a), mine(value_c)
    left, right = mine(jump), mine(jump[1:] + jump[:1])
    seg = lax.broadcasted_iota(jnp.int32, (GROUP, width), 0)
    u_t = state_ref[0] + wide(open_ref[0]) * a + wide(open_ref[2]) * c
    w_t = state_ref[1] + wide(open_ref[1]) * a + wide(open_ref[3]) * c
    jump_l = jnp.where(seg == 0, left, state_ref[2])
    jump_r = jnp.where(seg == GROUP - 1, right, state_ref[3])
    u = u_t - jump_l * (1.0 / 12.0)
    w = w_t - jump_r * (1.0 / 12.0)
    stride = send_ref.shape[0] // GROUP
    for i in range(comps):
        for r, value in enumerate((u_t, w_t, u, w)):
            part_i = value[:, i * LANES : (i + 1) * LANES]
            send_ref[pl.ds(4 * i + r, GROUP, stride=stride), :] = part_i
    send_ref[pl.ds(4 * comps, GROUP, stride=stride), :] = jnp.broadcast_to(energy, (GROUP, LANES))


def energy_kernel(recv_ref, out_ref):
    stride = recv_ref.shape[0] // GROUP
    energy = recv_ref[pl.ds(stride - 1, GROUP, stride=stride), :]
    out_ref[...] = jnp.broadcast_to(jnp.sum(energy, axis=0, keepdims=True), out_ref.shape)


def final_kernel(scale, recv_ref, energy_ref, g_ref, p_ref, q_ref, out_hbm, mean_hbm, out_ref, mean_ref, sems):
    comps, _, lines = g_ref.shape
    stride = recv_ref.shape[0] // GROUP
    row8 = lax.broadcasted_iota(jnp.int32, (8, LANES), 0)
    first, last = p_ref[...], q_ref[...]
    mean_ref[0, 0] = jnp.sum(energy_ref[...]) * scale
    copies = [pltpu.make_async_copy(mean_ref, mean_hbm, sems.at[comps])]
    copies[0].start()
    for c in range(comps):
        for j in range(GROUP):
            at = slice(j * LANES, (j + 1) * LANES)
            base = stride * j + 4 * c
            u_t, w_t, u, w = [recv_ref[base + r : base + r + 1, :] for r in range(4)]
            value = g_ref[c, :, at] - first * u_t - last * w_t
            out_ref[c, 0:8, at] = jnp.where(row8 == 0, u, value[0:8])
            out_ref[c, 8 : CELLS - 8, at] = value[8 : CELLS - 8]
            out_ref[c, CELLS - 8 :, at] = jnp.where(row8 == 7, w, value[CELLS - 8 :])
        copy = pltpu.make_async_copy(out_ref.at[c], out_hbm.at[c], sems.at[c])
        copy.start()
        copies.append(copy)
    for copy in copies:
        copy.wait()


def on_device(velocity, blocks):
    comps, cells, lines = velocity.shape
    width = comps * LANES
    send_rows, back_rows = 8 * comps + 1, 4 * comps + 1
    yz_count = lax.axis_size("yz")
    groups = [[GROUP * t + i for i in range(GROUP)] for t in range(GROUPS)]
    shape = functools.partial(jax.ShapeDtypeStruct, dtype=F32)

    g, send, p_rows, q_rows = pl.pallas_call(
        local_kernel,
        in_specs=[
            pl.BlockSpec(memory_space=pltpu.HBM),
            pl.BlockSpec(memory_space=pltpu.HBM),
        ],
        out_specs=[pl.BlockSpec(memory_space=pltpu.VMEM)] * 4,
        out_shape=[
            shape((comps, cells, lines)),
            shape((GROUP * send_rows, LANES)),
            shape((cells, LANES)),
            shape((cells, LANES)),
        ],
        scratch_shapes=[
            pltpu.VMEM((comps, cells, lines), F32),
            pltpu.VMEM((cells + 16, 6 * cells), BF16),
            pltpu.VMEM((cells, LANES), F32),
            pltpu.VMEM((cells - 2, 1, cells - 2), F32),
            pltpu.SemaphoreType.DMA((comps + 1,)),
        ],
        compiler_params=LARGE,
        name="local_solve",
    )(
        pltpu.with_memory_space_constraint(velocity, pltpu.HBM),
        pltpu.with_memory_space_constraint(jnp.transpose(blocks, (1, 0, 2)), pltpu.HBM),
    )

    def spread(value, axis, **kwargs):
        rows = value.reshape(value.shape[0], 1, LANES)
        return lax.all_to_all(rows, axis, 0, 0, tiled=True, **kwargs).reshape(value.shape)

    recv = spread(send, "gx", axis_index_groups=groups)
    msg, state, opened = pl.pallas_call(
        group_kernel,
        out_shape=[
            shape((8, width + LANES)),
            shape((4, GROUP, width)),
            shape((4, GROUP, LANES)),
        ],
        compiler_params=SMALL,
        name="group_solve",
    )(recv)

    def joined(value, pairs):
        members = [[GROUP * t + i for t in pair] for pair in pairs for i in range(GROUP)]
        return lax.all_gather(value, "gx", axis_index_groups=members)

    near = joined(msg, ((0, 1), (2, 3)))
    every = joined(near, ((0, 3), (1, 2))).reshape(GROUPS, 8, width + LANES)
    send_back = pl.pallas_call(
        join_kernel,
        out_shape=shape((GROUP * back_rows, LANES)),
        compiler_params=SMALL,
        name="join_groups",
    )(every, state, opened)
    back = spread(send_back, "gx", axis_index_groups=groups)
    energy = pl.pallas_call(
        energy_kernel,
        out_shape=shape((yz_count, LANES)),
        compiler_params=SMALL,
        name="line_energy",
    )(back)
    energies = spread(energy, "yz")
    total_count = comps * cells * lines * lax.axis_size("gx") * yz_count
    derivative, mean_square = pl.pallas_call(
        functools.partial(final_kernel, 1.0 / total_count),
        in_specs=[pl.BlockSpec(memory_space=pltpu.VMEM)] * 5,
        out_specs=[pl.BlockSpec(memory_space=pltpu.HBM)] * 2,
        out_shape=[shape((comps, cells, lines)), shape((1, 1))],
        scratch_shapes=[
            pltpu.VMEM((comps, cells, lines), F32),
            pltpu.SMEM((1, 1), F32),
            pltpu.SemaphoreType.DMA((comps + 1,)),
        ],
        compiler_params=LARGE,
        name="final_update",
    )(back, energies, g, p_rows, q_rows)
    return derivative, mean_square[0, 0]


def solution(mesh):
    placed = (P(None, "gx", "yz"), P("gx", None, None))
    return jax.shard_map(
        on_device, mesh=mesh, in_specs=placed, out_specs=(P(None, "gx", "yz"), P()), check_vma=False
    )
```

```python
import functools

import jax
import jax.numpy as jnp
from jax import lax
from jax.experimental import pallas as pl
from jax.experimental.pallas import tpu as pltpu
from jax.sharding import PartitionSpec as P

COUPLING = 1.0 / 3.0
NEAR_WEIGHT = 7.0 / 9.0
FAR_WEIGHT = 1.0 / 36.0

GROUP = 16
GROUPS = 4
LANES = 128
CELLS = 64
CHUNK = 512
F32 = jnp.float32
BF16 = jnp.bfloat16
SMALL = pltpu.CompilerParams(vmem_limit_bytes=8 * 1024 * 1024)
LARGE = pltpu.CompilerParams(vmem_limit_bytes=16 * 1024 * 1024)


def lane_row(value, lanes=LANES):
    return jnp.broadcast_to(value, (1, lanes))


def tiled(value, copies):
    return jnp.concatenate([value] * copies, axis=1)


def parts_of(value):
    high = value.astype(BF16)
    rest = value - high.astype(F32)
    middle = rest.astype(BF16)
    return high, middle, (rest - middle.astype(F32)).astype(BF16)


def local_kernel(
    v_hbm, block_hbm, g_ref, send_ref, p_ref, q_ref, v_ref, mat_ref, pad_ref, block_ref, sems
):
    comps, _, lines = v_ref.shape
    inner = CELLS - 2
    stride = send_ref.shape[0] // GROUP
    block_copy = pltpu.make_async_copy(block_hbm, block_ref, sems.at[comps])
    block_copy.start()
    copies = [pltpu.make_async_copy(v_hbm.at[c], v_ref.at[c], sems.at[c]) for c in range(comps)]
    for copy in copies:
        copy.start()

    pad_ref[...] = jnp.zeros(pad_ref.shape, F32)
    block_copy.wait()
    pad_ref[0:inner, 0:inner] = block_ref[:, 0, :]
    padded = pltpu.roll(pltpu.roll(pad_ref[...], 1, 0), 1, 1)
    first = jnp.broadcast_to(COUPLING * padded[:, 1:2], (CELLS, LANES))
    last = jnp.broadcast_to(COUPLING * padded[:, inner : inner + 1], (CELLS, LANES))
    p_ref[...] = first
    q_ref[...] = last
    cols = lax.broadcasted_iota(jnp.int32, (1, LANES), 1)
    top = jnp.where(cols == 0, 1.0, 0.0) - COUPLING * padded[1:2]
    bottom = jnp.where(cols == CELLS - 1, 1.0, 0.0) - COUPLING * padded[inner : inner + 1]
    first_sum = jnp.sum(first * padded, axis=0, keepdims=True)
    last_sum = jnp.sum(last * padded, axis=0, keepdims=True)
    rows = lax.broadcasted_iota(jnp.int32, (16, LANES), 0)
    extra = jnp.where(rows == 0, top, 0.0)
    extra = jnp.where(rows == 1, bottom, extra)
    extra = jnp.where(rows == 2, first_sum, extra)
    extra = jnp.where(rows == 3, last_sum, extra)
    matrix = jnp.concatenate([padded, extra], 0)
    beside = pltpu.roll(matrix, 1, 1) + pltpu.roll(matrix, LANES - 1, 1)
    matrix = NEAR_WEIGHT * matrix + FAR_WEIGHT * beside
    high, middle, low = parts_of(matrix[:, 0:CELLS])
    mat_ref[...] = jnp.concatenate([high, middle, low, high, middle, high], 1)

    row8 = lax.broadcasted_iota(jnp.int32, (8, CHUNK), 0)
    energy = jnp.zeros((1, LANES), F32)
    for c in range(comps):
        copies[c].wait()
        for start in range(0, lines, CHUNK):
            v = v_ref[c, :, start : start + CHUNK]
            edge_0, edge_1 = v[0:1], v[CELLS - 1 : CELLS]
            below = jnp.concatenate([edge_0, v[: CELLS - 1]], 0)
            above = jnp.concatenate([v[1:], edge_1], 0)
            high, middle, low = parts_of(above - below)
            stacked = jnp.concatenate([high, high, high, middle, middle, low], 0)
            out = jnp.dot(mat_ref[...], stacked, preferred_element_type=F32)
            g = out[0:CELLS]
            g_ref[c, :, start : start + CHUNK] = g
            squares = jnp.sum(g * g, axis=0, keepdims=True)
            rows = out[CELLS : CELLS + 8]
            rows = jnp.where((row8 == 4) | (row8 == 5), pltpu.roll(v[0:8], 4, 0), rows)
            rows = jnp.where(row8 >= 6, v[CELLS - 8 : CELLS], rows)
            for j in range(CHUNK // LANES):
                at = slice(j * LANES, (j + 1) * LANES)
                energy = energy + squares[:, at]
                to = stride * (start // LANES + j) + 8 * c
                send_ref[to : to + 8, :] = rows[:, at]

    coefs = energy + pltpu.roll(energy, LANES // 2, 1)
    numbers = [
        first[1:2],
        last[1:2],
        first[inner : inner + 1],
        last[inner : inner + 1],
        jnp.sum(first * first, axis=0, keepdims=True),
        jnp.sum(first * last, axis=0, keepdims=True),
        jnp.sum(last * last, axis=0, keepdims=True),
    ]
    for i, number in enumerate(numbers):
        coefs = jnp.where(cols == i, number, coefs)
    for j in range(GROUP):
        to = stride * j + 8 * comps
        send_ref[to : to + 1, :] = coefs


def group_kernel(recv_ref, msg_ref, state_ref, open_ref):
    stride = recv_ref.shape[0] // GROUP
    comps = stride // 8
    width = comps * LANES

    def rows(r):
        parts = [recv_ref[pl.ds(8 * i + r, GROUP, stride=stride), :] for i in range(comps)]
        return jnp.concatenate(parts, 1)

    numbers = recv_ref[pl.ds(8 * comps, GROUP, stride=stride), :]

    def coef(r):
        return jnp.broadcast_to(numbers[:, r : r + 1], (GROUP, LANES))

    seg = lax.broadcasted_iota(jnp.int32, (GROUP, width), 0)
    seg_1 = lax.broadcasted_iota(jnp.int32, (GROUP, LANES), 0)

    def prev(x, s=1):
        return pltpu.roll(x, s, 0)

    def following(x, s=1):
        return pltpu.roll(x, GROUP - s, 0)

    b_first, b_last, pg, qg, v_0, v_1, v_62, v_63 = [rows(r) for r in range(8)]
    p_0, q_0, p_61, q_61, pp, pq, qq = [coef(r) for r in range(7)]
    upper = lax.broadcasted_iota(jnp.int32, (GROUP, LANES), 1) >= LANES // 2
    energy = jnp.where(upper, numbers, 0.0)
    jump_l = jnp.where(seg == 0, 0.0, prev(v_63) - v_0)
    jump_l2 = jnp.where(seg == 0, 0.0, prev(v_62) - v_0)
    jump_r = jnp.where(seg == GROUP - 1, 0.0, v_63 - following(v_0))
    jump_r2 = jnp.where(seg == GROUP - 1, 0.0, following(v_1) - v_63)
    b_first = b_first - (2.0 / 3.0) * jump_l - FAR_WEIGHT * jump_l2
    b_last = b_last - (2.0 / 3.0) * jump_r + FAR_WEIGHT * jump_r2

    unit_first = jnp.where(seg_1 == 0, 1.0, 0.0)
    unit_last = jnp.where(seg_1 == GROUP - 1, 1.0, 0.0)
    zero = jnp.zeros((GROUP, LANES), F32)
    third = jnp.full((GROUP, LANES), COUPLING, F32)
    rhs_f = jnp.concatenate([b_first, unit_first, zero], 1)
    rhs_l = jnp.concatenate([b_last, zero, unit_last], 1)
    f = (jnp.where(seg_1 == 0, 0.0, third), 1.0 - COUPLING * p_0, -COUPLING * q_0, rhs_f)
    l = (-COUPLING * p_61, 1.0 - COUPLING * q_61, jnp.where(seg_1 == GROUP - 1, 0.0, third), rhs_l)

    def reduce_level(mine, below, above):
        ratio_low = mine[0] / below[1]
        ratio_high = mine[2] / above[1]
        return (
            -ratio_low * below[0],
            mine[1] - ratio_low * below[2] - ratio_high * above[0],
            -ratio_high * above[2],
            mine[3] - tiled(ratio_low, comps + 2) * below[3] - tiled(ratio_high, comps + 2) * above[3],
        )

    f, l = (
        reduce_level(f, tuple(prev(x) for x in l), l),
        reduce_level(l, f, tuple(following(x) for x in f)),
    )
    step = 1
    while step < GROUP:
        f = reduce_level(f, tuple(prev(x, step) for x in f), tuple(following(x, step) for x in f))
        l = reduce_level(l, tuple(prev(x, step) for x in l), tuple(following(x, step) for x in l))
        step *= 2
    sol_f = f[3] / tiled(f[1], comps + 2)
    sol_l = l[3] / tiled(l[1], comps + 2)
    x_f, a_f, c_f = sol_f[:, :width], sol_f[:, width : width + LANES], sol_f[:, width + LANES :]
    x_l, a_l, c_l = sol_l[:, :width], sol_l[:, width : width + LANES], sol_l[:, width + LANES :]

    pp1, qq1 = pp + 1.0, qq + 1.0
    d_l, d_r = jump_l * (1.0 / 12.0), jump_r * (1.0 / 12.0)
    pq_w = tiled(pq, comps)
    m_f = tiled(pp1, comps) * x_f + pq_w * x_l - pg - d_l
    m_l = tiled(qq1, comps) * x_l + pq_w * x_f - qg - d_r

    def total(x):
        return jnp.sum(x, axis=0, keepdims=True)

    line_a = 2.0 * total(tiled(a_f, comps) * m_f + tiled(a_l, comps) * m_l)
    line_c = 2.0 * total(tiled(c_f, comps) * m_f + tiled(c_l, comps) * m_l)
    base = total(x_f * (m_f - pg - d_l) + x_l * (m_l - qg - d_r) + d_l * d_l + d_r * d_r)
    part = total(energy) * (1.0 / GROUP)
    for i in range(comps):
        part = part + base[:, i * LANES : (i + 1) * LANES]
    quad_aa = total(pp1 * a_f * a_f + 2.0 * pq * a_f * a_l + qq1 * a_l * a_l)
    quad_ac = total(pp1 * a_f * c_f + pq * (a_f * c_l + a_l * c_f) + qq1 * a_l * c_l)
    quad_cc = total(pp1 * c_f * c_f + 2.0 * pq * c_f * c_l + qq1 * c_l * c_l)

    end = GROUP - 1
    msg_ref[:, 0:width] = jnp.concatenate(
        [x_f[0:1], x_l[end:], line_a, line_c, v_0[0:1], v_1[0:1], v_62[end:], v_63[end:]], 0
    )
    msg_ref[:, width : width + LANES] = jnp.concatenate(
        [a_f[0:1], a_l[end:], c_f[0:1], c_l[end:], quad_aa, quad_ac, quad_cc, part], 0
    )
    state_ref[0] = x_f
    state_ref[1] = x_l
    state_ref[2] = jump_l
    state_ref[3] = jump_r
    open_ref[0] = a_f
    open_ref[1] = a_l
    open_ref[2] = c_f
    open_ref[3] = c_l


def eliminate(matrix, rhs, wide):
    size = len(rhs)
    matrix = [list(r) for r in matrix]
    rhs = list(rhs)
    inverse = [None] * size
    for k in range(size):
        inverse[k] = 1.0 / matrix[k][k]
        for i in range(k + 1, size):
            if matrix[i][k] is None:
                continue
            ratio = matrix[i][k] * inverse[k]
            for j in range(k + 1, size):
                if matrix[k][j] is not None:
                    old = matrix[i][j]
                    change = ratio * matrix[k][j]
                    matrix[i][j] = -change if old is None else old - change
            rhs[i] = rhs[i] - wide(ratio) * rhs[k]
    found = [None] * size
    for k in reversed(range(size)):
        value = rhs[k]
        for j in range(k + 1, size):
            if matrix[k][j] is not None:
                value = value - wide(matrix[k][j]) * found[j]
        found[k] = value * wide(inverse[k])
    return found


def join_kernel(all_ref, state_ref, open_ref, send_ref):
    width = state_ref.shape[2]
    comps = width // LANES
    group = lax.axis_index("gx") // GROUP

    def wide(x):
        return tiled(x, comps)

    tile = [all_ref[(0, 2, 3, 1)[t]] for t in range(GROUPS)]
    data = [[m[r : r + 1, 0:width] for r in range(8)] for m in tile]
    scal = [[m[r : r + 1, width:] for r in range(8)] for m in tile]
    x_f, x_l, line_a, line_c, v_0, v_1, v_62, v_63 = [[d[r] for d in data] for r in range(8)]
    a_f, a_l, c_f, c_l, q_aa, q_ac, q_cc, part = [[s[r] for s in scal] for r in range(8)]

    one = jnp.ones((1, LANES), F32)
    jump = [v_63[t - 1] - v_0[t] for t in range(GROUPS)]
    matrix, rhs = [], []
    for t in range(GROUPS):
        before, after = (t - 1) % GROUPS, (t + 1) % GROUPS
        row_a, row_c = [None] * (2 * GROUPS), [None] * (2 * GROUPS)
        row_a[2 * t] = one
        row_a[2 * before] = COUPLING * a_l[before]
        row_a[2 * before + 1] = COUPLING * c_l[before]
        row_c[2 * t + 1] = one
        row_c[2 * after] = COUPLING * a_f[after]
        row_c[2 * after + 1] = COUPLING * c_f[after]
        matrix += [row_a, row_c]
        rhs.append(
            -COUPLING * x_l[before] - (2.0 / 3.0) * jump[t] - FAR_WEIGHT * (v_62[before] - v_0[t])
        )
        rhs.append(
            -COUPLING * x_f[after] - (2.0 / 3.0) * jump[after] + FAR_WEIGHT * (v_1[after] - v_63[t])
        )
    found = eliminate(matrix, rhs, wide)
    value_a, value_c = found[0::2], found[1::2]

    energy = jnp.zeros((1, LANES), F32)
    for t in range(GROUPS):
        a, c = value_a[t], value_c[t]
        after = (t + 1) % GROUPS
        u_end = x_f[t] + wide(a_f[t]) * a + wide(c_f[t]) * c
        w_end = x_l[t] + wide(a_l[t]) * a + wide(c_l[t]) * c
        d_l, d_r = jump[t] * (1.0 / 12.0), jump[after] * (1.0 / 12.0)
        lines = a * (line_a[t] + wide(q_aa[t]) * a + wide(2.0 * q_ac[t]) * c)
        lines = lines + c * (line_c[t] + wide(q_cc[t]) * c)
        lines = lines + d_l * (d_l - 2.0 * u_end) + d_r * (d_r - 2.0 * w_end)
        energy = energy + part[t]
        for i in range(comps):
            energy = energy + lines[:, i * LANES : (i + 1) * LANES]

    def mine(values):
        result = values[0]
        for t in range(1, GROUPS):
            result = jnp.where(group == t, values[t], result)
        return result

    a, c = mine(value_a), mine(value_c)
    left, right = mine(jump), mine(jump[1:] + jump[:1])
    seg = lax.broadcasted_iota(jnp.int32, (GROUP, width), 0)
    u_t = state_ref[0] + wide(open_ref[0]) * a + wide(open_ref[2]) * c
    w_t = state_ref[1] + wide(open_ref[1]) * a + wide(open_ref[3]) * c
    jump_l = jnp.where(seg == 0, left, state_ref[2])
    jump_r = jnp.where(seg == GROUP - 1, right, state_ref[3])
    u = u_t - jump_l * (1.0 / 12.0)
    w = w_t - jump_r * (1.0 / 12.0)
    stride = send_ref.shape[0] // GROUP
    for i in range(comps):
        for r, value in enumerate((u_t, w_t, u, w)):
            part_i = value[:, i * LANES : (i + 1) * LANES]
            send_ref[pl.ds(4 * i + r, GROUP, stride=stride), :] = part_i
    send_ref[pl.ds(4 * comps, GROUP, stride=stride), :] = jnp.broadcast_to(energy, (GROUP, LANES))


def update_cells(recv_ref, g_ref, p_ref, q_ref, out_hbm, out_ref, sems):
    comps, _, lines = g_ref.shape
    stride = recv_ref.shape[0] // GROUP
    row8 = lax.broadcasted_iota(jnp.int32, (8, LANES), 0)
    first, last = p_ref[...], q_ref[...]
    copies = []
    for c in range(comps):
        for j in range(GROUP):
            at = slice(j * LANES, (j + 1) * LANES)
            base = stride * j + 4 * c
            u_t, w_t, u, w = [recv_ref[base + r : base + r + 1, :] for r in range(4)]
            value = g_ref[c, :, at] - first * u_t - last * w_t
            out_ref[c, 0:8, at] = jnp.where(row8 == 0, u, value[0:8])
            out_ref[c, 8 : CELLS - 8, at] = value[8 : CELLS - 8]
            out_ref[c, CELLS - 8 :, at] = jnp.where(row8 == 7, w, value[CELLS - 8 :])
        copy = pltpu.make_async_copy(out_ref.at[c], out_hbm.at[c], sems.at[c])
        copy.start()
        copies.append(copy)
    for copy in copies:
        copy.wait()


def early_device():
    place = lax.axis_index("yz")
    return (place % 2 == 1) | (place == 0)


def early_kernel(recv_ref, g_ref, p_ref, q_ref, out_hbm, energy_ref, out_ref, sems):
    stride = recv_ref.shape[0] // GROUP
    energy = recv_ref[pl.ds(stride - 1, GROUP, stride=stride), :]
    energy_ref[...] = jnp.broadcast_to(jnp.sum(energy, axis=0, keepdims=True), energy_ref.shape)

    @pl.when(early_device())
    def _():
        update_cells(recv_ref, g_ref, p_ref, q_ref, out_hbm, out_ref, sems)


def late_kernel(
    scale, begun_hbm, energy_ref, recv_ref, g_ref, p_ref, q_ref, out_hbm, mean_hbm, mean_ref, out_ref, sems
):
    comps = g_ref.shape[0]
    mean_ref[0, 0] = jnp.sum(energy_ref[...]) * scale
    mean_copy = pltpu.make_async_copy(mean_ref, mean_hbm, sems.at[comps])
    mean_copy.start()

    @pl.when(jnp.logical_not(early_device()))
    def _():
        update_cells(recv_ref, g_ref, p_ref, q_ref, out_hbm, out_ref, sems)

    mean_copy.wait()


def on_device(velocity, blocks):
    comps, cells, lines = velocity.shape
    width = comps * LANES
    send_rows, back_rows = 8 * comps + 1, 4 * comps + 1
    yz_count = lax.axis_size("yz")
    groups = [[GROUP * t + i for i in range(GROUP)] for t in range(GROUPS)]
    shape = functools.partial(jax.ShapeDtypeStruct, dtype=F32)

    g, send, p_rows, q_rows = pl.pallas_call(
        local_kernel,
        in_specs=[
            pl.BlockSpec(memory_space=pltpu.HBM),
            pl.BlockSpec(memory_space=pltpu.HBM),
        ],
        out_specs=[pl.BlockSpec(memory_space=pltpu.VMEM)] * 4,
        out_shape=[
            shape((comps, cells, lines)),
            shape((GROUP * send_rows, LANES)),
            shape((cells, LANES)),
            shape((cells, LANES)),
        ],
        scratch_shapes=[
            pltpu.VMEM((comps, cells, lines), F32),
            pltpu.VMEM((cells + 16, 6 * cells), BF16),
            pltpu.VMEM((cells, LANES), F32),
            pltpu.VMEM((cells - 2, 1, cells - 2), F32),
            pltpu.SemaphoreType.DMA((comps + 1,)),
        ],
        compiler_params=LARGE,
        name="local_solve",
    )(
        pltpu.with_memory_space_constraint(velocity, pltpu.HBM),
        pltpu.with_memory_space_constraint(jnp.transpose(blocks, (1, 0, 2)), pltpu.HBM),
    )

    def spread(value, axis, **kwargs):
        rows = value.reshape(value.shape[0], 1, LANES)
        return lax.all_to_all(rows, axis, 0, 0, tiled=True, **kwargs).reshape(value.shape)

    recv = spread(send, "gx", axis_index_groups=groups)
    msg, state, opened = pl.pallas_call(
        group_kernel,
        out_shape=[
            shape((8, width + LANES)),
            shape((4, GROUP, width)),
            shape((4, GROUP, LANES)),
        ],
        compiler_params=SMALL,
        name="group_solve",
    )(recv)

    def joined(value, pairs):
        members = [[GROUP * t + i for t in pair] for pair in pairs for i in range(GROUP)]
        return lax.all_gather(value, "gx", axis_index_groups=members)

    near = joined(msg, ((0, 3), (1, 2)))
    every = joined(near, ((0, 1), (3, 2))).reshape(GROUPS, 8, width + LANES)
    send_back = pl.pallas_call(
        join_kernel,
        out_shape=shape((GROUP * back_rows, LANES)),
        compiler_params=SMALL,
        name="join_groups",
    )(every, state, opened)
    back = spread(send_back, "gx", axis_index_groups=groups)
    begun, energy = pl.pallas_call(
        early_kernel,
        in_specs=[pl.BlockSpec(memory_space=pltpu.VMEM)] * 4,
        out_specs=[
            pl.BlockSpec(memory_space=pltpu.HBM),
            pl.BlockSpec(memory_space=pltpu.VMEM),
        ],
        out_shape=[shape((comps, cells, lines)), shape((yz_count, LANES))],
        scratch_shapes=[
            pltpu.VMEM((comps, cells, lines), F32),
            pltpu.SemaphoreType.DMA((comps,)),
        ],
        compiler_params=LARGE,
        name="early_update",
    )(back, g, p_rows, q_rows)
    energies = spread(energy, "yz")
    total_count = comps * cells * lines * lax.axis_size("gx") * yz_count
    derivative, mean_square = pl.pallas_call(
        functools.partial(late_kernel, 1.0 / total_count),
        in_specs=[pl.BlockSpec(memory_space=pltpu.HBM)]
        + [pl.BlockSpec(memory_space=pltpu.VMEM)] * 5,
        out_specs=[pl.BlockSpec(memory_space=pltpu.HBM)] * 2,
        out_shape=[shape((comps, cells, lines)), shape((1, 1))],
        input_output_aliases={0: 0},
        scratch_shapes=[
            pltpu.SMEM((1, 1), F32),
            pltpu.VMEM((comps, cells, lines), F32),
            pltpu.SemaphoreType.DMA((comps + 1,)),
        ],
        compiler_params=LARGE,
        name="late_update",
    )(begun, energies, back, g, p_rows, q_rows)
    return derivative, mean_square[0, 0]


def solution(mesh):
    placed = (P(None, "gx", "yz"), P("gx", None, None))
    return jax.shard_map(
        on_device, mesh=mesh, in_specs=placed, out_specs=(P(None, "gx", "yz"), P()), check_vma=False
    )
```

```python
import functools

import jax
import jax.numpy as jnp
from jax import lax
from jax.experimental import pallas as pl
from jax.experimental.pallas import tpu as pltpu
from jax.sharding import PartitionSpec as P

COUPLING = 1.0 / 3.0
NEAR_WEIGHT = 7.0 / 9.0
FAR_WEIGHT = 1.0 / 36.0

GROUP = 16
GROUPS = 4
ORDER = tuple(4 * z + y for y in (2, 3, 1, 0) for z in (2, 1, 3, 0))
YZ_ORDER = (5, 4, 7, 6, 3, 2, 1, 0)
LANES = 128
CELLS = 64
CHUNK = 512
F32 = jnp.float32
BF16 = jnp.bfloat16
SMALL = pltpu.CompilerParams(vmem_limit_bytes=8 * 1024 * 1024)
LARGE = pltpu.CompilerParams(vmem_limit_bytes=16 * 1024 * 1024)


def lane_row(value, lanes=LANES):
    return jnp.broadcast_to(value, (1, lanes))


def tiled(value, copies):
    return jnp.concatenate([value] * copies, axis=1)


def parts_of(value):
    high = value.astype(BF16)
    rest = value - high.astype(F32)
    middle = rest.astype(BF16)
    return high, middle, (rest - middle.astype(F32)).astype(BF16)


def local_kernel(
    v_hbm, block_hbm, g_ref, send_ref, p_ref, q_ref, v_ref, mat_ref, pad_ref, block_ref, sems
):
    comps, _, lines = v_ref.shape
    inner = CELLS - 2
    stride = send_ref.shape[0] // GROUP
    block_copy = pltpu.make_async_copy(block_hbm, block_ref, sems.at[comps])
    block_copy.start()
    copies = [pltpu.make_async_copy(v_hbm.at[c], v_ref.at[c], sems.at[c]) for c in range(comps)]
    for copy in copies:
        copy.start()

    pad_ref[...] = jnp.zeros(pad_ref.shape, F32)
    block_copy.wait()
    pad_ref[0:inner, 0:inner] = block_ref[:, 0, :]
    padded = pltpu.roll(pltpu.roll(pad_ref[...], 1, 0), 1, 1)
    first = jnp.broadcast_to(COUPLING * padded[:, 1:2], (CELLS, LANES))
    last = jnp.broadcast_to(COUPLING * padded[:, inner : inner + 1], (CELLS, LANES))
    p_ref[...] = first
    q_ref[...] = last
    cols = lax.broadcasted_iota(jnp.int32, (1, LANES), 1)
    top = jnp.where(cols == 0, 1.0, 0.0) - COUPLING * padded[1:2]
    bottom = jnp.where(cols == CELLS - 1, 1.0, 0.0) - COUPLING * padded[inner : inner + 1]
    first_sum = jnp.sum(first * padded, axis=0, keepdims=True)
    last_sum = jnp.sum(last * padded, axis=0, keepdims=True)
    rows = lax.broadcasted_iota(jnp.int32, (16, LANES), 0)
    extra = jnp.where(rows == 0, top, 0.0)
    extra = jnp.where(rows == 1, bottom, extra)
    extra = jnp.where(rows == 2, first_sum, extra)
    extra = jnp.where(rows == 3, last_sum, extra)
    matrix = jnp.concatenate([padded, extra], 0)
    beside = pltpu.roll(matrix, 1, 1) + pltpu.roll(matrix, LANES - 1, 1)
    matrix = NEAR_WEIGHT * matrix + FAR_WEIGHT * beside
    high, middle, low = parts_of(matrix[:, 0:CELLS])
    mat_ref[...] = jnp.concatenate([high, middle, low, high, middle, high], 1)

    row8 = lax.broadcasted_iota(jnp.int32, (8, CHUNK), 0)
    energy = jnp.zeros((1, LANES), F32)
    for c in range(comps):
        copies[c].wait()
        for start in range(0, lines, CHUNK):
            v = v_ref[c, :, start : start + CHUNK]
            edge_0, edge_1 = v[0:1], v[CELLS - 1 : CELLS]
            below = jnp.concatenate([edge_0, v[: CELLS - 1]], 0)
            above = jnp.concatenate([v[1:], edge_1], 0)
            high, middle, low = parts_of(above - below)
            stacked = jnp.concatenate([high, high, high, middle, middle, low], 0)
            out = jnp.dot(mat_ref[...], stacked, preferred_element_type=F32)
            g = out[0:CELLS]
            g_ref[c, :, start : start + CHUNK] = g
            squares = jnp.sum(g * g, axis=0, keepdims=True)
            rows = out[CELLS : CELLS + 8]
            rows = jnp.where((row8 == 4) | (row8 == 5), pltpu.roll(v[0:8], 4, 0), rows)
            rows = jnp.where(row8 >= 6, v[CELLS - 8 : CELLS], rows)
            for j in range(CHUNK // LANES):
                at = slice(j * LANES, (j + 1) * LANES)
                energy = energy + squares[:, at]
                to = stride * (start // LANES + j) + 8 * c
                send_ref[to : to + 8, :] = rows[:, at]

    coefs = energy + pltpu.roll(energy, LANES // 2, 1)
    numbers = [
        first[1:2],
        last[1:2],
        first[inner : inner + 1],
        last[inner : inner + 1],
        jnp.sum(first * first, axis=0, keepdims=True),
        jnp.sum(first * last, axis=0, keepdims=True),
        jnp.sum(last * last, axis=0, keepdims=True),
    ]
    for i, number in enumerate(numbers):
        coefs = jnp.where(cols == i, number, coefs)
    for j in range(GROUP):
        to = stride * j + 8 * comps
        send_ref[to : to + 1, :] = coefs


def group_kernel(recv_ref, msg_ref, state_ref, open_ref, block_ref):
    count = recv_ref.shape[0] // GROUP
    stride = block_ref.shape[0] // GROUP
    comps = count // 8
    for i, place in enumerate(ORDER):
        to = stride * place
        block_ref[to : to + count, :] = recv_ref[count * i : count * (i + 1), :]
    width = comps * LANES

    def rows(r):
        parts = [block_ref[pl.ds(8 * i + r, GROUP, stride=stride), :] for i in range(comps)]
        return jnp.concatenate(parts, 1)

    numbers = block_ref[pl.ds(8 * comps, GROUP, stride=stride), :]

    def coef(r):
        return jnp.broadcast_to(numbers[:, r : r + 1], (GROUP, LANES))

    seg = lax.broadcasted_iota(jnp.int32, (GROUP, width), 0)
    seg_1 = lax.broadcasted_iota(jnp.int32, (GROUP, LANES), 0)

    def prev(x, s=1):
        return pltpu.roll(x, s, 0)

    def following(x, s=1):
        return pltpu.roll(x, GROUP - s, 0)

    b_first, b_last, pg, qg, v_0, v_1, v_62, v_63 = [rows(r) for r in range(8)]
    p_0, q_0, p_61, q_61, pp, pq, qq = [coef(r) for r in range(7)]
    upper = lax.broadcasted_iota(jnp.int32, (GROUP, LANES), 1) >= LANES // 2
    energy = jnp.where(upper, numbers, 0.0)
    jump_l = jnp.where(seg == 0, 0.0, prev(v_63) - v_0)
    jump_l2 = jnp.where(seg == 0, 0.0, prev(v_62) - v_0)
    jump_r = jnp.where(seg == GROUP - 1, 0.0, v_63 - following(v_0))
    jump_r2 = jnp.where(seg == GROUP - 1, 0.0, following(v_1) - v_63)
    b_first = b_first - (2.0 / 3.0) * jump_l - FAR_WEIGHT * jump_l2
    b_last = b_last - (2.0 / 3.0) * jump_r + FAR_WEIGHT * jump_r2

    unit_first = jnp.where(seg_1 == 0, 1.0, 0.0)
    unit_last = jnp.where(seg_1 == GROUP - 1, 1.0, 0.0)
    zero = jnp.zeros((GROUP, LANES), F32)
    third = jnp.full((GROUP, LANES), COUPLING, F32)
    rhs_f = jnp.concatenate([b_first, unit_first, zero], 1)
    rhs_l = jnp.concatenate([b_last, zero, unit_last], 1)
    f = (jnp.where(seg_1 == 0, 0.0, third), 1.0 - COUPLING * p_0, -COUPLING * q_0, rhs_f)
    l = (-COUPLING * p_61, 1.0 - COUPLING * q_61, jnp.where(seg_1 == GROUP - 1, 0.0, third), rhs_l)

    def reduce_level(mine, below, above):
        ratio_low = mine[0] / below[1]
        ratio_high = mine[2] / above[1]
        return (
            -ratio_low * below[0],
            mine[1] - ratio_low * below[2] - ratio_high * above[0],
            -ratio_high * above[2],
            mine[3] - tiled(ratio_low, comps + 2) * below[3] - tiled(ratio_high, comps + 2) * above[3],
        )

    f, l = (
        reduce_level(f, tuple(prev(x) for x in l), l),
        reduce_level(l, f, tuple(following(x) for x in f)),
    )
    step = 1
    while step < GROUP:
        f = reduce_level(f, tuple(prev(x, step) for x in f), tuple(following(x, step) for x in f))
        l = reduce_level(l, tuple(prev(x, step) for x in l), tuple(following(x, step) for x in l))
        step *= 2
    sol_f = f[3] / tiled(f[1], comps + 2)
    sol_l = l[3] / tiled(l[1], comps + 2)
    x_f, a_f, c_f = sol_f[:, :width], sol_f[:, width : width + LANES], sol_f[:, width + LANES :]
    x_l, a_l, c_l = sol_l[:, :width], sol_l[:, width : width + LANES], sol_l[:, width + LANES :]

    pp1, qq1 = pp + 1.0, qq + 1.0
    d_l, d_r = jump_l * (1.0 / 12.0), jump_r * (1.0 / 12.0)
    pq_w = tiled(pq, comps)
    m_f = tiled(pp1, comps) * x_f + pq_w * x_l - pg - d_l
    m_l = tiled(qq1, comps) * x_l + pq_w * x_f - qg - d_r

    def total(x):
        return jnp.sum(x, axis=0, keepdims=True)

    line_a = 2.0 * total(tiled(a_f, comps) * m_f + tiled(a_l, comps) * m_l)
    line_c = 2.0 * total(tiled(c_f, comps) * m_f + tiled(c_l, comps) * m_l)
    base = total(x_f * (m_f - pg - d_l) + x_l * (m_l - qg - d_r) + d_l * d_l + d_r * d_r)
    part = total(energy) * (1.0 / GROUP)
    for i in range(comps):
        part = part + base[:, i * LANES : (i + 1) * LANES]
    quad_aa = total(pp1 * a_f * a_f + 2.0 * pq * a_f * a_l + qq1 * a_l * a_l)
    quad_ac = total(pp1 * a_f * c_f + pq * (a_f * c_l + a_l * c_f) + qq1 * a_l * c_l)
    quad_cc = total(pp1 * c_f * c_f + 2.0 * pq * c_f * c_l + qq1 * c_l * c_l)

    end = GROUP - 1
    msg_ref[:, 0:width] = jnp.concatenate(
        [x_f[0:1], x_l[end:], line_a, line_c, v_0[0:1], v_1[0:1], v_62[end:], v_63[end:]], 0
    )
    msg_ref[:, width : width + LANES] = jnp.concatenate(
        [a_f[0:1], a_l[end:], c_f[0:1], c_l[end:], quad_aa, quad_ac, quad_cc, part], 0
    )
    state_ref[0] = x_f
    state_ref[1] = x_l
    state_ref[2] = jump_l
    state_ref[3] = jump_r
    open_ref[0] = a_f
    open_ref[1] = a_l
    open_ref[2] = c_f
    open_ref[3] = c_l


def eliminate(matrix, rhs, wide):
    size = len(rhs)
    matrix = [list(r) for r in matrix]
    rhs = list(rhs)
    inverse = [None] * size
    for k in range(size):
        inverse[k] = 1.0 / matrix[k][k]
        for i in range(k + 1, size):
            if matrix[i][k] is None:
                continue
            ratio = matrix[i][k] * inverse[k]
            for j in range(k + 1, size):
                if matrix[k][j] is not None:
                    old = matrix[i][j]
                    change = ratio * matrix[k][j]
                    matrix[i][j] = -change if old is None else old - change
            rhs[i] = rhs[i] - wide(ratio) * rhs[k]
    found = [None] * size
    for k in reversed(range(size)):
        value = rhs[k]
        for j in range(k + 1, size):
            if matrix[k][j] is not None:
                value = value - wide(matrix[k][j]) * found[j]
        found[k] = value * wide(inverse[k])
    return found


def unpacked(message, width):
    return (
        [message[r : r + 1, 0:width] for r in range(8)],
        [message[r : r + 1, width:] for r in range(8)],
    )


def pair_kernel(both_ref, msg_ref, state_ref, open_ref):
    width = both_ref.shape[2] - LANES
    comps = width // LANES

    def wide(x):
        return tiled(x, comps)

    left, l = unpacked(both_ref[0], width)
    right, r = unpacked(both_ref[1], width)
    x_f, x_l, line_a, line_c, v_0, v_1, v_62, v_63 = [list(p) for p in zip(left, right)]
    a_f, a_l, c_f, c_l, q_aa, q_ac, q_cc, part = [list(p) for p in zip(l, r)]

    jump = v_63[0] - v_0[1]
    rhs_c = -COUPLING * x_f[1] - (2.0 / 3.0) * jump + FAR_WEIGHT * (v_1[1] - v_63[0])
    rhs_a = -COUPLING * x_l[0] - (2.0 / 3.0) * jump - FAR_WEIGHT * (v_62[0] - v_0[1])
    inverse = 1.0 / (1.0 - (COUPLING * a_f[1]) * (COUPLING * c_l[0]))
    to_c, to_a = COUPLING * a_f[1] * inverse, COUPLING * c_l[0] * inverse
    c_0 = wide(inverse) * rhs_c - wide(to_c) * rhs_a
    c_alpha = to_c * (COUPLING * a_l[0])
    c_gamma = -inverse * (COUPLING * c_f[1])
    a_0 = wide(inverse) * rhs_a - wide(to_a) * rhs_c
    a_alpha = -inverse * (COUPLING * a_l[0])
    a_gamma = to_a * (COUPLING * c_f[1])

    d = jump * (1.0 / 12.0)
    inner_u = x_f[1] + wide(a_f[1]) * a_0
    inner_w = x_l[0] + wide(c_l[0]) * c_0
    both_alpha = a_f[1] * a_alpha + a_l[0] + c_l[0] * c_alpha
    both_gamma = a_f[1] * a_gamma + c_f[1] + c_l[0] * c_gamma
    slope_c = line_c[0] + wide(2.0 * q_cc[0]) * c_0
    slope_a = line_a[1] + wide(2.0 * q_aa[1]) * a_0
    line_alpha = line_a[0] + wide(2.0 * q_ac[0]) * c_0 + wide(c_alpha) * slope_c
    line_alpha = line_alpha + wide(a_alpha) * slope_a - wide(2.0 * both_alpha) * d
    line_gamma = line_c[1] + wide(2.0 * q_ac[1]) * a_0 + wide(a_gamma) * slope_a
    line_gamma = line_gamma + wide(c_gamma) * slope_c - wide(2.0 * both_gamma) * d
    base = c_0 * (line_c[0] + wide(q_cc[0]) * c_0) + a_0 * (line_a[1] + wide(q_aa[1]) * a_0)
    base = base + 2.0 * d * (d - inner_u - inner_w)
    total = part[0] + part[1]
    for i in range(comps):
        total = total + base[:, i * LANES : (i + 1) * LANES]
    q_alpha = q_aa[0] + c_alpha * (2.0 * q_ac[0] + q_cc[0] * c_alpha) + q_aa[1] * a_alpha * a_alpha
    q_gamma = q_cc[1] + a_gamma * (2.0 * q_ac[1] + q_aa[1] * a_gamma) + q_cc[0] * c_gamma * c_gamma
    q_mixed = c_gamma * (q_ac[0] + q_cc[0] * c_alpha) + a_alpha * (q_ac[1] + q_aa[1] * a_gamma)

    msg_ref[:, 0:width] = jnp.concatenate(
        [
            x_f[0] + wide(c_f[0]) * c_0,
            x_l[1] + wide(a_l[1]) * a_0,
            line_alpha,
            line_gamma,
            v_0[0],
            v_1[0],
            v_62[1],
            v_63[1],
        ],
        0,
    )
    msg_ref[:, width:] = jnp.concatenate(
        [
            a_f[0] + c_f[0] * c_alpha,
            a_l[1] * a_alpha,
            c_f[0] * c_gamma,
            c_l[1] + a_l[1] * a_gamma,
            q_alpha,
            q_mixed,
            q_gamma,
            total,
        ],
        0,
    )
    none = jnp.zeros_like(jump)
    state_ref[...] = jnp.concatenate([c_0, a_0, jump] + [none] * 5, 0)
    none = jnp.zeros_like(inverse)
    open_ref[...] = jnp.concatenate([c_alpha, c_gamma, a_alpha, a_gamma] + [none] * 4, 0)


def join_kernel(all_ref, pair_ref, pair_open_ref, state_ref, open_ref, send_ref, block_ref):
    width = state_ref.shape[2]
    comps = width // LANES
    group = lax.axis_index("gx") // GROUP
    pairs = all_ref.shape[0]

    def wide(x):
        return tiled(x, comps)

    data, scal = zip(*[unpacked(all_ref[t], width) for t in range(pairs)])
    x_f, x_l, line_a, line_c, v_0, v_1, v_62, v_63 = [[d[r] for d in data] for r in range(8)]
    a_f, a_l, c_f, c_l, q_aa, q_ac, q_cc, part = [[s[r] for s in scal] for r in range(8)]

    one = jnp.ones((1, LANES), F32)
    jump = [v_63[t - 1] - v_0[t] for t in range(pairs)]
    matrix, rhs = [], []
    for t in range(pairs):
        before, after = (t - 1) % pairs, (t + 1) % pairs
        row_a, row_c = [None] * (2 * pairs), [None] * (2 * pairs)
        row_a[2 * t] = one
        row_a[2 * before] = COUPLING * a_l[before]
        row_a[2 * before + 1] = COUPLING * c_l[before]
        row_c[2 * t + 1] = one
        row_c[2 * after] = COUPLING * a_f[after]
        row_c[2 * after + 1] = COUPLING * c_f[after]
        matrix += [row_a, row_c]
        rhs.append(
            -COUPLING * x_l[before] - (2.0 / 3.0) * jump[t] - FAR_WEIGHT * (v_62[before] - v_0[t])
        )
        rhs.append(
            -COUPLING * x_f[after] - (2.0 / 3.0) * jump[after] + FAR_WEIGHT * (v_1[after] - v_63[t])
        )
    found = eliminate(matrix, rhs, wide)
    value_a, value_c = found[0::2], found[1::2]

    energy = jnp.zeros((1, LANES), F32)
    for t in range(pairs):
        a, c = value_a[t], value_c[t]
        after = (t + 1) % pairs
        u_end = x_f[t] + wide(a_f[t]) * a + wide(c_f[t]) * c
        w_end = x_l[t] + wide(a_l[t]) * a + wide(c_l[t]) * c
        d_l, d_r = jump[t] * (1.0 / 12.0), jump[after] * (1.0 / 12.0)
        lines = a * (line_a[t] + wide(q_aa[t]) * a + wide(2.0 * q_ac[t]) * c)
        lines = lines + c * (line_c[t] + wide(q_cc[t]) * c)
        lines = lines + d_l * (d_l - 2.0 * u_end) + d_r * (d_r - 2.0 * w_end)
        energy = energy + part[t]
        for i in range(comps):
            energy = energy + lines[:, i * LANES : (i + 1) * LANES]

    first_pair = (group == 0) | (group == 3)
    on_left = (group == 3) | (group == 1)

    def mine(values):
        return jnp.where(first_pair, values[0], values[1])

    alpha, gamma = mine(value_a), mine(value_c)
    inner = [pair_ref[r : r + 1, :] for r in range(3)]
    slope = [wide(pair_open_ref[r : r + 1, :]) for r in range(4)]
    inner_c = inner[0] + slope[0] * alpha + slope[1] * gamma
    inner_a = inner[1] + slope[2] * alpha + slope[3] * gamma
    a, c = jnp.where(on_left, alpha, inner_a), jnp.where(on_left, inner_c, gamma)
    left = jnp.where(on_left, mine(jump), inner[2])
    right = jnp.where(on_left, inner[2], mine(jump[1:] + jump[:1]))
    seg = lax.broadcasted_iota(jnp.int32, (GROUP, width), 0)
    u_t = state_ref[0] + wide(open_ref[0]) * a + wide(open_ref[2]) * c
    w_t = state_ref[1] + wide(open_ref[1]) * a + wide(open_ref[3]) * c
    jump_l = jnp.where(seg == 0, left, state_ref[2])
    jump_r = jnp.where(seg == GROUP - 1, right, state_ref[3])
    u = u_t - jump_l * (1.0 / 12.0)
    w = w_t - jump_r * (1.0 / 12.0)
    count = send_ref.shape[0] // GROUP
    stride = block_ref.shape[0] // GROUP
    for i in range(comps):
        for r, value in enumerate((u_t, w_t, u, w)):
            part_i = value[:, i * LANES : (i + 1) * LANES]
            block_ref[pl.ds(4 * i + r, GROUP, stride=stride), :] = part_i
    block_ref[pl.ds(4 * comps, GROUP, stride=stride), :] = jnp.broadcast_to(energy, (GROUP, LANES))
    for i, place in enumerate(ORDER):
        send_ref[count * i : count * (i + 1), :] = block_ref[stride * place : stride * place + count, :]


def update_cells(recv_ref, g_ref, p_ref, q_ref, out_hbm, out_ref, sems):
    comps, _, lines = g_ref.shape
    stride = recv_ref.shape[0] // GROUP
    row8 = lax.broadcasted_iota(jnp.int32, (8, LANES), 0)
    first, last = p_ref[...], q_ref[...]
    copies = []
    for c in range(comps):
        for j in range(GROUP):
            at = slice(j * LANES, (j + 1) * LANES)
            base = stride * j + 4 * c
            u_t, w_t, u, w = [recv_ref[base + r : base + r + 1, :] for r in range(4)]
            value = g_ref[c, :, at] - first * u_t - last * w_t
            out_ref[c, 0:8, at] = jnp.where(row8 == 0, u, value[0:8])
            out_ref[c, 8 : CELLS - 8, at] = value[8 : CELLS - 8]
            out_ref[c, CELLS - 8 :, at] = jnp.where(row8 == 7, w, value[CELLS - 8 :])
        copy = pltpu.make_async_copy(out_ref.at[c], out_hbm.at[c], sems.at[c])
        copy.start()
        copies.append(copy)
    for copy in copies:
        copy.wait()


def early_device():
    place = lax.axis_index("yz")
    return (place % 2 == 1) | (place == 0)


def early_kernel(recv_ref, g_ref, p_ref, q_ref, out_hbm, energy_ref, out_ref, sems):
    stride = recv_ref.shape[0] // GROUP
    energy = recv_ref[pl.ds(stride - 1, GROUP, stride=stride), :]
    energy_ref[...] = jnp.broadcast_to(jnp.sum(energy, axis=0, keepdims=True), energy_ref.shape)

    @pl.when(early_device())
    def _():
        update_cells(recv_ref, g_ref, p_ref, q_ref, out_hbm, out_ref, sems)


def late_kernel(
    scale, begun_hbm, energy_ref, recv_ref, g_ref, p_ref, q_ref, out_hbm, mean_hbm, mean_ref, out_ref, sems
):
    comps = g_ref.shape[0]
    mean_ref[0, 0] = jnp.sum(energy_ref[...]) * scale
    mean_copy = pltpu.make_async_copy(mean_ref, mean_hbm, sems.at[comps])
    mean_copy.start()

    @pl.when(jnp.logical_not(early_device()))
    def _():
        update_cells(recv_ref, g_ref, p_ref, q_ref, out_hbm, out_ref, sems)

    mean_copy.wait()


def on_device(velocity, blocks):
    comps, cells, lines = velocity.shape
    width = comps * LANES
    send_rows, back_rows = 8 * comps + 1, 4 * comps + 1
    yz_count = lax.axis_size("yz")
    groups = [[GROUP * t + i for i in ORDER] for t in range(GROUPS)]
    shape = functools.partial(jax.ShapeDtypeStruct, dtype=F32)

    g, send, p_rows, q_rows = pl.pallas_call(
        local_kernel,
        in_specs=[
            pl.BlockSpec(memory_space=pltpu.HBM),
            pl.BlockSpec(memory_space=pltpu.HBM),
        ],
        out_specs=[pl.BlockSpec(memory_space=pltpu.VMEM)] * 4,
        out_shape=[
            shape((comps, cells, lines)),
            shape((GROUP * send_rows, LANES)),
            shape((cells, LANES)),
            shape((cells, LANES)),
        ],
        scratch_shapes=[
            pltpu.VMEM((comps, cells, lines), F32),
            pltpu.VMEM((cells + 16, 6 * cells), BF16),
            pltpu.VMEM((cells, LANES), F32),
            pltpu.VMEM((cells - 2, 1, cells - 2), F32),
            pltpu.SemaphoreType.DMA((comps + 1,)),
        ],
        compiler_params=LARGE,
        name="local_solve",
    )(
        pltpu.with_memory_space_constraint(velocity, pltpu.HBM),
        pltpu.with_memory_space_constraint(jnp.transpose(blocks, (1, 0, 2)), pltpu.HBM),
    )

    def spread(value, axis, **kwargs):
        rows = value.reshape(value.shape[0], 1, LANES)
        return lax.all_to_all(rows, axis, 0, 0, tiled=True, **kwargs).reshape(value.shape)

    recv = spread(send, "gx", axis_index_groups=groups)
    msg, state, opened = pl.pallas_call(
        group_kernel,
        out_shape=[
            shape((8, width + LANES)),
            shape((4, GROUP, width)),
            shape((4, GROUP, LANES)),
        ],
        scratch_shapes=[pltpu.VMEM((GROUP * 8 * (comps + 1), LANES), F32)],
        compiler_params=SMALL,
        name="group_solve",
    )(recv)

    def joined(value, pairs):
        members = [[GROUP * t + i for t in pair] for pair in pairs for i in range(GROUP)]
        return lax.all_gather(value, "gx", axis_index_groups=members)

    near = joined(msg, ((3, 0), (1, 2)))
    pair_msg, pair_state, pair_open = pl.pallas_call(
        pair_kernel,
        out_shape=[shape((8, width + LANES)), shape((8, width)), shape((8, LANES))],
        compiler_params=SMALL,
        name="pair_groups",
    )(near)
    every = joined(pair_msg, ((0, 1), (3, 2)))
    send_back = pl.pallas_call(
        join_kernel,
        out_shape=shape((GROUP * back_rows, LANES)),
        scratch_shapes=[pltpu.VMEM((GROUP * -(-back_rows // 8) * 8, LANES), F32)],
        compiler_params=SMALL,
        name="join_groups",
    )(every, pair_state, pair_open, state, opened)
    back = spread(send_back, "gx", axis_index_groups=groups)
    begun, energy = pl.pallas_call(
        early_kernel,
        in_specs=[pl.BlockSpec(memory_space=pltpu.VMEM)] * 4,
        out_specs=[
            pl.BlockSpec(memory_space=pltpu.HBM),
            pl.BlockSpec(memory_space=pltpu.VMEM),
        ],
        out_shape=[shape((comps, cells, lines)), shape((yz_count, LANES))],
        scratch_shapes=[
            pltpu.VMEM((comps, cells, lines), F32),
            pltpu.SemaphoreType.DMA((comps,)),
        ],
        compiler_params=LARGE,
        name="early_update",
    )(back, g, p_rows, q_rows)
    energies = spread(energy, "yz", axis_index_groups=[YZ_ORDER])
    total_count = comps * cells * lines * lax.axis_size("gx") * yz_count
    derivative, mean_square = pl.pallas_call(
        functools.partial(late_kernel, 1.0 / total_count),
        in_specs=[pl.BlockSpec(memory_space=pltpu.HBM)]
        + [pl.BlockSpec(memory_space=pltpu.VMEM)] * 5,
        out_specs=[pl.BlockSpec(memory_space=pltpu.HBM)] * 2,
        out_shape=[shape((comps, cells, lines)), shape((1, 1))],
        input_output_aliases={0: 0},
        scratch_shapes=[
            pltpu.SMEM((1, 1), F32),
            pltpu.VMEM((comps, cells, lines), F32),
            pltpu.SemaphoreType.DMA((comps + 1,)),
        ],
        compiler_params=LARGE,
        name="late_update",
    )(begun, energies, back, g, p_rows, q_rows)
    return derivative, mean_square[0, 0]


def solution(mesh):
    placed = (P(None, "gx", "yz"), P("gx", None, None))
    return jax.shard_map(
        on_device, mesh=mesh, in_specs=placed, out_specs=(P(None, "gx", "yz"), P()), check_vma=False
    )
```

```python
import functools

import jax
import jax.numpy as jnp
from jax import lax
from jax.experimental import pallas as pl
from jax.experimental.pallas import tpu as pltpu
from jax.sharding import PartitionSpec as P

COUPLING = 1.0 / 3.0
NEAR_WEIGHT = 7.0 / 9.0
FAR_WEIGHT = 1.0 / 36.0

GROUP = 16
GROUPS = 4
ORDER_OUT = tuple(4 * z + y for y in (2, 3, 1, 0) for z in (2, 3, 0, 1))
ORDER_BACK = tuple(4 * z + y for y in (2, 3, 1, 0) for z in (2, 3, 0, 1))
YZ_ORDER = (5, 4, 7, 6, 3, 2, 1, 0)
LANES = 128
CELLS = 64
CHUNK = 512
F32 = jnp.float32
BF16 = jnp.bfloat16
SMALL = pltpu.CompilerParams(vmem_limit_bytes=8 * 1024 * 1024)
LARGE = pltpu.CompilerParams(vmem_limit_bytes=16 * 1024 * 1024)


def lane_row(value, lanes=LANES):
    return jnp.broadcast_to(value, (1, lanes))


def tiled(value, copies):
    return jnp.concatenate([value] * copies, axis=1)


def parts_of(value):
    high = value.astype(BF16)
    rest = value - high.astype(F32)
    middle = rest.astype(BF16)
    return high, middle, (rest - middle.astype(F32)).astype(BF16)


def local_kernel(
    v_hbm, block_hbm, g_ref, send_ref, p_ref, q_ref, v_ref, mat_ref, pad_ref, block_ref, sems
):
    comps, _, lines = v_ref.shape
    inner = CELLS - 2
    stride = send_ref.shape[0] // GROUP
    block_copy = pltpu.make_async_copy(block_hbm, block_ref, sems.at[comps])
    block_copy.start()
    copies = [pltpu.make_async_copy(v_hbm.at[c], v_ref.at[c], sems.at[c]) for c in range(comps)]
    for copy in copies:
        copy.start()

    pad_ref[...] = jnp.zeros(pad_ref.shape, F32)
    block_copy.wait()
    pad_ref[0:inner, 0:inner] = block_ref[:, 0, :]
    padded = pltpu.roll(pltpu.roll(pad_ref[...], 1, 0), 1, 1)
    first = jnp.broadcast_to(COUPLING * padded[:, 1:2], (CELLS, LANES))
    last = jnp.broadcast_to(COUPLING * padded[:, inner : inner + 1], (CELLS, LANES))
    p_ref[...] = first
    q_ref[...] = last
    cols = lax.broadcasted_iota(jnp.int32, (1, LANES), 1)
    top = jnp.where(cols == 0, 1.0, 0.0) - COUPLING * padded[1:2]
    bottom = jnp.where(cols == CELLS - 1, 1.0, 0.0) - COUPLING * padded[inner : inner + 1]
    first_sum = jnp.sum(first * padded, axis=0, keepdims=True)
    last_sum = jnp.sum(last * padded, axis=0, keepdims=True)
    rows = lax.broadcasted_iota(jnp.int32, (16, LANES), 0)
    extra = jnp.where(rows == 0, top, 0.0)
    extra = jnp.where(rows == 1, bottom, extra)
    extra = jnp.where(rows == 2, first_sum, extra)
    extra = jnp.where(rows == 3, last_sum, extra)
    matrix = jnp.concatenate([padded, extra], 0)
    beside = pltpu.roll(matrix, 1, 1) + pltpu.roll(matrix, LANES - 1, 1)
    matrix = NEAR_WEIGHT * matrix + FAR_WEIGHT * beside
    high, middle, low = parts_of(matrix[:, 0:CELLS])
    mat_ref[...] = jnp.concatenate([high, middle, low, high, middle, high], 1)

    row8 = lax.broadcasted_iota(jnp.int32, (8, CHUNK), 0)
    energy = jnp.zeros((1, LANES), F32)
    for c in range(comps):
        copies[c].wait()
        for start in range(0, lines, CHUNK):
            v = v_ref[c, :, start : start + CHUNK]
            edge_0, edge_1 = v[0:1], v[CELLS - 1 : CELLS]
            below = jnp.concatenate([edge_0, v[: CELLS - 1]], 0)
            above = jnp.concatenate([v[1:], edge_1], 0)
            high, middle, low = parts_of(above - below)
            stacked = jnp.concatenate([high, high, high, middle, middle, low], 0)
            out = jnp.dot(mat_ref[...], stacked, preferred_element_type=F32)
            g = out[0:CELLS]
            g_ref[c, :, start : start + CHUNK] = g
            squares = jnp.sum(g * g, axis=0, keepdims=True)
            rows = out[CELLS : CELLS + 8]
            rows = jnp.where((row8 == 4) | (row8 == 5), pltpu.roll(v[0:8], 4, 0), rows)
            rows = jnp.where(row8 >= 6, v[CELLS - 8 : CELLS], rows)
            for j in range(CHUNK // LANES):
                at = slice(j * LANES, (j + 1) * LANES)
                energy = energy + squares[:, at]
                to = stride * (start // LANES + j) + 8 * c
                send_ref[to : to + 8, :] = rows[:, at]

    coefs = energy + pltpu.roll(energy, LANES // 2, 1)
    numbers = [
        first[1:2],
        last[1:2],
        first[inner : inner + 1],
        last[inner : inner + 1],
        jnp.sum(first * first, axis=0, keepdims=True),
        jnp.sum(first * last, axis=0, keepdims=True),
        jnp.sum(last * last, axis=0, keepdims=True),
    ]
    for i, number in enumerate(numbers):
        coefs = jnp.where(cols == i, number, coefs)
    for j in range(GROUP):
        to = stride * j + 8 * comps
        send_ref[to : to + 1, :] = coefs


def group_kernel(recv_ref, msg_ref, state_ref, open_ref, block_ref):
    count = recv_ref.shape[0] // GROUP
    stride = block_ref.shape[0] // GROUP
    comps = count // 8
    for i, place in enumerate(ORDER_OUT):
        to = stride * place
        block_ref[to : to + count, :] = recv_ref[count * i : count * (i + 1), :]
    width = comps * LANES

    def rows(r):
        parts = [block_ref[pl.ds(8 * i + r, GROUP, stride=stride), :] for i in range(comps)]
        return jnp.concatenate(parts, 1)

    numbers = block_ref[pl.ds(8 * comps, GROUP, stride=stride), :]

    def coef(r):
        return jnp.broadcast_to(numbers[:, r : r + 1], (GROUP, LANES))

    seg = lax.broadcasted_iota(jnp.int32, (GROUP, width), 0)
    seg_1 = lax.broadcasted_iota(jnp.int32, (GROUP, LANES), 0)

    def prev(x, s=1):
        return pltpu.roll(x, s, 0)

    def following(x, s=1):
        return pltpu.roll(x, GROUP - s, 0)

    b_first, b_last, pg, qg, v_0, v_1, v_62, v_63 = [rows(r) for r in range(8)]
    p_0, q_0, p_61, q_61, pp, pq, qq = [coef(r) for r in range(7)]
    upper = lax.broadcasted_iota(jnp.int32, (GROUP, LANES), 1) >= LANES // 2
    energy = jnp.where(upper, numbers, 0.0)
    jump_l = jnp.where(seg == 0, 0.0, prev(v_63) - v_0)
    jump_l2 = jnp.where(seg == 0, 0.0, prev(v_62) - v_0)
    jump_r = jnp.where(seg == GROUP - 1, 0.0, v_63 - following(v_0))
    jump_r2 = jnp.where(seg == GROUP - 1, 0.0, following(v_1) - v_63)
    b_first = b_first - (2.0 / 3.0) * jump_l - FAR_WEIGHT * jump_l2
    b_last = b_last - (2.0 / 3.0) * jump_r + FAR_WEIGHT * jump_r2

    unit_first = jnp.where(seg_1 == 0, 1.0, 0.0)
    unit_last = jnp.where(seg_1 == GROUP - 1, 1.0, 0.0)
    zero = jnp.zeros((GROUP, LANES), F32)
    third = jnp.full((GROUP, LANES), COUPLING, F32)
    rhs_f = jnp.concatenate([b_first, unit_first, zero], 1)
    rhs_l = jnp.concatenate([b_last, zero, unit_last], 1)
    f = (jnp.where(seg_1 == 0, 0.0, third), 1.0 - COUPLING * p_0, -COUPLING * q_0, rhs_f)
    l = (-COUPLING * p_61, 1.0 - COUPLING * q_61, jnp.where(seg_1 == GROUP - 1, 0.0, third), rhs_l)

    def reduce_level(mine, below, above):
        ratio_low = mine[0] / below[1]
        ratio_high = mine[2] / above[1]
        return (
            -ratio_low * below[0],
            mine[1] - ratio_low * below[2] - ratio_high * above[0],
            -ratio_high * above[2],
            mine[3] - tiled(ratio_low, comps + 2) * below[3] - tiled(ratio_high, comps + 2) * above[3],
        )

    f, l = (
        reduce_level(f, tuple(prev(x) for x in l), l),
        reduce_level(l, f, tuple(following(x) for x in f)),
    )
    step = 1
    while step < GROUP:
        f = reduce_level(f, tuple(prev(x, step) for x in f), tuple(following(x, step) for x in f))
        l = reduce_level(l, tuple(prev(x, step) for x in l), tuple(following(x, step) for x in l))
        step *= 2
    sol_f = f[3] / tiled(f[1], comps + 2)
    sol_l = l[3] / tiled(l[1], comps + 2)
    x_f, a_f, c_f = sol_f[:, :width], sol_f[:, width : width + LANES], sol_f[:, width + LANES :]
    x_l, a_l, c_l = sol_l[:, :width], sol_l[:, width : width + LANES], sol_l[:, width + LANES :]

    pp1, qq1 = pp + 1.0, qq + 1.0
    d_l, d_r = jump_l * (1.0 / 12.0), jump_r * (1.0 / 12.0)
    pq_w = tiled(pq, comps)
    m_f = tiled(pp1, comps) * x_f + pq_w * x_l - pg - d_l
    m_l = tiled(qq1, comps) * x_l + pq_w * x_f - qg - d_r

    def total(x):
        return jnp.sum(x, axis=0, keepdims=True)

    line_a = 2.0 * total(tiled(a_f, comps) * m_f + tiled(a_l, comps) * m_l)
    line_c = 2.0 * total(tiled(c_f, comps) * m_f + tiled(c_l, comps) * m_l)
    base = total(x_f * (m_f - pg - d_l) + x_l * (m_l - qg - d_r) + d_l * d_l + d_r * d_r)
    part = total(energy) * (1.0 / GROUP)
    for i in range(comps):
        part = part + base[:, i * LANES : (i + 1) * LANES]
    quad_aa = total(pp1 * a_f * a_f + 2.0 * pq * a_f * a_l + qq1 * a_l * a_l)
    quad_ac = total(pp1 * a_f * c_f + pq * (a_f * c_l + a_l * c_f) + qq1 * a_l * c_l)
    quad_cc = total(pp1 * c_f * c_f + 2.0 * pq * c_f * c_l + qq1 * c_l * c_l)

    end = GROUP - 1
    msg_ref[:, 0:width] = jnp.concatenate(
        [x_f[0:1], x_l[end:], line_a, line_c, v_0[0:1], v_1[0:1], v_62[end:], v_63[end:]], 0
    )
    msg_ref[:, width : width + LANES] = jnp.concatenate(
        [a_f[0:1], a_l[end:], c_f[0:1], c_l[end:], quad_aa, quad_ac, quad_cc, part], 0
    )
    state_ref[0] = x_f
    state_ref[1] = x_l
    state_ref[2] = jump_l
    state_ref[3] = jump_r
    open_ref[0] = a_f
    open_ref[1] = a_l
    open_ref[2] = c_f
    open_ref[3] = c_l


def eliminate(matrix, rhs, wide):
    size = len(rhs)
    matrix = [list(r) for r in matrix]
    rhs = list(rhs)
    inverse = [None] * size
    for k in range(size):
        inverse[k] = 1.0 / matrix[k][k]
        for i in range(k + 1, size):
            if matrix[i][k] is None:
                continue
            ratio = matrix[i][k] * inverse[k]
            for j in range(k + 1, size):
                if matrix[k][j] is not None:
                    old = matrix[i][j]
                    change = ratio * matrix[k][j]
                    matrix[i][j] = -change if old is None else old - change
            rhs[i] = rhs[i] - wide(ratio) * rhs[k]
    found = [None] * size
    for k in reversed(range(size)):
        value = rhs[k]
        for j in range(k + 1, size):
            if matrix[k][j] is not None:
                value = value - wide(matrix[k][j]) * found[j]
        found[k] = value * wide(inverse[k])
    return found


def unpacked(message, width):
    return (
        [message[r : r + 1, 0:width] for r in range(8)],
        [message[r : r + 1, width:] for r in range(8)],
    )


def pair_kernel(both_ref, msg_ref, state_ref, open_ref):
    width = both_ref.shape[2] - LANES
    comps = width // LANES

    def wide(x):
        return tiled(x, comps)

    left, l = unpacked(both_ref[0], width)
    right, r = unpacked(both_ref[1], width)
    x_f, x_l, line_a, line_c, v_0, v_1, v_62, v_63 = [list(p) for p in zip(left, right)]
    a_f, a_l, c_f, c_l, q_aa, q_ac, q_cc, part = [list(p) for p in zip(l, r)]

    jump = v_63[0] - v_0[1]
    rhs_c = -COUPLING * x_f[1] - (2.0 / 3.0) * jump + FAR_WEIGHT * (v_1[1] - v_63[0])
    rhs_a = -COUPLING * x_l[0] - (2.0 / 3.0) * jump - FAR_WEIGHT * (v_62[0] - v_0[1])
    inverse = 1.0 / (1.0 - (COUPLING * a_f[1]) * (COUPLING * c_l[0]))
    to_c, to_a = COUPLING * a_f[1] * inverse, COUPLING * c_l[0] * inverse
    c_0 = wide(inverse) * rhs_c - wide(to_c) * rhs_a
    c_alpha = to_c * (COUPLING * a_l[0])
    c_gamma = -inverse * (COUPLING * c_f[1])
    a_0 = wide(inverse) * rhs_a - wide(to_a) * rhs_c
    a_alpha = -inverse * (COUPLING * a_l[0])
    a_gamma = to_a * (COUPLING * c_f[1])

    d = jump * (1.0 / 12.0)
    inner_u = x_f[1] + wide(a_f[1]) * a_0
    inner_w = x_l[0] + wide(c_l[0]) * c_0
    both_alpha = a_f[1] * a_alpha + a_l[0] + c_l[0] * c_alpha
    both_gamma = a_f[1] * a_gamma + c_f[1] + c_l[0] * c_gamma
    slope_c = line_c[0] + wide(2.0 * q_cc[0]) * c_0
    slope_a = line_a[1] + wide(2.0 * q_aa[1]) * a_0
    line_alpha = line_a[0] + wide(2.0 * q_ac[0]) * c_0 + wide(c_alpha) * slope_c
    line_alpha = line_alpha + wide(a_alpha) * slope_a - wide(2.0 * both_alpha) * d
    line_gamma = line_c[1] + wide(2.0 * q_ac[1]) * a_0 + wide(a_gamma) * slope_a
    line_gamma = line_gamma + wide(c_gamma) * slope_c - wide(2.0 * both_gamma) * d
    base = c_0 * (line_c[0] + wide(q_cc[0]) * c_0) + a_0 * (line_a[1] + wide(q_aa[1]) * a_0)
    base = base + 2.0 * d * (d - inner_u - inner_w)
    total = part[0] + part[1]
    for i in range(comps):
        total = total + base[:, i * LANES : (i + 1) * LANES]
    q_alpha = q_aa[0] + c_alpha * (2.0 * q_ac[0] + q_cc[0] * c_alpha) + q_aa[1] * a_alpha * a_alpha
    q_gamma = q_cc[1] + a_gamma * (2.0 * q_ac[1] + q_aa[1] * a_gamma) + q_cc[0] * c_gamma * c_gamma
    q_mixed = c_gamma * (q_ac[0] + q_cc[0] * c_alpha) + a_alpha * (q_ac[1] + q_aa[1] * a_gamma)

    msg_ref[:, 0:width] = jnp.concatenate(
        [
            x_f[0] + wide(c_f[0]) * c_0,
            x_l[1] + wide(a_l[1]) * a_0,
            line_alpha,
            line_gamma,
            v_0[0],
            v_1[0],
            v_62[1],
            v_63[1],
        ],
        0,
    )
    msg_ref[:, width:] = jnp.concatenate(
        [
            a_f[0] + c_f[0] * c_alpha,
            a_l[1] * a_alpha,
            c_f[0] * c_gamma,
            c_l[1] + a_l[1] * a_gamma,
            q_alpha,
            q_mixed,
            q_gamma,
            total,
        ],
        0,
    )
    none = jnp.zeros_like(jump)
    state_ref[...] = jnp.concatenate([c_0, a_0, jump] + [none] * 5, 0)
    none = jnp.zeros_like(inverse)
    open_ref[...] = jnp.concatenate([c_alpha, c_gamma, a_alpha, a_gamma] + [none] * 4, 0)


def join_kernel(all_ref, pair_ref, pair_open_ref, state_ref, open_ref, send_ref, block_ref):
    width = state_ref.shape[2]
    comps = width // LANES
    group = lax.axis_index("gx") // GROUP
    pairs = all_ref.shape[0]

    def wide(x):
        return tiled(x, comps)

    data, scal = zip(*[unpacked(all_ref[t], width) for t in range(pairs)])
    x_f, x_l, line_a, line_c, v_0, v_1, v_62, v_63 = [[d[r] for d in data] for r in range(8)]
    a_f, a_l, c_f, c_l, q_aa, q_ac, q_cc, part = [[s[r] for s in scal] for r in range(8)]

    one = jnp.ones((1, LANES), F32)
    jump = [v_63[t - 1] - v_0[t] for t in range(pairs)]
    matrix, rhs = [], []
    for t in range(pairs):
        before, after = (t - 1) % pairs, (t + 1) % pairs
        row_a, row_c = [None] * (2 * pairs), [None] * (2 * pairs)
        row_a[2 * t] = one
        row_a[2 * before] = COUPLING * a_l[before]
        row_a[2 * before + 1] = COUPLING * c_l[before]
        row_c[2 * t + 1] = one
        row_c[2 * after] = COUPLING * a_f[after]
        row_c[2 * after + 1] = COUPLING * c_f[after]
        matrix += [row_a, row_c]
        rhs.append(
            -COUPLING * x_l[before] - (2.0 / 3.0) * jump[t] - FAR_WEIGHT * (v_62[before] - v_0[t])
        )
        rhs.append(
            -COUPLING * x_f[after] - (2.0 / 3.0) * jump[after] + FAR_WEIGHT * (v_1[after] - v_63[t])
        )
    found = eliminate(matrix, rhs, wide)
    value_a, value_c = found[0::2], found[1::2]

    energy = jnp.zeros((1, LANES), F32)
    for t in range(pairs):
        a, c = value_a[t], value_c[t]
        after = (t + 1) % pairs
        u_end = x_f[t] + wide(a_f[t]) * a + wide(c_f[t]) * c
        w_end = x_l[t] + wide(a_l[t]) * a + wide(c_l[t]) * c
        d_l, d_r = jump[t] * (1.0 / 12.0), jump[after] * (1.0 / 12.0)
        lines = a * (line_a[t] + wide(q_aa[t]) * a + wide(2.0 * q_ac[t]) * c)
        lines = lines + c * (line_c[t] + wide(q_cc[t]) * c)
        lines = lines + d_l * (d_l - 2.0 * u_end) + d_r * (d_r - 2.0 * w_end)
        energy = energy + part[t]
        for i in range(comps):
            energy = energy + lines[:, i * LANES : (i + 1) * LANES]

    first_pair = (group == 0) | (group == 3)
    on_left = (group == 3) | (group == 1)

    def mine(values):
        return jnp.where(first_pair, values[0], values[1])

    alpha, gamma = mine(value_a), mine(value_c)
    inner = [pair_ref[r : r + 1, :] for r in range(3)]
    slope = [wide(pair_open_ref[r : r + 1, :]) for r in range(4)]
    inner_c = inner[0] + slope[0] * alpha + slope[1] * gamma
    inner_a = inner[1] + slope[2] * alpha + slope[3] * gamma
    a, c = jnp.where(on_left, alpha, inner_a), jnp.where(on_left, inner_c, gamma)
    left = jnp.where(on_left, mine(jump), inner[2])
    right = jnp.where(on_left, inner[2], mine(jump[1:] + jump[:1]))
    seg = lax.broadcasted_iota(jnp.int32, (GROUP, width), 0)
    u_t = state_ref[0] + wide(open_ref[0]) * a + wide(open_ref[2]) * c
    w_t = state_ref[1] + wide(open_ref[1]) * a + wide(open_ref[3]) * c
    jump_l = jnp.where(seg == 0, left, state_ref[2])
    jump_r = jnp.where(seg == GROUP - 1, right, state_ref[3])
    u = u_t - jump_l * (1.0 / 12.0)
    w = w_t - jump_r * (1.0 / 12.0)
    count = send_ref.shape[0] // GROUP
    stride = block_ref.shape[0] // GROUP
    for i in range(comps):
        for r, value in enumerate((u_t, w_t, u, w)):
            part_i = value[:, i * LANES : (i + 1) * LANES]
            block_ref[pl.ds(4 * i + r, GROUP, stride=stride), :] = part_i
    block_ref[pl.ds(4 * comps, GROUP, stride=stride), :] = jnp.broadcast_to(energy, (GROUP, LANES))
    for i, place in enumerate(ORDER_BACK):
        send_ref[count * i : count * (i + 1), :] = block_ref[stride * place : stride * place + count, :]


def update_cells(recv_ref, g_ref, p_ref, q_ref, out_hbm, out_ref, sems):
    comps, _, lines = g_ref.shape
    stride = recv_ref.shape[0] // GROUP
    row8 = lax.broadcasted_iota(jnp.int32, (8, LANES), 0)
    first, last = p_ref[...], q_ref[...]
    copies = []
    for c in range(comps):
        for j, place in enumerate(ORDER_OUT):
            at = slice(j * LANES, (j + 1) * LANES)
            base = stride * ORDER_BACK.index(place) + 4 * c
            u_t, w_t, u, w = [recv_ref[base + r : base + r + 1, :] for r in range(4)]
            value = g_ref[c, :, at] - first * u_t - last * w_t
            out_ref[c, 0:8, at] = jnp.where(row8 == 0, u, value[0:8])
            out_ref[c, 8 : CELLS - 8, at] = value[8 : CELLS - 8]
            out_ref[c, CELLS - 8 :, at] = jnp.where(row8 == 7, w, value[CELLS - 8 :])
        copy = pltpu.make_async_copy(out_ref.at[c], out_hbm.at[c], sems.at[c])
        copy.start()
        copies.append(copy)
    for copy in copies:
        copy.wait()


def early_device():
    return lax.axis_index("yz") % 2 == 1


def early_kernel(recv_ref, g_ref, p_ref, q_ref, out_hbm, energy_ref, out_ref, sems):
    stride = recv_ref.shape[0] // GROUP
    energy = recv_ref[pl.ds(stride - 1, GROUP, stride=stride), :]
    energy_ref[...] = jnp.broadcast_to(jnp.sum(energy, axis=0, keepdims=True), energy_ref.shape)

    @pl.when(early_device())
    def _():
        update_cells(recv_ref, g_ref, p_ref, q_ref, out_hbm, out_ref, sems)


def late_kernel(
    scale, begun_hbm, energy_ref, recv_ref, g_ref, p_ref, q_ref, out_hbm, mean_hbm, mean_ref, out_ref, sems
):
    comps = g_ref.shape[0]
    mean_ref[0, 0] = jnp.sum(energy_ref[...]) * scale
    mean_copy = pltpu.make_async_copy(mean_ref, mean_hbm, sems.at[comps])
    mean_copy.start()

    @pl.when(jnp.logical_not(early_device()))
    def _():
        update_cells(recv_ref, g_ref, p_ref, q_ref, out_hbm, out_ref, sems)

    mean_copy.wait()


def on_device(velocity, blocks):
    comps, cells, lines = velocity.shape
    width = comps * LANES
    send_rows, back_rows = 8 * comps + 1, 4 * comps + 1
    yz_count = lax.axis_size("yz")
    groups_out = [[GROUP * t + i for i in ORDER_OUT] for t in range(GROUPS)]
    groups_back = [[GROUP * t + i for i in ORDER_BACK] for t in range(GROUPS)]
    shape = functools.partial(jax.ShapeDtypeStruct, dtype=F32)

    g, send, p_rows, q_rows = pl.pallas_call(
        local_kernel,
        in_specs=[
            pl.BlockSpec(memory_space=pltpu.HBM),
            pl.BlockSpec(memory_space=pltpu.HBM),
        ],
        out_specs=[pl.BlockSpec(memory_space=pltpu.VMEM)] * 4,
        out_shape=[
            shape((comps, cells, lines)),
            shape((GROUP * send_rows, LANES)),
            shape((cells, LANES)),
            shape((cells, LANES)),
        ],
        scratch_shapes=[
            pltpu.VMEM((comps, cells, lines), F32),
            pltpu.VMEM((cells + 16, 6 * cells), BF16),
            pltpu.VMEM((cells, LANES), F32),
            pltpu.VMEM((cells - 2, 1, cells - 2), F32),
            pltpu.SemaphoreType.DMA((comps + 1,)),
        ],
        compiler_params=LARGE,
        name="local_solve",
    )(
        pltpu.with_memory_space_constraint(velocity, pltpu.HBM),
        pltpu.with_memory_space_constraint(jnp.transpose(blocks, (1, 0, 2)), pltpu.HBM),
    )

    def spread(value, axis, **kwargs):
        rows = value.reshape(value.shape[0], 1, LANES)
        return lax.all_to_all(rows, axis, 0, 0, tiled=True, **kwargs).reshape(value.shape)

    recv = spread(send, "gx", axis_index_groups=groups_out)
    msg, state, opened = pl.pallas_call(
        group_kernel,
        out_shape=[
            shape((8, width + LANES)),
            shape((4, GROUP, width)),
            shape((4, GROUP, LANES)),
        ],
        scratch_shapes=[pltpu.VMEM((GROUP * 8 * (comps + 1), LANES), F32)],
        compiler_params=SMALL,
        name="group_solve",
    )(recv)

    def joined(value, pairs):
        members = [[GROUP * t + i for t in pair] for pair in pairs for i in range(GROUP)]
        return lax.all_gather(value, "gx", axis_index_groups=members)

    near = joined(msg, ((3, 0), (1, 2)))
    pair_msg, pair_state, pair_open = pl.pallas_call(
        pair_kernel,
        out_shape=[shape((8, width + LANES)), shape((8, width)), shape((8, LANES))],
        compiler_params=SMALL,
        name="pair_groups",
    )(near)
    every = joined(pair_msg, ((0, 1), (3, 2)))
    send_back = pl.pallas_call(
        join_kernel,
        out_shape=shape((GROUP * back_rows, LANES)),
        scratch_shapes=[pltpu.VMEM((GROUP * -(-back_rows // 8) * 8, LANES), F32)],
        compiler_params=SMALL,
        name="join_groups",
    )(every, pair_state, pair_open, state, opened)
    back = spread(send_back, "gx", axis_index_groups=groups_back)
    begun, energy = pl.pallas_call(
        early_kernel,
        in_specs=[pl.BlockSpec(memory_space=pltpu.VMEM)] * 4,
        out_specs=[
            pl.BlockSpec(memory_space=pltpu.HBM),
            pl.BlockSpec(memory_space=pltpu.VMEM),
        ],
        out_shape=[shape((comps, cells, lines)), shape((yz_count, LANES))],
        scratch_shapes=[
            pltpu.VMEM((comps, cells, lines), F32),
            pltpu.SemaphoreType.DMA((comps,)),
        ],
        compiler_params=LARGE,
        name="early_update",
    )(back, g, p_rows, q_rows)
    energies = spread(energy, "yz", axis_index_groups=[YZ_ORDER])
    total_count = comps * cells * lines * lax.axis_size("gx") * yz_count
    derivative, mean_square = pl.pallas_call(
        functools.partial(late_kernel, 1.0 / total_count),
        in_specs=[pl.BlockSpec(memory_space=pltpu.HBM)]
        + [pl.BlockSpec(memory_space=pltpu.VMEM)] * 5,
        out_specs=[pl.BlockSpec(memory_space=pltpu.HBM)] * 2,
        out_shape=[shape((comps, cells, lines)), shape((1, 1))],
        input_output_aliases={0: 0},
        scratch_shapes=[
            pltpu.SMEM((1, 1), F32),
            pltpu.VMEM((comps, cells, lines), F32),
            pltpu.SemaphoreType.DMA((comps + 1,)),
        ],
        compiler_params=LARGE,
        name="late_update",
    )(begun, energies, back, g, p_rows, q_rows)
    return derivative, mean_square[0, 0]


def solution(mesh):
    placed = (P(None, "gx", "yz"), P("gx", None, None))
    return jax.shard_map(
        on_device, mesh=mesh, in_specs=placed, out_specs=(P(None, "gx", "yz"), P()), check_vma=False
    )
```

```python
import functools

import jax
import jax.numpy as jnp
from jax import lax
from jax.experimental import pallas as pl
from jax.experimental.pallas import tpu as pltpu
from jax.sharding import PartitionSpec as P

COUPLING = 1.0 / 3.0
NEAR_WEIGHT = 7.0 / 9.0
FAR_WEIGHT = 1.0 / 36.0

GROUP = 16
GROUPS = 4
ORDER_OUT = tuple(4 * z + y for y in (2, 3, 1, 0) for z in (2, 3, 0, 1))
ORDER_BACK = tuple(4 * z + y for y in (2, 3, 1, 0) for z in (2, 3, 0, 1))
YZ_ORDER = (5, 4, 3, 2, 7, 6, 1, 0)
LANES = 128
CELLS = 64
CHUNK = 512
F32 = jnp.float32
BF16 = jnp.bfloat16
SMALL = pltpu.CompilerParams(vmem_limit_bytes=8 * 1024 * 1024)
LARGE = pltpu.CompilerParams(vmem_limit_bytes=16 * 1024 * 1024)


def lane_row(value, lanes=LANES):
    return jnp.broadcast_to(value, (1, lanes))


def tiled(value, copies):
    return jnp.concatenate([value] * copies, axis=1)


def parts_of(value):
    high = value.astype(BF16)
    rest = value - high.astype(F32)
    middle = rest.astype(BF16)
    return high, middle, (rest - middle.astype(F32)).astype(BF16)


def local_kernel(
    v_hbm, block_hbm, g_ref, send_ref, p_ref, q_ref, v_ref, mat_ref, pad_ref, block_ref, sems
):
    comps, _, lines = v_ref.shape
    inner = CELLS - 2
    stride = send_ref.shape[0] // GROUP
    block_copy = pltpu.make_async_copy(block_hbm, block_ref, sems.at[comps])
    block_copy.start()
    copies = [pltpu.make_async_copy(v_hbm.at[c], v_ref.at[c], sems.at[c]) for c in range(comps)]
    for copy in copies:
        copy.start()

    pad_ref[...] = jnp.zeros(pad_ref.shape, F32)
    block_copy.wait()
    pad_ref[0:inner, 0:inner] = block_ref[:, 0, :]
    padded = pltpu.roll(pltpu.roll(pad_ref[...], 1, 0), 1, 1)
    first = jnp.broadcast_to(COUPLING * padded[:, 1:2], (CELLS, LANES))
    last = jnp.broadcast_to(COUPLING * padded[:, inner : inner + 1], (CELLS, LANES))
    p_ref[...] = first
    q_ref[...] = last
    cols = lax.broadcasted_iota(jnp.int32, (1, LANES), 1)
    top = jnp.where(cols == 0, 1.0, 0.0) - COUPLING * padded[1:2]
    bottom = jnp.where(cols == CELLS - 1, 1.0, 0.0) - COUPLING * padded[inner : inner + 1]
    first_sum = jnp.sum(first * padded, axis=0, keepdims=True)
    last_sum = jnp.sum(last * padded, axis=0, keepdims=True)
    rows = lax.broadcasted_iota(jnp.int32, (16, LANES), 0)
    extra = jnp.where(rows == 0, top, 0.0)
    extra = jnp.where(rows == 1, bottom, extra)
    extra = jnp.where(rows == 2, first_sum, extra)
    extra = jnp.where(rows == 3, last_sum, extra)
    matrix = jnp.concatenate([padded, extra], 0)
    beside = pltpu.roll(matrix, 1, 1) + pltpu.roll(matrix, LANES - 1, 1)
    matrix = NEAR_WEIGHT * matrix + FAR_WEIGHT * beside
    high, middle, low = parts_of(matrix[:, 0:CELLS])
    mat_ref[...] = jnp.concatenate([high, middle, low, high, middle, high], 1)

    row8 = lax.broadcasted_iota(jnp.int32, (8, CHUNK), 0)
    energy = jnp.zeros((1, LANES), F32)
    for c in range(comps):
        copies[c].wait()
        for start in range(0, lines, CHUNK):
            v = v_ref[c, :, start : start + CHUNK]
            edge_0, edge_1 = v[0:1], v[CELLS - 1 : CELLS]
            below = jnp.concatenate([edge_0, v[: CELLS - 1]], 0)
            above = jnp.concatenate([v[1:], edge_1], 0)
            high, middle, low = parts_of(above - below)
            stacked = jnp.concatenate([high, high, high, middle, middle, low], 0)
            out = jnp.dot(mat_ref[...], stacked, preferred_element_type=F32)
            g = out[0:CELLS]
            g_ref[c, :, start : start + CHUNK] = g
            squares = jnp.sum(g * g, axis=0, keepdims=True)
            rows = out[CELLS : CELLS + 8]
            rows = jnp.where((row8 == 4) | (row8 == 5), pltpu.roll(v[0:8], 4, 0), rows)
            rows = jnp.where(row8 >= 6, v[CELLS - 8 : CELLS], rows)
            for j in range(CHUNK // LANES):
                at = slice(j * LANES, (j + 1) * LANES)
                energy = energy + squares[:, at]
                to = stride * (start // LANES + j) + 8 * c
                send_ref[to : to + 8, :] = rows[:, at]

    coefs = energy + pltpu.roll(energy, LANES // 2, 1)
    numbers = [
        first[1:2],
        last[1:2],
        first[inner : inner + 1],
        last[inner : inner + 1],
        jnp.sum(first * first, axis=0, keepdims=True),
        jnp.sum(first * last, axis=0, keepdims=True),
        jnp.sum(last * last, axis=0, keepdims=True),
    ]
    for i, number in enumerate(numbers):
        coefs = jnp.where(cols == i, number, coefs)
    for j in range(GROUP):
        to = stride * j + 8 * comps
        send_ref[to : to + 1, :] = coefs


def group_kernel(recv_ref, msg_ref, state_ref, open_ref, block_ref):
    count = recv_ref.shape[0] // GROUP
    stride = block_ref.shape[0] // GROUP
    comps = count // 8
    for i, place in enumerate(ORDER_OUT):
        to = stride * place
        block_ref[to : to + count, :] = recv_ref[count * i : count * (i + 1), :]
    width = comps * LANES

    def rows(r):
        parts = [block_ref[pl.ds(8 * i + r, GROUP, stride=stride), :] for i in range(comps)]
        return jnp.concatenate(parts, 1)

    numbers = block_ref[pl.ds(8 * comps, GROUP, stride=stride), :]

    def coef(r):
        return jnp.broadcast_to(numbers[:, r : r + 1], (GROUP, LANES))

    seg = lax.broadcasted_iota(jnp.int32, (GROUP, width), 0)
    seg_1 = lax.broadcasted_iota(jnp.int32, (GROUP, LANES), 0)

    def prev(x, s=1):
        return pltpu.roll(x, s, 0)

    def following(x, s=1):
        return pltpu.roll(x, GROUP - s, 0)

    b_first, b_last, pg, qg, v_0, v_1, v_62, v_63 = [rows(r) for r in range(8)]
    p_0, q_0, p_61, q_61, pp, pq, qq = [coef(r) for r in range(7)]
    upper = lax.broadcasted_iota(jnp.int32, (GROUP, LANES), 1) >= LANES // 2
    energy = jnp.where(upper, numbers, 0.0)
    jump_l = jnp.where(seg == 0, 0.0, prev(v_63) - v_0)
    jump_l2 = jnp.where(seg == 0, 0.0, prev(v_62) - v_0)
    jump_r = jnp.where(seg == GROUP - 1, 0.0, v_63 - following(v_0))
    jump_r2 = jnp.where(seg == GROUP - 1, 0.0, following(v_1) - v_63)
    b_first = b_first - (2.0 / 3.0) * jump_l - FAR_WEIGHT * jump_l2
    b_last = b_last - (2.0 / 3.0) * jump_r + FAR_WEIGHT * jump_r2

    unit_first = jnp.where(seg_1 == 0, 1.0, 0.0)
    unit_last = jnp.where(seg_1 == GROUP - 1, 1.0, 0.0)
    zero = jnp.zeros((GROUP, LANES), F32)
    third = jnp.full((GROUP, LANES), COUPLING, F32)
    rhs_f = jnp.concatenate([b_first, unit_first, zero], 1)
    rhs_l = jnp.concatenate([b_last, zero, unit_last], 1)
    f = (jnp.where(seg_1 == 0, 0.0, third), 1.0 - COUPLING * p_0, -COUPLING * q_0, rhs_f)
    l = (-COUPLING * p_61, 1.0 - COUPLING * q_61, jnp.where(seg_1 == GROUP - 1, 0.0, third), rhs_l)

    def reduce_level(mine, below, above):
        ratio_low = mine[0] / below[1]
        ratio_high = mine[2] / above[1]
        return (
            -ratio_low * below[0],
            mine[1] - ratio_low * below[2] - ratio_high * above[0],
            -ratio_high * above[2],
            mine[3] - tiled(ratio_low, comps + 2) * below[3] - tiled(ratio_high, comps + 2) * above[3],
        )

    f, l = (
        reduce_level(f, tuple(prev(x) for x in l), l),
        reduce_level(l, f, tuple(following(x) for x in f)),
    )
    step = 1
    while step < GROUP:
        f = reduce_level(f, tuple(prev(x, step) for x in f), tuple(following(x, step) for x in f))
        l = reduce_level(l, tuple(prev(x, step) for x in l), tuple(following(x, step) for x in l))
        step *= 2
    sol_f = f[3] / tiled(f[1], comps + 2)
    sol_l = l[3] / tiled(l[1], comps + 2)
    x_f, a_f, c_f = sol_f[:, :width], sol_f[:, width : width + LANES], sol_f[:, width + LANES :]
    x_l, a_l, c_l = sol_l[:, :width], sol_l[:, width : width + LANES], sol_l[:, width + LANES :]

    pp1, qq1 = pp + 1.0, qq + 1.0
    d_l, d_r = jump_l * (1.0 / 12.0), jump_r * (1.0 / 12.0)
    pq_w = tiled(pq, comps)
    m_f = tiled(pp1, comps) * x_f + pq_w * x_l - pg - d_l
    m_l = tiled(qq1, comps) * x_l + pq_w * x_f - qg - d_r

    def total(x):
        return jnp.sum(x, axis=0, keepdims=True)

    line_a = 2.0 * total(tiled(a_f, comps) * m_f + tiled(a_l, comps) * m_l)
    line_c = 2.0 * total(tiled(c_f, comps) * m_f + tiled(c_l, comps) * m_l)
    base = total(x_f * (m_f - pg - d_l) + x_l * (m_l - qg - d_r) + d_l * d_l + d_r * d_r)
    part = total(energy) * (1.0 / GROUP)
    for i in range(comps):
        part = part + base[:, i * LANES : (i + 1) * LANES]
    quad_aa = total(pp1 * a_f * a_f + 2.0 * pq * a_f * a_l + qq1 * a_l * a_l)
    quad_ac = total(pp1 * a_f * c_f + pq * (a_f * c_l + a_l * c_f) + qq1 * a_l * c_l)
    quad_cc = total(pp1 * c_f * c_f + 2.0 * pq * c_f * c_l + qq1 * c_l * c_l)

    end = GROUP - 1
    msg_ref[:, 0:width] = jnp.concatenate(
        [x_f[0:1], x_l[end:], line_a, line_c, v_0[0:1], v_1[0:1], v_62[end:], v_63[end:]], 0
    )
    msg_ref[:, width : width + LANES] = jnp.concatenate(
        [a_f[0:1], a_l[end:], c_f[0:1], c_l[end:], quad_aa, quad_ac, quad_cc, part], 0
    )
    state_ref[0] = x_f
    state_ref[1] = x_l
    state_ref[2] = jump_l
    state_ref[3] = jump_r
    open_ref[0] = a_f
    open_ref[1] = a_l
    open_ref[2] = c_f
    open_ref[3] = c_l


def eliminate(matrix, rhs, wide):
    size = len(rhs)
    matrix = [list(r) for r in matrix]
    rhs = list(rhs)
    inverse = [None] * size
    for k in range(size):
        inverse[k] = 1.0 / matrix[k][k]
        for i in range(k + 1, size):
            if matrix[i][k] is None:
                continue
            ratio = matrix[i][k] * inverse[k]
            for j in range(k + 1, size):
                if matrix[k][j] is not None:
                    old = matrix[i][j]
                    change = ratio * matrix[k][j]
                    matrix[i][j] = -change if old is None else old - change
            rhs[i] = rhs[i] - wide(ratio) * rhs[k]
    found = [None] * size
    for k in reversed(range(size)):
        value = rhs[k]
        for j in range(k + 1, size):
            if matrix[k][j] is not None:
                value = value - wide(matrix[k][j]) * found[j]
        found[k] = value * wide(inverse[k])
    return found


def unpacked(message, width):
    return (
        [message[r : r + 1, 0:width] for r in range(8)],
        [message[r : r + 1, width:] for r in range(8)],
    )


def pair_kernel(both_ref, msg_ref, state_ref, open_ref):
    width = both_ref.shape[2] - LANES
    comps = width // LANES

    def wide(x):
        return tiled(x, comps)

    left, l = unpacked(both_ref[0], width)
    right, r = unpacked(both_ref[1], width)
    x_f, x_l, line_a, line_c, v_0, v_1, v_62, v_63 = [list(p) for p in zip(left, right)]
    a_f, a_l, c_f, c_l, q_aa, q_ac, q_cc, part = [list(p) for p in zip(l, r)]

    jump = v_63[0] - v_0[1]
    rhs_c = -COUPLING * x_f[1] - (2.0 / 3.0) * jump + FAR_WEIGHT * (v_1[1] - v_63[0])
    rhs_a = -COUPLING * x_l[0] - (2.0 / 3.0) * jump - FAR_WEIGHT * (v_62[0] - v_0[1])
    inverse = 1.0 / (1.0 - (COUPLING * a_f[1]) * (COUPLING * c_l[0]))
    to_c, to_a = COUPLING * a_f[1] * inverse, COUPLING * c_l[0] * inverse
    c_0 = wide(inverse) * rhs_c - wide(to_c) * rhs_a
    c_alpha = to_c * (COUPLING * a_l[0])
    c_gamma = -inverse * (COUPLING * c_f[1])
    a_0 = wide(inverse) * rhs_a - wide(to_a) * rhs_c
    a_alpha = -inverse * (COUPLING * a_l[0])
    a_gamma = to_a * (COUPLING * c_f[1])

    d = jump * (1.0 / 12.0)
    inner_u = x_f[1] + wide(a_f[1]) * a_0
    inner_w = x_l[0] + wide(c_l[0]) * c_0
    both_alpha = a_f[1] * a_alpha + a_l[0] + c_l[0] * c_alpha
    both_gamma = a_f[1] * a_gamma + c_f[1] + c_l[0] * c_gamma
    slope_c = line_c[0] + wide(2.0 * q_cc[0]) * c_0
    slope_a = line_a[1] + wide(2.0 * q_aa[1]) * a_0
    line_alpha = line_a[0] + wide(2.0 * q_ac[0]) * c_0 + wide(c_alpha) * slope_c
    line_alpha = line_alpha + wide(a_alpha) * slope_a - wide(2.0 * both_alpha) * d
    line_gamma = line_c[1] + wide(2.0 * q_ac[1]) * a_0 + wide(a_gamma) * slope_a
    line_gamma = line_gamma + wide(c_gamma) * slope_c - wide(2.0 * both_gamma) * d
    base = c_0 * (line_c[0] + wide(q_cc[0]) * c_0) + a_0 * (line_a[1] + wide(q_aa[1]) * a_0)
    base = base + 2.0 * d * (d - inner_u - inner_w)
    total = part[0] + part[1]
    for i in range(comps):
        total = total + base[:, i * LANES : (i + 1) * LANES]
    q_alpha = q_aa[0] + c_alpha * (2.0 * q_ac[0] + q_cc[0] * c_alpha) + q_aa[1] * a_alpha * a_alpha
    q_gamma = q_cc[1] + a_gamma * (2.0 * q_ac[1] + q_aa[1] * a_gamma) + q_cc[0] * c_gamma * c_gamma
    q_mixed = c_gamma * (q_ac[0] + q_cc[0] * c_alpha) + a_alpha * (q_ac[1] + q_aa[1] * a_gamma)

    msg_ref[:, 0:width] = jnp.concatenate(
        [
            x_f[0] + wide(c_f[0]) * c_0,
            x_l[1] + wide(a_l[1]) * a_0,
            line_alpha,
            line_gamma,
            v_0[0],
            v_1[0],
            v_62[1],
            v_63[1],
        ],
        0,
    )
    msg_ref[:, width:] = jnp.concatenate(
        [
            a_f[0] + c_f[0] * c_alpha,
            a_l[1] * a_alpha,
            c_f[0] * c_gamma,
            c_l[1] + a_l[1] * a_gamma,
            q_alpha,
            q_mixed,
            q_gamma,
            total,
        ],
        0,
    )
    none = jnp.zeros_like(jump)
    state_ref[...] = jnp.concatenate([c_0, a_0, jump] + [none] * 5, 0)
    none = jnp.zeros_like(inverse)
    open_ref[...] = jnp.concatenate([c_alpha, c_gamma, a_alpha, a_gamma] + [none] * 4, 0)


def join_kernel(all_ref, pair_ref, pair_open_ref, state_ref, open_ref, send_ref, block_ref):
    width = state_ref.shape[2]
    comps = width // LANES
    group = lax.axis_index("gx") // GROUP
    pairs = all_ref.shape[0]

    def wide(x):
        return tiled(x, comps)

    data, scal = zip(*[unpacked(all_ref[t], width) for t in range(pairs)])
    x_f, x_l, line_a, line_c, v_0, v_1, v_62, v_63 = [[d[r] for d in data] for r in range(8)]
    a_f, a_l, c_f, c_l, q_aa, q_ac, q_cc, part = [[s[r] for s in scal] for r in range(8)]

    one = jnp.ones((1, LANES), F32)
    jump = [v_63[t - 1] - v_0[t] for t in range(pairs)]
    matrix, rhs = [], []
    for t in range(pairs):
        before, after = (t - 1) % pairs, (t + 1) % pairs
        row_a, row_c = [None] * (2 * pairs), [None] * (2 * pairs)
        row_a[2 * t] = one
        row_a[2 * before] = COUPLING * a_l[before]
        row_a[2 * before + 1] = COUPLING * c_l[before]
        row_c[2 * t + 1] = one
        row_c[2 * after] = COUPLING * a_f[after]
        row_c[2 * after + 1] = COUPLING * c_f[after]
        matrix += [row_a, row_c]
        rhs.append(
            -COUPLING * x_l[before] - (2.0 / 3.0) * jump[t] - FAR_WEIGHT * (v_62[before] - v_0[t])
        )
        rhs.append(
            -COUPLING * x_f[after] - (2.0 / 3.0) * jump[after] + FAR_WEIGHT * (v_1[after] - v_63[t])
        )
    found = eliminate(matrix, rhs, wide)
    value_a, value_c = found[0::2], found[1::2]

    energy = jnp.zeros((1, LANES), F32)
    for t in range(pairs):
        a, c = value_a[t], value_c[t]
        after = (t + 1) % pairs
        u_end = x_f[t] + wide(a_f[t]) * a + wide(c_f[t]) * c
        w_end = x_l[t] + wide(a_l[t]) * a + wide(c_l[t]) * c
        d_l, d_r = jump[t] * (1.0 / 12.0), jump[after] * (1.0 / 12.0)
        lines = a * (line_a[t] + wide(q_aa[t]) * a + wide(2.0 * q_ac[t]) * c)
        lines = lines + c * (line_c[t] + wide(q_cc[t]) * c)
        lines = lines + d_l * (d_l - 2.0 * u_end) + d_r * (d_r - 2.0 * w_end)
        energy = energy + part[t]
        for i in range(comps):
            energy = energy + lines[:, i * LANES : (i + 1) * LANES]

    first_pair = (group == 0) | (group == 3)
    on_left = (group == 3) | (group == 1)

    def mine(values):
        return jnp.where(first_pair, values[0], values[1])

    alpha, gamma = mine(value_a), mine(value_c)
    inner = [pair_ref[r : r + 1, :] for r in range(3)]
    slope = [wide(pair_open_ref[r : r + 1, :]) for r in range(4)]
    inner_c = inner[0] + slope[0] * alpha + slope[1] * gamma
    inner_a = inner[1] + slope[2] * alpha + slope[3] * gamma
    a, c = jnp.where(on_left, alpha, inner_a), jnp.where(on_left, inner_c, gamma)
    left = jnp.where(on_left, mine(jump), inner[2])
    right = jnp.where(on_left, inner[2], mine(jump[1:] + jump[:1]))
    seg = lax.broadcasted_iota(jnp.int32, (GROUP, width), 0)
    u_t = state_ref[0] + wide(open_ref[0]) * a + wide(open_ref[2]) * c
    w_t = state_ref[1] + wide(open_ref[1]) * a + wide(open_ref[3]) * c
    jump_l = jnp.where(seg == 0, left, state_ref[2])
    jump_r = jnp.where(seg == GROUP - 1, right, state_ref[3])
    u = u_t - jump_l * (1.0 / 12.0)
    w = w_t - jump_r * (1.0 / 12.0)
    count = send_ref.shape[0] // GROUP
    stride = block_ref.shape[0] // GROUP
    for i in range(comps):
        for r, value in enumerate((u_t, w_t, u, w)):
            part_i = value[:, i * LANES : (i + 1) * LANES]
            block_ref[pl.ds(4 * i + r, GROUP, stride=stride), :] = part_i
    block_ref[pl.ds(4 * comps, GROUP, stride=stride), :] = jnp.broadcast_to(energy, (GROUP, LANES))
    for i, place in enumerate(ORDER_BACK):
        send_ref[count * i : count * (i + 1), :] = block_ref[stride * place : stride * place + count, :]


def update_cells(recv_ref, g_ref, p_ref, q_ref, out_hbm, out_ref, sems):
    comps, _, lines = g_ref.shape
    stride = recv_ref.shape[0] // GROUP
    row8 = lax.broadcasted_iota(jnp.int32, (8, LANES), 0)
    first, last = p_ref[...], q_ref[...]
    copies = []
    for c in range(comps):
        for j, place in enumerate(ORDER_OUT):
            at = slice(j * LANES, (j + 1) * LANES)
            base = stride * ORDER_BACK.index(place) + 4 * c
            u_t, w_t, u, w = [recv_ref[base + r : base + r + 1, :] for r in range(4)]
            value = g_ref[c, :, at] - first * u_t - last * w_t
            out_ref[c, 0:8, at] = jnp.where(row8 == 0, u, value[0:8])
            out_ref[c, 8 : CELLS - 8, at] = value[8 : CELLS - 8]
            out_ref[c, CELLS - 8 :, at] = jnp.where(row8 == 7, w, value[CELLS - 8 :])
            if c == comps - 1 and j == GROUP // 2 - 1:
                half = (c, slice(None), pl.ds(0, lines // 2))
                copies.append(pltpu.make_async_copy(out_ref.at[half], out_hbm.at[half], sems.at[c]))
                copies[-1].start()
        if c < comps - 1:
            copies.append(pltpu.make_async_copy(out_ref.at[c], out_hbm.at[c], sems.at[c]))
        else:
            half = (c, slice(None), pl.ds(lines // 2, lines // 2))
            copies.append(pltpu.make_async_copy(out_ref.at[half], out_hbm.at[half], sems.at[comps]))
        copies[-1].start()
    for copy in copies:
        copy.wait()


def early_device():
    return lax.axis_index("yz") % 2 == 1


def early_kernel(recv_ref, g_ref, p_ref, q_ref, out_hbm, energy_ref, out_ref, sems):
    stride = recv_ref.shape[0] // GROUP
    energy = recv_ref[pl.ds(stride - 1, GROUP, stride=stride), :]
    energy_ref[...] = jnp.broadcast_to(jnp.sum(energy, axis=0, keepdims=True), energy_ref.shape)

    @pl.when(early_device())
    def _():
        update_cells(recv_ref, g_ref, p_ref, q_ref, out_hbm, out_ref, sems)


def late_kernel(
    scale, begun_hbm, energy_ref, recv_ref, g_ref, p_ref, q_ref, out_hbm, mean_hbm, mean_ref, out_ref, sems
):
    comps = g_ref.shape[0]
    mean_ref[0, 0] = jnp.sum(energy_ref[...]) * scale
    mean_copy = pltpu.make_async_copy(mean_ref, mean_hbm, sems.at[comps + 1])
    mean_copy.start()

    @pl.when(jnp.logical_not(early_device()))
    def _():
        update_cells(recv_ref, g_ref, p_ref, q_ref, out_hbm, out_ref, sems)

    mean_copy.wait()


def on_device(velocity, blocks):
    comps, cells, lines = velocity.shape
    width = comps * LANES
    send_rows, back_rows = 8 * comps + 1, 4 * comps + 1
    yz_count = lax.axis_size("yz")
    groups_out = [[GROUP * t + i for i in ORDER_OUT] for t in range(GROUPS)]
    groups_back = [[GROUP * t + i for i in ORDER_BACK] for t in range(GROUPS)]
    shape = functools.partial(jax.ShapeDtypeStruct, dtype=F32)

    g, send, p_rows, q_rows = pl.pallas_call(
        local_kernel,
        in_specs=[
            pl.BlockSpec(memory_space=pltpu.HBM),
            pl.BlockSpec(memory_space=pltpu.HBM),
        ],
        out_specs=[pl.BlockSpec(memory_space=pltpu.VMEM)] * 4,
        out_shape=[
            shape((comps, cells, lines)),
            shape((GROUP * send_rows, LANES)),
            shape((cells, LANES)),
            shape((cells, LANES)),
        ],
        scratch_shapes=[
            pltpu.VMEM((comps, cells, lines), F32),
            pltpu.VMEM((cells + 16, 6 * cells), BF16),
            pltpu.VMEM((cells, LANES), F32),
            pltpu.VMEM((cells - 2, 1, cells - 2), F32),
            pltpu.SemaphoreType.DMA((comps + 1,)),
        ],
        compiler_params=LARGE,
        name="local_solve",
    )(
        pltpu.with_memory_space_constraint(velocity, pltpu.HBM),
        pltpu.with_memory_space_constraint(jnp.transpose(blocks, (1, 0, 2)), pltpu.HBM),
    )

    def spread(value, axis, **kwargs):
        rows = value.reshape(value.shape[0], 1, LANES)
        return lax.all_to_all(rows, axis, 0, 0, tiled=True, **kwargs).reshape(value.shape)

    recv = spread(send, "gx", axis_index_groups=groups_out)
    msg, state, opened = pl.pallas_call(
        group_kernel,
        out_shape=[
            shape((8, width + LANES)),
            shape((4, GROUP, width)),
            shape((4, GROUP, LANES)),
        ],
        scratch_shapes=[pltpu.VMEM((GROUP * 8 * (comps + 1), LANES), F32)],
        compiler_params=SMALL,
        name="group_solve",
    )(recv)

    def joined(value, pairs):
        members = [[GROUP * t + i for t in pair] for pair in pairs for i in range(GROUP)]
        return lax.all_gather(value, "gx", axis_index_groups=members)

    near = joined(msg, ((3, 0), (1, 2)))
    pair_msg, pair_state, pair_open = pl.pallas_call(
        pair_kernel,
        out_shape=[shape((8, width + LANES)), shape((8, width)), shape((8, LANES))],
        compiler_params=SMALL,
        name="pair_groups",
    )(near)
    every = joined(pair_msg, ((0, 1), (3, 2)))
    send_back = pl.pallas_call(
        join_kernel,
        out_shape=shape((GROUP * back_rows, LANES)),
        scratch_shapes=[pltpu.VMEM((GROUP * -(-back_rows // 8) * 8, LANES), F32)],
        compiler_params=SMALL,
        name="join_groups",
    )(every, pair_state, pair_open, state, opened)
    back = spread(send_back, "gx", axis_index_groups=groups_back)
    begun, energy = pl.pallas_call(
        early_kernel,
        in_specs=[pl.BlockSpec(memory_space=pltpu.VMEM)] * 4,
        out_specs=[
            pl.BlockSpec(memory_space=pltpu.HBM),
            pl.BlockSpec(memory_space=pltpu.VMEM),
        ],
        out_shape=[shape((comps, cells, lines)), shape((yz_count, LANES))],
        scratch_shapes=[
            pltpu.VMEM((comps, cells, lines), F32),
            pltpu.SemaphoreType.DMA((comps + 1,)),
        ],
        compiler_params=LARGE,
        name="early_update",
    )(back, g, p_rows, q_rows)
    energies = spread(energy, "yz", axis_index_groups=[YZ_ORDER])
    total_count = comps * cells * lines * lax.axis_size("gx") * yz_count
    derivative, mean_square = pl.pallas_call(
        functools.partial(late_kernel, 1.0 / total_count),
        in_specs=[pl.BlockSpec(memory_space=pltpu.HBM)]
        + [pl.BlockSpec(memory_space=pltpu.VMEM)] * 5,
        out_specs=[pl.BlockSpec(memory_space=pltpu.HBM)] * 2,
        out_shape=[shape((comps, cells, lines)), shape((1, 1))],
        input_output_aliases={0: 0},
        scratch_shapes=[
            pltpu.SMEM((1, 1), F32),
            pltpu.VMEM((comps, cells, lines), F32),
            pltpu.SemaphoreType.DMA((comps + 2,)),
        ],
        compiler_params=LARGE,
        name="late_update",
    )(begun, energies, back, g, p_rows, q_rows)
    return derivative, mean_square[0, 0]


def solution(mesh):
    placed = (P(None, "gx", "yz"), P("gx", None, None))
    return jax.shard_map(
        on_device, mesh=mesh, in_specs=placed, out_specs=(P(None, "gx", "yz"), P()), check_vma=False
    )
```

```python
import functools

import jax
import jax.numpy as jnp
from jax import lax
from jax.experimental import pallas as pl
from jax.experimental.pallas import tpu as pltpu
from jax.sharding import PartitionSpec as P

COUPLING = 1.0 / 3.0
NEAR_WEIGHT = 7.0 / 9.0
FAR_WEIGHT = 1.0 / 36.0

GROUP = 16
GROUPS = 4
ORDER_OUT = tuple(4 * z + y for y in (2, 3, 1, 0) for z in (2, 3, 0, 1))
ORDER_BACK = tuple(4 * z + y for y in (2, 3, 1, 0) for z in (2, 3, 0, 1))
YZ_ORDER = (5, 4, 3, 2, 7, 6, 1, 0)
LANES = 128
CELLS = 64
CHUNK = 512
F32 = jnp.float32
BF16 = jnp.bfloat16
SMALL = pltpu.CompilerParams(vmem_limit_bytes=8 * 1024 * 1024)
LARGE = pltpu.CompilerParams(vmem_limit_bytes=16 * 1024 * 1024)


def lane_row(value, lanes=LANES):
    return jnp.broadcast_to(value, (1, lanes))


def tiled(value, copies):
    return jnp.concatenate([value] * copies, axis=1)


def parts_of(value):
    high = value.astype(BF16)
    rest = value - high.astype(F32)
    middle = rest.astype(BF16)
    return high, middle, (rest - middle.astype(F32)).astype(BF16)


def local_kernel(
    v_hbm, block_hbm, g_ref, send_ref, p_ref, q_ref, v_ref, mat_ref, pad_ref, block_ref, sems
):
    comps, _, lines = v_ref.shape
    inner = CELLS - 2
    stride = send_ref.shape[0] // GROUP
    block_copy = pltpu.make_async_copy(block_hbm, block_ref, sems.at[comps])
    block_copy.start()
    copies = [pltpu.make_async_copy(v_hbm.at[c], v_ref.at[c], sems.at[c]) for c in range(comps)]
    for copy in copies:
        copy.start()

    pad_ref[...] = jnp.zeros(pad_ref.shape, F32)
    block_copy.wait()
    pad_ref[0:inner, 0:inner] = block_ref[:, 0, :]
    padded = pltpu.roll(pltpu.roll(pad_ref[...], 1, 0), 1, 1)
    first = jnp.broadcast_to(COUPLING * padded[:, 1:2], (CELLS, LANES))
    last = jnp.broadcast_to(COUPLING * padded[:, inner : inner + 1], (CELLS, LANES))
    p_ref[...] = first
    q_ref[...] = last
    cols = lax.broadcasted_iota(jnp.int32, (1, LANES), 1)
    top = jnp.where(cols == 0, 1.0, 0.0) - COUPLING * padded[1:2]
    bottom = jnp.where(cols == CELLS - 1, 1.0, 0.0) - COUPLING * padded[inner : inner + 1]
    first_sum = jnp.sum(first * padded, axis=0, keepdims=True)
    last_sum = jnp.sum(last * padded, axis=0, keepdims=True)
    rows = lax.broadcasted_iota(jnp.int32, (16, LANES), 0)
    extra = jnp.where(rows == 0, top, 0.0)
    extra = jnp.where(rows == 1, bottom, extra)
    extra = jnp.where(rows == 2, first_sum, extra)
    extra = jnp.where(rows == 3, last_sum, extra)
    matrix = jnp.concatenate([padded, extra], 0)
    beside = pltpu.roll(matrix, 1, 1) + pltpu.roll(matrix, LANES - 1, 1)
    matrix = NEAR_WEIGHT * matrix + FAR_WEIGHT * beside
    high, middle, low = parts_of(matrix[:, 0:CELLS])
    mat_ref[...] = jnp.concatenate([high, middle, low, high, middle, high], 1)

    row8 = lax.broadcasted_iota(jnp.int32, (8, CHUNK), 0)
    energy = jnp.zeros((1, LANES), F32)
    for c in range(comps):
        copies[c].wait()
        for start in range(0, lines, CHUNK):
            v = v_ref[c, :, start : start + CHUNK]
            edge_0, edge_1 = v[0:1], v[CELLS - 1 : CELLS]
            below = jnp.concatenate([edge_0, v[: CELLS - 1]], 0)
            above = jnp.concatenate([v[1:], edge_1], 0)
            high, middle, low = parts_of(above - below)
            stacked = jnp.concatenate([high, high, high, middle, middle, low], 0)
            out = jnp.dot(mat_ref[...], stacked, preferred_element_type=F32)
            g = out[0:CELLS]
            g_ref[c, :, start : start + CHUNK] = g
            squares = jnp.sum(g * g, axis=0, keepdims=True)
            rows = out[CELLS : CELLS + 8]
            rows = jnp.where((row8 == 4) | (row8 == 5), pltpu.roll(v[0:8], 4, 0), rows)
            rows = jnp.where(row8 >= 6, v[CELLS - 8 : CELLS], rows)
            for j in range(CHUNK // LANES):
                at = slice(j * LANES, (j + 1) * LANES)
                energy = energy + squares[:, at]
                to = stride * (start // LANES + j) + 8 * c
                send_ref[to : to + 8, :] = rows[:, at]

    coefs = energy + pltpu.roll(energy, LANES // 2, 1)
    numbers = [
        first[1:2],
        last[1:2],
        first[inner : inner + 1],
        last[inner : inner + 1],
        jnp.sum(first * first, axis=0, keepdims=True),
        jnp.sum(first * last, axis=0, keepdims=True),
        jnp.sum(last * last, axis=0, keepdims=True),
    ]
    for i, number in enumerate(numbers):
        coefs = jnp.where(cols == i, number, coefs)
    for j in range(GROUP):
        to = stride * j + 8 * comps
        send_ref[to : to + 1, :] = coefs


def group_kernel(recv_ref, msg_ref, state_ref, open_ref, block_ref):
    count = recv_ref.shape[0] // GROUP
    stride = block_ref.shape[0] // GROUP
    comps = count // 8
    for i, place in enumerate(ORDER_OUT):
        to = stride * place
        block_ref[to : to + count, :] = recv_ref[count * i : count * (i + 1), :]
    width = comps * LANES

    def rows(r):
        parts = [block_ref[pl.ds(8 * i + r, GROUP, stride=stride), :] for i in range(comps)]
        return jnp.concatenate(parts, 1)

    numbers = block_ref[pl.ds(8 * comps, GROUP, stride=stride), :]

    def coef(r):
        return jnp.broadcast_to(numbers[:, r : r + 1], (GROUP, LANES))

    seg = lax.broadcasted_iota(jnp.int32, (GROUP, width), 0)
    seg_1 = lax.broadcasted_iota(jnp.int32, (GROUP, LANES), 0)

    def prev(x, s=1):
        return pltpu.roll(x, s, 0)

    def following(x, s=1):
        return pltpu.roll(x, GROUP - s, 0)

    b_first, b_last, pg, qg, v_0, v_1, v_62, v_63 = [rows(r) for r in range(8)]
    p_0, q_0, p_61, q_61, pp, pq, qq = [coef(r) for r in range(7)]
    upper = lax.broadcasted_iota(jnp.int32, (GROUP, LANES), 1) >= LANES // 2
    energy = jnp.where(upper, numbers, 0.0)
    jump_l = jnp.where(seg == 0, 0.0, prev(v_63) - v_0)
    jump_l2 = jnp.where(seg == 0, 0.0, prev(v_62) - v_0)
    jump_r = jnp.where(seg == GROUP - 1, 0.0, v_63 - following(v_0))
    jump_r2 = jnp.where(seg == GROUP - 1, 0.0, following(v_1) - v_63)
    b_first = b_first - (2.0 / 3.0) * jump_l - FAR_WEIGHT * jump_l2
    b_last = b_last - (2.0 / 3.0) * jump_r + FAR_WEIGHT * jump_r2

    unit_first = jnp.where(seg_1 == 0, 1.0, 0.0)
    unit_last = jnp.where(seg_1 == GROUP - 1, 1.0, 0.0)
    zero = jnp.zeros((GROUP, LANES), F32)
    third = jnp.full((GROUP, LANES), COUPLING, F32)
    rhs_f = jnp.concatenate([b_first, unit_first, zero], 1)
    rhs_l = jnp.concatenate([b_last, zero, unit_last], 1)
    f = (jnp.where(seg_1 == 0, 0.0, third), 1.0 - COUPLING * p_0, -COUPLING * q_0, rhs_f)
    l = (-COUPLING * p_61, 1.0 - COUPLING * q_61, jnp.where(seg_1 == GROUP - 1, 0.0, third), rhs_l)

    def reduce_level(mine, below, above):
        ratio_low = mine[0] / below[1]
        ratio_high = mine[2] / above[1]
        return (
            -ratio_low * below[0],
            mine[1] - ratio_low * below[2] - ratio_high * above[0],
            -ratio_high * above[2],
            mine[3] - tiled(ratio_low, comps + 2) * below[3] - tiled(ratio_high, comps + 2) * above[3],
        )

    f, l = (
        reduce_level(f, tuple(prev(x) for x in l), l),
        reduce_level(l, f, tuple(following(x) for x in f)),
    )
    step = 1
    while step < GROUP:
        f = reduce_level(f, tuple(prev(x, step) for x in f), tuple(following(x, step) for x in f))
        l = reduce_level(l, tuple(prev(x, step) for x in l), tuple(following(x, step) for x in l))
        step *= 2
    sol_f = f[3] / tiled(f[1], comps + 2)
    sol_l = l[3] / tiled(l[1], comps + 2)
    x_f, a_f, c_f = sol_f[:, :width], sol_f[:, width : width + LANES], sol_f[:, width + LANES :]
    x_l, a_l, c_l = sol_l[:, :width], sol_l[:, width : width + LANES], sol_l[:, width + LANES :]

    pp1, qq1 = pp + 1.0, qq + 1.0
    d_l, d_r = jump_l * (1.0 / 12.0), jump_r * (1.0 / 12.0)
    pq_w = tiled(pq, comps)
    m_f = tiled(pp1, comps) * x_f + pq_w * x_l - pg - d_l
    m_l = tiled(qq1, comps) * x_l + pq_w * x_f - qg - d_r

    def total(x):
        return jnp.sum(x, axis=0, keepdims=True)

    line_a = 2.0 * total(tiled(a_f, comps) * m_f + tiled(a_l, comps) * m_l)
    line_c = 2.0 * total(tiled(c_f, comps) * m_f + tiled(c_l, comps) * m_l)
    base = total(x_f * (m_f - pg - d_l) + x_l * (m_l - qg - d_r) + d_l * d_l + d_r * d_r)
    part = total(energy) * (1.0 / GROUP)
    for i in range(comps):
        part = part + base[:, i * LANES : (i + 1) * LANES]
    quad_aa = total(pp1 * a_f * a_f + 2.0 * pq * a_f * a_l + qq1 * a_l * a_l)
    quad_ac = total(pp1 * a_f * c_f + pq * (a_f * c_l + a_l * c_f) + qq1 * a_l * c_l)
    quad_cc = total(pp1 * c_f * c_f + 2.0 * pq * c_f * c_l + qq1 * c_l * c_l)

    end = GROUP - 1
    msg_ref[:, 0:width] = jnp.concatenate(
        [x_f[0:1], x_l[end:], line_a, line_c, v_0[0:1], v_1[0:1], v_62[end:], v_63[end:]], 0
    )
    msg_ref[:, width : width + LANES] = jnp.concatenate(
        [a_f[0:1], a_l[end:], c_f[0:1], c_l[end:], quad_aa, quad_ac, quad_cc, part], 0
    )
    state_ref[0] = x_f
    state_ref[1] = x_l
    state_ref[2] = jump_l
    state_ref[3] = jump_r
    open_ref[0] = a_f
    open_ref[1] = a_l
    open_ref[2] = c_f
    open_ref[3] = c_l


def eliminate(matrix, rhs, wide):
    size = len(rhs)
    matrix = [list(r) for r in matrix]
    rhs = list(rhs)
    inverse = [None] * size
    for k in range(size):
        inverse[k] = 1.0 / matrix[k][k]
        for i in range(k + 1, size):
            if matrix[i][k] is None:
                continue
            ratio = matrix[i][k] * inverse[k]
            for j in range(k + 1, size):
                if matrix[k][j] is not None:
                    old = matrix[i][j]
                    change = ratio * matrix[k][j]
                    matrix[i][j] = -change if old is None else old - change
            rhs[i] = rhs[i] - wide(ratio) * rhs[k]
    found = [None] * size
    for k in reversed(range(size)):
        value = rhs[k]
        for j in range(k + 1, size):
            if matrix[k][j] is not None:
                value = value - wide(matrix[k][j]) * found[j]
        found[k] = value * wide(inverse[k])
    return found


def unpacked(message, width):
    return (
        [message[r : r + 1, 0:width] for r in range(8)],
        [message[r : r + 1, width:] for r in range(8)],
    )


def pair_kernel(both_ref, msg_ref, state_ref, open_ref):
    width = both_ref.shape[2] - LANES
    comps = width // LANES

    def wide(x):
        return tiled(x, comps)

    left, l = unpacked(both_ref[0], width)
    right, r = unpacked(both_ref[1], width)
    x_f, x_l, line_a, line_c, v_0, v_1, v_62, v_63 = [list(p) for p in zip(left, right)]
    a_f, a_l, c_f, c_l, q_aa, q_ac, q_cc, part = [list(p) for p in zip(l, r)]

    jump = v_63[0] - v_0[1]
    rhs_c = -COUPLING * x_f[1] - (2.0 / 3.0) * jump + FAR_WEIGHT * (v_1[1] - v_63[0])
    rhs_a = -COUPLING * x_l[0] - (2.0 / 3.0) * jump - FAR_WEIGHT * (v_62[0] - v_0[1])
    inverse = 1.0 / (1.0 - (COUPLING * a_f[1]) * (COUPLING * c_l[0]))
    to_c, to_a = COUPLING * a_f[1] * inverse, COUPLING * c_l[0] * inverse
    c_0 = wide(inverse) * rhs_c - wide(to_c) * rhs_a
    c_alpha = to_c * (COUPLING * a_l[0])
    c_gamma = -inverse * (COUPLING * c_f[1])
    a_0 = wide(inverse) * rhs_a - wide(to_a) * rhs_c
    a_alpha = -inverse * (COUPLING * a_l[0])
    a_gamma = to_a * (COUPLING * c_f[1])

    d = jump * (1.0 / 12.0)
    inner_u = x_f[1] + wide(a_f[1]) * a_0
    inner_w = x_l[0] + wide(c_l[0]) * c_0
    both_alpha = a_f[1] * a_alpha + a_l[0] + c_l[0] * c_alpha
    both_gamma = a_f[1] * a_gamma + c_f[1] + c_l[0] * c_gamma
    slope_c = line_c[0] + wide(2.0 * q_cc[0]) * c_0
    slope_a = line_a[1] + wide(2.0 * q_aa[1]) * a_0
    line_alpha = line_a[0] + wide(2.0 * q_ac[0]) * c_0 + wide(c_alpha) * slope_c
    line_alpha = line_alpha + wide(a_alpha) * slope_a - wide(2.0 * both_alpha) * d
    line_gamma = line_c[1] + wide(2.0 * q_ac[1]) * a_0 + wide(a_gamma) * slope_a
    line_gamma = line_gamma + wide(c_gamma) * slope_c - wide(2.0 * both_gamma) * d
    base = c_0 * (line_c[0] + wide(q_cc[0]) * c_0) + a_0 * (line_a[1] + wide(q_aa[1]) * a_0)
    base = base + 2.0 * d * (d - inner_u - inner_w)
    total = part[0] + part[1]
    for i in range(comps):
        total = total + base[:, i * LANES : (i + 1) * LANES]
    q_alpha = q_aa[0] + c_alpha * (2.0 * q_ac[0] + q_cc[0] * c_alpha) + q_aa[1] * a_alpha * a_alpha
    q_gamma = q_cc[1] + a_gamma * (2.0 * q_ac[1] + q_aa[1] * a_gamma) + q_cc[0] * c_gamma * c_gamma
    q_mixed = c_gamma * (q_ac[0] + q_cc[0] * c_alpha) + a_alpha * (q_ac[1] + q_aa[1] * a_gamma)

    msg_ref[:, 0:width] = jnp.concatenate(
        [
            x_f[0] + wide(c_f[0]) * c_0,
            x_l[1] + wide(a_l[1]) * a_0,
            line_alpha,
            line_gamma,
            v_0[0],
            v_1[0],
            v_62[1],
            v_63[1],
        ],
        0,
    )
    msg_ref[:, width:] = jnp.concatenate(
        [
            a_f[0] + c_f[0] * c_alpha,
            a_l[1] * a_alpha,
            c_f[0] * c_gamma,
            c_l[1] + a_l[1] * a_gamma,
            q_alpha,
            q_mixed,
            q_gamma,
            total,
        ],
        0,
    )
    none = jnp.zeros_like(jump)
    state_ref[...] = jnp.concatenate([c_0, a_0, jump] + [none] * 5, 0)
    none = jnp.zeros_like(inverse)
    open_ref[...] = jnp.concatenate([c_alpha, c_gamma, a_alpha, a_gamma] + [none] * 4, 0)


def join_kernel(all_ref, pair_ref, pair_open_ref, state_ref, open_ref, send_ref, block_ref):
    width = state_ref.shape[2]
    comps = width // LANES
    group = lax.axis_index("gx") // GROUP
    pairs = all_ref.shape[0]

    def wide(x):
        return tiled(x, comps)

    data, scal = zip(*[unpacked(all_ref[t], width) for t in range(pairs)])
    x_f, x_l, line_a, line_c, v_0, v_1, v_62, v_63 = [[d[r] for d in data] for r in range(8)]
    a_f, a_l, c_f, c_l, q_aa, q_ac, q_cc, part = [[s[r] for s in scal] for r in range(8)]

    one = jnp.ones((1, LANES), F32)
    jump = [v_63[t - 1] - v_0[t] for t in range(pairs)]
    matrix, rhs = [], []
    for t in range(pairs):
        before, after = (t - 1) % pairs, (t + 1) % pairs
        row_a, row_c = [None] * (2 * pairs), [None] * (2 * pairs)
        row_a[2 * t] = one
        row_a[2 * before] = COUPLING * a_l[before]
        row_a[2 * before + 1] = COUPLING * c_l[before]
        row_c[2 * t + 1] = one
        row_c[2 * after] = COUPLING * a_f[after]
        row_c[2 * after + 1] = COUPLING * c_f[after]
        matrix += [row_a, row_c]
        rhs.append(
            -COUPLING * x_l[before] - (2.0 / 3.0) * jump[t] - FAR_WEIGHT * (v_62[before] - v_0[t])
        )
        rhs.append(
            -COUPLING * x_f[after] - (2.0 / 3.0) * jump[after] + FAR_WEIGHT * (v_1[after] - v_63[t])
        )
    found = eliminate(matrix, rhs, wide)
    value_a, value_c = found[0::2], found[1::2]

    energy = jnp.zeros((1, LANES), F32)
    for t in range(pairs):
        a, c = value_a[t], value_c[t]
        after = (t + 1) % pairs
        u_end = x_f[t] + wide(a_f[t]) * a + wide(c_f[t]) * c
        w_end = x_l[t] + wide(a_l[t]) * a + wide(c_l[t]) * c
        d_l, d_r = jump[t] * (1.0 / 12.0), jump[after] * (1.0 / 12.0)
        lines = a * (line_a[t] + wide(q_aa[t]) * a + wide(2.0 * q_ac[t]) * c)
        lines = lines + c * (line_c[t] + wide(q_cc[t]) * c)
        lines = lines + d_l * (d_l - 2.0 * u_end) + d_r * (d_r - 2.0 * w_end)
        energy = energy + part[t]
        for i in range(comps):
            energy = energy + lines[:, i * LANES : (i + 1) * LANES]

    first_pair = (group == 0) | (group == 3)
    on_left = (group == 3) | (group == 1)

    def mine(values):
        return jnp.where(first_pair, values[0], values[1])

    alpha, gamma = mine(value_a), mine(value_c)
    inner = [pair_ref[r : r + 1, :] for r in range(3)]
    slope = [wide(pair_open_ref[r : r + 1, :]) for r in range(4)]
    inner_c = inner[0] + slope[0] * alpha + slope[1] * gamma
    inner_a = inner[1] + slope[2] * alpha + slope[3] * gamma
    a, c = jnp.where(on_left, alpha, inner_a), jnp.where(on_left, inner_c, gamma)
    left = jnp.where(on_left, mine(jump), inner[2])
    right = jnp.where(on_left, inner[2], mine(jump[1:] + jump[:1]))
    seg = lax.broadcasted_iota(jnp.int32, (GROUP, width), 0)
    u_t = state_ref[0] + wide(open_ref[0]) * a + wide(open_ref[2]) * c
    w_t = state_ref[1] + wide(open_ref[1]) * a + wide(open_ref[3]) * c
    jump_l = jnp.where(seg == 0, left, state_ref[2])
    jump_r = jnp.where(seg == GROUP - 1, right, state_ref[3])
    u = u_t - jump_l * (1.0 / 12.0)
    w = w_t - jump_r * (1.0 / 12.0)
    count = send_ref.shape[0] // GROUP
    stride = block_ref.shape[0] // GROUP
    for i in range(comps):
        for r, value in enumerate((u_t, w_t, u, w)):
            part_i = value[:, i * LANES : (i + 1) * LANES]
            block_ref[pl.ds(4 * i + r, GROUP, stride=stride), :] = part_i
    block_ref[pl.ds(4 * comps, GROUP, stride=stride), :] = jnp.broadcast_to(energy, (GROUP, LANES))
    for i, place in enumerate(ORDER_BACK):
        send_ref[count * i : count * (i + 1), :] = block_ref[stride * place : stride * place + count, :]


def update_cells(recv_ref, g_ref, p_ref, q_ref, out_hbm, out_ref, sems):
    comps, _, lines = g_ref.shape
    stride = recv_ref.shape[0] // GROUP
    row8 = lax.broadcasted_iota(jnp.int32, (8, LANES), 0)
    first, last = p_ref[...], q_ref[...]
    copies = []
    for c in range(comps):
        for j, place in enumerate(ORDER_OUT):
            at = slice(j * LANES, (j + 1) * LANES)
            base = stride * ORDER_BACK.index(place) + 4 * c
            u_t, w_t, u, w = [recv_ref[base + r : base + r + 1, :] for r in range(4)]
            value = g_ref[c, :, at] - first * u_t - last * w_t
            out_ref[c, 0:8, at] = jnp.where(row8 == 0, u, value[0:8])
            out_ref[c, 8 : CELLS - 8, at] = value[8 : CELLS - 8]
            out_ref[c, CELLS - 8 :, at] = jnp.where(row8 == 7, w, value[CELLS - 8 :])
            if c == comps - 1 and j == 3 * GROUP // 4 - 1:
                half = (c, slice(None), pl.ds(0, 3 * lines // 4))
                copies.append(pltpu.make_async_copy(out_ref.at[half], out_hbm.at[half], sems.at[c]))
                copies[-1].start()
        if c < comps - 1:
            copies.append(pltpu.make_async_copy(out_ref.at[c], out_hbm.at[c], sems.at[c]))
        else:
            half = (c, slice(None), pl.ds(3 * lines // 4, lines // 4))
            copies.append(pltpu.make_async_copy(out_ref.at[half], out_hbm.at[half], sems.at[comps]))
        copies[-1].start()
    for copy in copies:
        copy.wait()


def early_device():
    return lax.axis_index("yz") % 2 == 1


def early_kernel(recv_ref, g_ref, p_ref, q_ref, out_hbm, energy_ref, out_ref, sems):
    stride = recv_ref.shape[0] // GROUP
    energy = recv_ref[pl.ds(stride - 1, GROUP, stride=stride), :]
    energy_ref[...] = jnp.broadcast_to(jnp.sum(energy, axis=0, keepdims=True), energy_ref.shape)

    @pl.when(early_device())
    def _():
        update_cells(recv_ref, g_ref, p_ref, q_ref, out_hbm, out_ref, sems)


def late_kernel(
    scale, begun_hbm, energy_ref, recv_ref, g_ref, p_ref, q_ref, out_hbm, mean_hbm, mean_ref, out_ref, sems
):
    comps = g_ref.shape[0]
    mean_ref[0, 0] = jnp.sum(energy_ref[...]) * scale
    mean_copy = pltpu.make_async_copy(mean_ref, mean_hbm, sems.at[comps + 1])
    mean_copy.start()

    @pl.when(jnp.logical_not(early_device()))
    def _():
        update_cells(recv_ref, g_ref, p_ref, q_ref, out_hbm, out_ref, sems)

    mean_copy.wait()


def on_device(velocity, blocks):
    comps, cells, lines = velocity.shape
    width = comps * LANES
    send_rows, back_rows = 8 * comps + 1, 4 * comps + 1
    yz_count = lax.axis_size("yz")
    groups_out = [[GROUP * t + i for i in ORDER_OUT] for t in range(GROUPS)]
    groups_back = [[GROUP * t + i for i in ORDER_BACK] for t in range(GROUPS)]
    shape = functools.partial(jax.ShapeDtypeStruct, dtype=F32)

    g, send, p_rows, q_rows = pl.pallas_call(
        local_kernel,
        in_specs=[
            pl.BlockSpec(memory_space=pltpu.HBM),
            pl.BlockSpec(memory_space=pltpu.HBM),
        ],
        out_specs=[pl.BlockSpec(memory_space=pltpu.VMEM)] * 4,
        out_shape=[
            shape((comps, cells, lines)),
            shape((GROUP * send_rows, LANES)),
            shape((cells, LANES)),
            shape((cells, LANES)),
        ],
        scratch_shapes=[
            pltpu.VMEM((comps, cells, lines), F32),
            pltpu.VMEM((cells + 16, 6 * cells), BF16),
            pltpu.VMEM((cells, LANES), F32),
            pltpu.VMEM((cells - 2, 1, cells - 2), F32),
            pltpu.SemaphoreType.DMA((comps + 1,)),
        ],
        compiler_params=LARGE,
        name="local_solve",
    )(
        pltpu.with_memory_space_constraint(velocity, pltpu.HBM),
        pltpu.with_memory_space_constraint(jnp.transpose(blocks, (1, 0, 2)), pltpu.HBM),
    )

    def spread(value, axis, **kwargs):
        rows = value.reshape(value.shape[0], 1, LANES)
        return lax.all_to_all(rows, axis, 0, 0, tiled=True, **kwargs).reshape(value.shape)

    recv = spread(send, "gx", axis_index_groups=groups_out)
    msg, state, opened = pl.pallas_call(
        group_kernel,
        out_shape=[
            shape((8, width + LANES)),
            shape((4, GROUP, width)),
            shape((4, GROUP, LANES)),
        ],
        scratch_shapes=[pltpu.VMEM((GROUP * 8 * (comps + 1), LANES), F32)],
        compiler_params=SMALL,
        name="group_solve",
    )(recv)

    def joined(value, pairs):
        members = [[GROUP * t + i for t in pair] for pair in pairs for i in range(GROUP)]
        return lax.all_gather(value, "gx", axis_index_groups=members)

    near = joined(msg, ((3, 0), (1, 2)))
    pair_msg, pair_state, pair_open = pl.pallas_call(
        pair_kernel,
        out_shape=[shape((8, width + LANES)), shape((8, width)), shape((8, LANES))],
        compiler_params=SMALL,
        name="pair_groups",
    )(near)
    every = joined(pair_msg, ((0, 1), (3, 2)))
    send_back = pl.pallas_call(
        join_kernel,
        out_shape=shape((GROUP * back_rows, LANES)),
        scratch_shapes=[pltpu.VMEM((GROUP * -(-back_rows // 8) * 8, LANES), F32)],
        compiler_params=SMALL,
        name="join_groups",
    )(every, pair_state, pair_open, state, opened)
    back = spread(send_back, "gx", axis_index_groups=groups_back)
    begun, energy = pl.pallas_call(
        early_kernel,
        in_specs=[pl.BlockSpec(memory_space=pltpu.VMEM)] * 4,
        out_specs=[
            pl.BlockSpec(memory_space=pltpu.HBM),
            pl.BlockSpec(memory_space=pltpu.VMEM),
        ],
        out_shape=[shape((comps, cells, lines)), shape((yz_count, LANES))],
        scratch_shapes=[
            pltpu.VMEM((comps, cells, lines), F32),
            pltpu.SemaphoreType.DMA((comps + 1,)),
        ],
        compiler_params=LARGE,
        name="early_update",
    )(back, g, p_rows, q_rows)
    energies = spread(energy, "yz", axis_index_groups=[YZ_ORDER])
    total_count = comps * cells * lines * lax.axis_size("gx") * yz_count
    derivative, mean_square = pl.pallas_call(
        functools.partial(late_kernel, 1.0 / total_count),
        in_specs=[pl.BlockSpec(memory_space=pltpu.HBM)]
        + [pl.BlockSpec(memory_space=pltpu.VMEM)] * 5,
        out_specs=[pl.BlockSpec(memory_space=pltpu.HBM)] * 2,
        out_shape=[shape((comps, cells, lines)), shape((1, 1))],
        input_output_aliases={0: 0},
        scratch_shapes=[
            pltpu.SMEM((1, 1), F32),
            pltpu.VMEM((comps, cells, lines), F32),
            pltpu.SemaphoreType.DMA((comps + 2,)),
        ],
        compiler_params=LARGE,
        name="late_update",
    )(begun, energies, back, g, p_rows, q_rows)
    return derivative, mean_square[0, 0]


def solution(mesh):
    placed = (P(None, "gx", "yz"), P("gx", None, None))
    return jax.shard_map(
        on_device, mesh=mesh, in_specs=placed, out_specs=(P(None, "gx", "yz"), P()), check_vma=False
    )
```
